32 devices in a mesh: seq: 8 (over z, x), tensor: 4 (over y, core).
Axes of the slice: x: 2, y: 2, z: 4, core: 2. Of those that a mesh axis runs over, the one named last changes fastest.
Arguments:
- inputs: bfloat16 [4096, 1024], P(('seq', 'tensor')), may hold values from -6 to 6
- cotangent: bfloat16 [4096, 1024], P(('seq', 'tensor')), may hold values from -6 to 6
- seq_lengths: int32 [8], replicated, may hold values from 1 to 3584, as said below
- norm_gains: float32 [4, 1024], replicated, may hold values from 0.5 to 1.5
- query_one: bfloat16 [1024, 256], P(None, 'tensor'), may hold values from -0.1875 to 0.1875
- key_one: bfloat16 [1024, 256], P(None, 'tensor'), may hold values from -0.1875 to 0.1875
- value_one: bfloat16 [1024, 1024], P(None, 'tensor'), may hold values from -0.1875 to 0.1875
- out_one: bfloat16 [1024, 1024], P('tensor'), may hold values from -1.5 to 1.5
- gate_one: bfloat16 [1024, 2752], P(None, 'tensor'), may hold values from -0.1875 to 0.1875
- up_one: bfloat16 [1024, 2752], P(None, 'tensor'), may hold values from -0.1875 to 0.1875
- down_one: bfloat16 [2752, 1024], P('tensor'), may hold values from -0.109375 to 0.109375
- query_two: bfloat16 [1024, 1024], P(None, 'tensor'), may hold values from -0.1875 to 0.1875
- key_two: bfloat16 [1024, 1024], P(None, 'tensor'), may hold values from -0.1875 to 0.1875
- value_two: bfloat16 [1024, 1024], P(None, 'tensor'), may hold values from -0.1875 to 0.1875
- out_two: bfloat16 [1024, 1024], P('tensor'), may hold values from -0.5 to 0.5
- gate_two: bfloat16 [1024, 2752], P(None, 'tensor'), may hold values from -0.1875 to 0.1875
- up_two: bfloat16 [1024, 2752], P(None, 'tensor'), may hold values from -0.1875 to 0.1875
- down_two: bfloat16 [2752, 1024], P('tensor'), may hold values from -0.109375 to 0.109375
Outputs:
- block_output: bfloat16 [4096, 1024], P(('seq', 'tensor'))
- input_grad: float32 [4096, 1024], P(('seq', 'tensor'))
- gain_grads: float32 [4, 1024], P(None, ('seq', 'tensor'))
- query_one_grad: float32 [1024, 256], P('seq', 'tensor')
- key_one_grad: float32 [1024, 256], P('seq', 'tensor')
- value_one_grad: float32 [1024, 1024], P('seq', 'tensor')
- out_one_grad: float32 [1024, 1024], P('tensor', 'seq')
- gate_one_grad: float32 [1024, 2752], P('seq', 'tensor')
- up_one_grad: float32 [1024, 2752], P('seq', 'tensor')
- down_one_grad: float32 [2752, 1024], P('tensor', 'seq')
- query_two_grad: float32 [1024, 1024], P('seq', 'tensor')
- key_two_grad: float32 [1024, 1024], P('seq', 'tensor')
- value_two_grad: float32 [1024, 1024], P('seq', 'tensor')
- out_two_grad: float32 [1024, 1024], P('tensor', 'seq')
- gate_two_grad: float32 [1024, 2752], P('seq', 'tensor')
- up_two_grad: float32 [1024, 2752], P('seq', 'tensor')
- down_two_grad: float32 [2752, 1024], P('tensor', 'seq')
The draws below stay inside these ranges and needn't reach their ends.
Inputs may be any that keep to these rules, and one draw needn't show every extreme that they name: `seq_lengths`: 8 sequences fill all 4096 tokens in order; the longest, never the first or the last, holds 3584 tokens and the others together 512.
All inputs are finite; a program needn't handle non-finite values.
Results may differ from the reference program's by a relative error of at most 0.035.
Values may be sent and summed in bfloat16 or wider, within the bound.
A program may use at most 192 MiB of HBM per device.

```python
import math
import jax
import jax.numpy as jnp
from jax import lax

D = 1024
H = 16
FEAT = 16
HEAD = 64
FF = 2752
WINDOW = 64
NSEQS = 8
TOK_DEV = 512
FEATS = 273
TOKENS = 4096


def draw_seq_lengths(key, part):
    key = jax.random.fold_in(key, 11)
    first_key, second_key = jax.random.split(key)
    cuts = jax.random.permutation(first_key, TOK_DEV - 1)[:NSEQS - 2] + 1
    cuts = jnp.sort(cuts.astype(jnp.int32))
    edges = jnp.concatenate([jnp.zeros((1,), jnp.int32), cuts, jnp.full((1,), TOK_DEV, jnp.int32)])
    short = edges[1:] - edges[:-1]
    place = jax.random.randint(second_key, (), 1, NSEQS - 1)
    index = jnp.arange(NSEQS, dtype=jnp.int32)
    lower = short[jnp.clip(index, 0, NSEQS - 2)]
    upper = short[jnp.clip(index - 1, 0, NSEQS - 2)]
    return jnp.where(index < place, lower, jnp.where(index == place, TOKENS - TOK_DEV, upper)).astype(jnp.int32)


def steps_of(rng, extent, cuts, low, top_value):
    level = 1.0
    for axis_at, parts in cuts:
        steps = jax.random.uniform(jax.random.fold_in(jax.random.fold_in(rng, 6), axis_at), (parts,), jnp.float32, low / len(cuts), top_value / len(cuts))
        level = level * jnp.repeat(jnp.exp(steps), extent[axis_at] // parts).reshape((-1,) + (1,) * (len(extent) - 1 - axis_at))
    return level


def gaussian(stream_key, shape, deviation, limit, cuts=(), held_as=jnp.bfloat16):
    drawn = jax.random.normal(stream_key, shape, jnp.float32) * deviation
    if len(cuts) > 0:
        drawn = steps_of(stream_key, shape, cuts, -0.22, 0.18) * drawn
    return jnp.clip(drawn, min=-limit, max=limit).astype(held_as)


def setup_inputs(seed: int = 0) -> dict:
    key_of = jax.random.split(jax.random.key(seed), 19)
    return {
        "inputs": gaussian(key_of[0], (TOKENS, D), 1.0, 6.0, ((0, 32),)),
        "cotangent": gaussian(key_of[1], (TOKENS, D), 1.0, 6.0, ((0, 32),)),
        "seq_lengths": draw_seq_lengths(jax.random.fold_in(key_of[18], 71), 0),
        "norm_gains": jnp.clip(1.0 + 0.1 * jax.random.normal(key_of[3], (4, D), jnp.float32), 0.5, 1.5),
        "query_one": gaussian(key_of[4], (D, H * FEAT), D ** -0.5, 0.1875, ((1, 4),)),
        "key_one": gaussian(key_of[5], (D, H * FEAT), D ** -0.5, 0.1875, ((1, 4),)),
        "value_one": gaussian(key_of[6], (D, H * HEAD), D ** -0.5, 0.1875, ((1, 4),)),
        "out_one": gaussian(key_of[7], (H * HEAD, D), (H * HEAD // 64) ** -0.5, 1.5, ((0, 4),)),
        "gate_one": gaussian(key_of[8], (D, FF), D ** -0.5, 0.1875, ((1, 4),)),
        "up_one": gaussian(key_of[9], (D, FF), D ** -0.5, 0.1875, ((1, 4),)),
        "down_one": gaussian(key_of[10], (FF, D), FF ** -0.5, 0.109375, ((0, 4),)),
        "query_two": gaussian(key_of[11], (D, H * HEAD), D ** -0.5, 0.1875, ((1, 4),)),
        "key_two": gaussian(key_of[12], (D, H * HEAD), D ** -0.5, 0.1875, ((1, 4),)),
        "value_two": gaussian(key_of[13], (D, H * HEAD), D ** -0.5, 0.1875, ((1, 4),)),
        "out_two": gaussian(key_of[14], (H * HEAD, D), (H * HEAD // 8) ** -0.5, 0.5, ((0, 4),)),
        "gate_two": gaussian(key_of[15], (D, FF), D ** -0.5, 0.1875, ((1, 4),)),
        "up_two": gaussian(key_of[16], (D, FF), D ** -0.5, 0.1875, ((1, 4),)),
        "down_two": gaussian(key_of[17], (FF, D), FF ** -0.5, 0.109375, ((0, 4),)),
    }


@jax.custom_vjp
def low(v):
    return lax.optimization_barrier(v.astype(jnp.bfloat16)).astype(jnp.float32)

@jax.custom_vjp
def low_back(v):
    return v

def low_keep(v):
    return (low(v), None)

def low_pass(kept, grad):
    return (grad,)

def back_keep(v):
    return (v, None)

def back_low(kept, grad):
    return (low(grad),)
low.defvjp(low_keep, low_pass)
low_back.defvjp(back_keep, back_low)
EPS = 1e-05
HIGH = lax.Precision.HIGHEST
ROOT_HALF = 0.5 ** 0.5
FLOOR_SCORE = -1e+30

def matmul(left, right):
    return jnp.dot(left, right, precision=HIGH, preferred_element_type=jnp.float32)

def features(values):
    outer = (values[..., :, None] * values[..., None, :]).reshape(values.shape[:-1] + (values.shape[-1] * values.shape[-1],))
    ones = jnp.ones(values.shape[:-1] + (1,), values.dtype)
    return jnp.concatenate([ones, values, outer * ROOT_HALF], axis=-1)

def rms_norm(values, gain):
    return values * lax.rsqrt(lax.optimization_barrier(jnp.mean(values * values, axis=-1, keepdims=True)) + EPS) * gain

def by_rows(function, arrays):
    total = arrays[0].shape[0]
    block = math.gcd(total, 4096)
    count = total // block
    shaped = tuple((item.reshape((count, block) + item.shape[1:]) for item in arrays))
    result = lax.map(jax.checkpoint(lambda pieces: function(*pieces)), shaped)
    return jax.tree.map(lambda item: item.reshape((total,) + item.shape[2:]), result)

def segment_ids(seq_lengths):
    ends = jnp.cumsum(seq_lengths).astype(jnp.int32)
    positions = lax.iota(jnp.int32, TOKENS)
    return lax.optimization_barrier(jnp.sum((positions[:, None] >= ends[None, :]).astype(jnp.int32), axis=1)).astype(jnp.int32)

def taylor_attention(query, key, value, segs):
    block = math.gcd(TOKENS, 512)
    count = TOKENS // block
    query_half = (query * 0.5).reshape(count, block, H, FEAT)
    key_half = (key * 0.5).reshape(count, block, H, FEAT)
    value_rows = value.reshape(count, block, H, HEAD)
    seg_rows = segs.reshape(count, block)

    def step(carry, pieces):
        state, norm_sum, last = carry
        query_blk, key_blk, value_blk, seg_blk = pieces
        inner_qk = jnp.einsum('ihf,jhf->hij', query_blk, key_blk, precision=HIGH)
        order = lax.iota(jnp.int32, block)
        allowed = (order[:, None] >= order[None, :]) & (seg_blk[:, None] == seg_blk[None, :])
        score = jnp.where(allowed[None], 1.0 + inner_qk + 0.5 * inner_qk * inner_qk, 0.0)
        numerator = jnp.einsum('hij,jhe->ihe', score, value_blk, precision=HIGH)
        totals = lax.optimization_barrier(jnp.sum(score, axis=2)).T
        query_feat = features(query_blk)
        key_feat = features(key_blk)
        carried = (seg_blk == last).astype(query.dtype)
        numerator = numerator + carried[:, None, None] * jnp.einsum('ihf,hfe->ihe', query_feat, state, precision=HIGH)
        totals = totals + carried[:, None] * jnp.einsum('ihf,hf->ih', query_feat, norm_sum, precision=HIGH)
        mixed = numerator / totals[:, :, None]
        tail = (seg_blk == seg_blk[-1]).astype(query.dtype)
        keep = (seg_blk[-1] == last).astype(query.dtype)
        state = keep * state + jnp.einsum('jhf,jhe->hfe', key_feat * tail[:, None, None], value_blk, precision=HIGH)
        norm_sum = keep * norm_sum + jnp.einsum('jhf,j->hf', key_feat, tail, precision=HIGH)
        return ((state, norm_sum, seg_blk[-1].astype(jnp.int32)), mixed)
    start = (jnp.zeros((H, FEATS, HEAD), query.dtype), jnp.zeros((H, FEATS), query.dtype), jnp.array(-1, jnp.int32))
    carry, mixed = lax.scan(jax.checkpoint(step), start, (query_half, key_half, value_rows, seg_rows))
    return mixed.reshape(TOKENS, H * HEAD)

def window_attention(query, key, value, segs):
    block = math.gcd(TOKENS, 512)
    span = WINDOW - 1
    key_pad = jnp.concatenate([jnp.zeros((span,) + key.shape[1:], key.dtype), key])
    value_pad = jnp.concatenate([jnp.zeros((span,) + value.shape[1:], value.dtype), value])
    seg_pad = jnp.concatenate([jnp.full((span,), -1, jnp.int32), segs.astype(jnp.int32)])

    def one(start):
        query_blk = lax.dynamic_slice_in_dim(query, start, block)
        key_blk = lax.dynamic_slice_in_dim(key_pad, start, block + span)
        value_blk = lax.dynamic_slice_in_dim(value_pad, start, block + span)
        query_seg = lax.dynamic_slice_in_dim(segs, start, block)
        key_seg = lax.dynamic_slice_in_dim(seg_pad, start, block + span)
        query_pos = lax.iota(jnp.int32, block)[:, None] + span
        key_pos = lax.iota(jnp.int32, block + span)[None, :]
        allowed = (key_pos <= query_pos) & (key_pos > query_pos - WINDOW) & (key_seg[None, :] == query_seg[:, None])
        score = jnp.einsum('ihe,jhe->hij', query_blk, key_blk, precision=HIGH) * HEAD ** (-0.5)
        score = jnp.where(allowed[None], score, FLOOR_SCORE)
        top = lax.optimization_barrier(jnp.max(score, axis=2, keepdims=True))
        weight = jnp.exp(score - top)
        prob = low(weight / lax.optimization_barrier(jnp.sum(weight, axis=2, keepdims=True)))
        return jnp.einsum('hij,jhe->ihe', prob, value_blk, precision=HIGH)
    starts = lax.iota(jnp.int32, TOKENS // block) * block
    mixed = lax.map(jax.checkpoint(one), starts)
    return mixed.reshape(TOKENS, H * HEAD)

def attention_branch(inputs, gain, w_query, w_key, w_value, w_out, segs, core, query_size):

    def project(rows):
        normed = low(rms_norm(rows, gain))
        query = low_back(low(matmul(normed, w_query)))
        key = low_back(low(matmul(normed, w_key)))
        value = low_back(low(matmul(normed, w_value)))
        return (query, key, value)
    query, key, value = by_rows(project, (inputs,))
    mixed = core(query.reshape(TOKENS, H, query_size), key.reshape(TOKENS, H, query_size), value.reshape(TOKENS, H, HEAD), segs)
    mixed = low_back(low(mixed))
    return by_rows(lambda rows: low_back(matmul(rows, w_out)), (mixed,))

def mlp_branch(inputs, gain, w_gate, w_up, w_down):

    def rows_fn(rows):
        normed = low(rms_norm(rows, gain))
        gate = low_back(matmul(normed, w_gate))
        up_val = low_back(matmul(normed, w_up))
        hidden = low(jax.nn.silu(gate) * up_val)
        return low_back(matmul(hidden, w_down))
    return by_rows(rows_fn, (inputs,))

def reference(inputs, cotangent, seq_lengths, norm_gains, query_one, key_one, value_one, out_one, gate_one, up_one, down_one, query_two, key_two, value_two, out_two, gate_two, up_two, down_two):
    segs = segment_ids(seq_lengths)
    weights = tuple((item.astype(jnp.float32) for item in (query_one, key_one, value_one, out_one, gate_one, up_one, down_one, query_two, key_two, value_two, out_two, gate_two, up_two, down_two)))

    def forward(start, gains, wq1, wk1, wv1, wo1, wg1, wu1, wd1, wq2, wk2, wv2, wo2, wg2, wu2, wd2):
        middle = start + attention_branch(start, gains[0], wq1, wk1, wv1, wo1, segs, taylor_attention, FEAT)
        layer_out = middle + mlp_branch(middle, gains[1], wg1, wu1, wd1)
        middle = layer_out + attention_branch(layer_out, gains[2], wq2, wk2, wv2, wo2, segs, window_attention, HEAD)
        return middle + mlp_branch(middle, gains[3], wg2, wu2, wd2)
    result, pullback = jax.vjp(forward, inputs.astype(jnp.float32), norm_gains, *weights)
    grads = pullback(cotangent.astype(jnp.float32))
    return (result.astype(jnp.bfloat16), grads[0], grads[1], grads[2], grads[3], grads[4], grads[5], grads[6], grads[7], grads[8], grads[9], grads[10], grads[11], grads[12], grads[13], grads[14], grads[15])
```

```python
import math

import jax
import jax.numpy as jnp
from jax import lax
from jax.experimental import pallas as pl
from jax.experimental.pallas import tpu as pltpu
from jax.sharding import PartitionSpec as P

FEAT = 16
HEAD = 64
WINDOW = 64


EPS = 1e-05
HIGH = lax.Precision.HIGHEST
ROOT_HALF = 0.5**0.5
FLOOR_SCORE = -1e30
SAME_DIMS = (((0,), (0,)), ((), ()))
BACK_DIMS = (((1,), (1,)), ((), ()))


def shortened(array):
    return jax.tree.map(lambda a: a.astype(jnp.bfloat16) if a.dtype == jnp.float32 else a, array)


def from_behind(block, axis, distance):
    devices = range(lax.axis_size(axis))
    route = [(i - distance, i) for i in devices if i - distance in devices]
    return lax.ppermute(block, axis, route)


def plain(left, right):
    return jnp.dot(left, right, preferred_element_type=jnp.float32)


def inner(left, right):
    return lax.dot_general(left, right, SAME_DIMS, preferred_element_type=jnp.float32)


def through(left, right):
    return lax.dot_general(left, right, BACK_DIMS, preferred_element_type=jnp.float32)


def features(values):
    outer = (values[..., :, None] * values[..., None, :]).reshape(
        values.shape[:-1] + (values.shape[-1] * values.shape[-1],)
    )
    ones = jnp.ones(values.shape[:-1] + (1,), jnp.float32)
    return jnp.concatenate([ones, values, outer * ROOT_HALF], axis=-1)


def segment_ids(seq_lengths, first, count):
    ends = jnp.cumsum(seq_lengths)
    positions = first + lax.iota(jnp.int32, count)
    return jnp.sum((positions[:, None] >= ends[None, :]).astype(jnp.int32), axis=1)


def start_flags(seq_lengths, stretch, n_seq):
    ends = jnp.cumsum(seq_lengths)
    owners = (ends - seq_lengths) // stretch
    devices = lax.iota(jnp.int32, n_seq)
    return jnp.max((owners[None, :] == devices[:, None]).astype(jnp.float32), axis=1)


def reach(flags, position, n_seq, forward):
    before = jnp.concatenate([jnp.zeros((1,), jnp.float32), jnp.cumsum(flags)])
    others = lax.iota(jnp.int32, n_seq)
    if forward:
        mine = lax.dynamic_index_in_dim(before, position, keepdims=False)
        clear = mine - before[1:] == 0.0
        return ((others < position) & clear).astype(jnp.float32)
    mine = lax.dynamic_index_in_dim(before, position + 1, keepdims=False)
    clear = before[:-1] - mine == 0.0
    return ((others > position) & clear).astype(jnp.float32)


def spread(part):
    return lax.all_gather(part, "tensor", axis=0, tiled=True)


def collect(product, rows):
    return lax.psum_scatter(
        product(jnp.int32(0), rows * lax.axis_size("tensor")).astype(jnp.bfloat16),
        "tensor",
        scatter_dimension=0,
        tiled=True,
    ).astype(jnp.float32)


def pass_states(state, norm_sum, place, backward):
    seq_lengths, stretch_start, stretch, position, n_seq, flags = place
    weights = reach(flags, position, n_seq, not backward)
    feats = state.shape[0]

    def absorb(carry, pieces):
        count = pieces[0].shape[0] // feats
        return (
            carry[0]
            + jnp.einsum("k,kfx->fx", weights, pieces[0].reshape(count, feats, -1), precision=HIGH),
            carry[1]
            + jnp.einsum("k,kfx->fx", weights, pieces[1].reshape(count, feats, -1), precision=HIGH),
        )

    empty = (jnp.zeros_like(state), jnp.zeros_like(norm_sum))
    if backward:
        return absorb(
            empty,
            (
                lax.all_gather(shortened(state), "seq", axis=0, tiled=True),
                lax.all_gather(shortened(norm_sum), "seq", axis=0, tiled=True),
            ),
        )
    return absorb(
        empty,
        (
            lax.all_gather(state.astype(jnp.bfloat16), "seq", axis=0, tiled=True).astype(
                jnp.float32
            ),
            lax.all_gather(norm_sum.astype(jnp.bfloat16), "seq", axis=0, tiled=True).astype(
                jnp.float32
            ),
        ),
    )


def taylor_pieces(query, key, value, place):
    seq_lengths, stretch_start, stretch, position, n_seq, flags = place
    heads = query.shape[1] // FEAT
    query_half = query.astype(jnp.float32).reshape(stretch, heads, FEAT) * 0.5
    key_half = key.astype(jnp.float32).reshape(stretch, heads, FEAT) * 0.5
    value_full = value.astype(jnp.float32).reshape(stretch, heads, HEAD)
    segs = segment_ids(seq_lengths, stretch_start, stretch)
    order = lax.iota(jnp.int32, stretch)
    allowed = (order[:, None] >= order[None, :]) & (segs[:, None] == segs[None, :])
    inner_qk = jnp.einsum("ihf,jhf->hij", query_half, key_half, precision=HIGH)
    score = jnp.where(allowed[None], 1.0 + inner_qk + 0.5 * inner_qk * inner_qk, 0.0)
    return (heads, query_half, key_half, value_full, segs, allowed, inner_qk, score)


def taylor_forward(query, key, value, place):
    seq_lengths, stretch_start, stretch, position, n_seq, flags = place
    heads, query_half, key_half, value_full, segs, allowed, inner_qk, score = taylor_pieces(
        query, key, value, place
    )
    previous = segment_ids(seq_lengths, stretch_start - 1, 1)[0]
    carried = (segs == previous).astype(jnp.float32)
    tail = (segs == segs[-1]).astype(jnp.float32)
    query_feat = features(query_half)
    key_feat = features(key_half)
    feats = key_feat.shape[-1]
    local_state = jnp.einsum(
        "jhf,jhe->fhe", key_feat * tail[:, None, None], value_full, precision=HIGH
    ).reshape(feats, heads * HEAD)
    local_norm = jnp.einsum("jhf,j->fh", key_feat, tail, precision=HIGH)
    numerator = jnp.einsum("hij,jhe->ihe", score, value_full, precision=HIGH)
    totals = jnp.sum(score, axis=2).T
    state_in, norm_in = pass_states(local_state, local_norm, place, False)
    state_three = state_in.reshape(feats, heads, HEAD)
    numerator = numerator + carried[:, None, None] * jnp.einsum(
        "ihf,fhe->ihe", query_feat, state_three, precision=HIGH
    )
    totals = totals + carried[:, None] * jnp.einsum(
        "ihf,fh->ih", query_feat, norm_in, precision=HIGH
    )
    mixed = numerator / totals[:, :, None]
    saved = (totals, mixed, query_feat, key_feat, state_in, norm_in, carried, tail)
    return (mixed.reshape(stretch, heads * HEAD), saved)


def taylor_backward(d_mixed, query, key, value, saved, place):
    seq_lengths, stretch_start, stretch, position, n_seq, flags = place
    totals, mixed, query_feat, key_feat, state_in, norm_in, carried, tail = saved
    heads, query_half, key_half, value_full, segs, allowed, inner_qk, score = taylor_pieces(
        query, key, value, place
    )
    feats = key_feat.shape[-1]
    d_out = d_mixed.astype(jnp.float32).reshape(stretch, heads, HEAD)
    d_numer = d_out / totals[:, :, None]
    d_total = -jnp.sum(d_out * mixed, axis=2) / totals
    d_score = (
        jnp.einsum("ihe,jhe->hij", d_numer, value_full, precision=HIGH) + d_total.T[:, :, None]
    )
    d_score = jnp.where(allowed[None], d_score, 0.0)
    d_value = jnp.einsum("hij,ihe->jhe", score, d_numer, precision=HIGH)
    d_inner = d_score * (1.0 + inner_qk)
    d_query = jnp.einsum("hij,jhf->ihf", d_inner, key_half, precision=HIGH)
    d_key = jnp.einsum("hij,ihf->jhf", d_inner, query_half, precision=HIGH)
    state_three = state_in.reshape(feats, heads, HEAD)
    carried_feat = query_feat * carried[:, None, None]
    d_qfeat = carried[:, None, None] * (
        jnp.einsum("ihe,fhe->ihf", d_numer, state_three, precision=HIGH)
        + d_total[:, :, None] * norm_in.T[None]
    )
    d_state = jnp.einsum("ihf,ihe->fhe", carried_feat, d_numer, precision=HIGH).reshape(
        feats, heads * HEAD
    )
    d_norm = jnp.einsum("ihf,ih->fh", carried_feat, d_total, precision=HIGH)
    grad_state, grad_norm = pass_states(d_state, d_norm, place, True)
    grad_three = grad_state.reshape(feats, heads, HEAD)
    d_kfeat = tail[:, None, None] * (
        jnp.einsum("fhe,jhe->jhf", grad_three, value_full, precision=HIGH) + grad_norm.T[None]
    )
    d_value = d_value + tail[:, None, None] * jnp.einsum(
        "jhf,fhe->jhe", key_feat, grad_three, precision=HIGH
    )
    d_query = d_query + jax.vjp(features, query_half)[1](d_qfeat)[0]
    d_key = d_key + jax.vjp(features, key_half)[1](d_kfeat)[0]
    return (
        (0.5 * d_query).reshape(stretch, heads * FEAT).astype(jnp.bfloat16),
        (0.5 * d_key).reshape(stretch, heads * FEAT).astype(jnp.bfloat16),
        d_value.reshape(stretch, heads * HEAD).astype(jnp.bfloat16),
    )


def window_allowed(key_segs, stretch_start, first, block, span):
    query_row = first + lax.iota(jnp.int32, block)[:, None] + span
    key_col = first + lax.iota(jnp.int32, block + span)[None, :]
    query_seg = key_segs[first + span : first + span + block]
    return (
        (key_col <= query_row)
        & (key_col > query_row - WINDOW)
        & (key_segs[None, :] == query_seg[:, None])
        & (stretch_start - span + key_col >= 0)
    )


def window_forward(query, key, value, place):
    seq_lengths, stretch_start, stretch, position, n_seq, flags = place
    span = WINDOW - 1
    heads = query.shape[1] // HEAD
    prev_key, prev_value = from_behind((key[stretch - span :], value[stretch - span :]), "seq", 1)
    keys = jnp.concatenate([prev_key, key]).reshape(stretch + span, heads, HEAD)
    values = jnp.concatenate([prev_value, value]).reshape(stretch + span, heads, HEAD)
    queries = query.reshape(stretch, heads, HEAD)
    key_segs = segment_ids(seq_lengths, stretch_start - span, stretch + span)
    block = math.gcd(stretch, 512)
    allowed = window_allowed(key_segs, stretch_start, 0, block, span)
    score = jnp.einsum(
        "ihe,jhe->hij", queries, keys, preferred_element_type=jnp.float32
    ) * HEAD ** (-0.5)
    score = jnp.where(allowed[None], score, FLOOR_SCORE)
    top = jnp.max(score, axis=2, keepdims=True)
    weight = jnp.exp(score - top)
    total = jnp.sum(weight, axis=2, keepdims=True)
    prob = (weight / total).astype(jnp.bfloat16)
    outputs = jnp.einsum("hij,jhe->ihe", prob, values, preferred_element_type=jnp.float32)
    log_totals = top + jnp.log(total)
    mixed = outputs.reshape(stretch, heads * HEAD)
    return (mixed, (keys, values, key_segs, log_totals))


def window_backward(d_mixed, query, key, value, saved, place):
    seq_lengths, stretch_start, stretch, position, n_seq, flags = place
    keys, values, key_segs, log_totals = saved
    span = WINDOW - 1
    heads = query.shape[1] // HEAD
    queries = query.reshape(stretch, heads, HEAD)
    d_out = d_mixed.reshape(stretch, heads, HEAD)
    block = math.gcd(stretch, 512)
    d_keys = jnp.zeros((stretch + span, heads, HEAD), jnp.float32)
    d_values = jnp.zeros((stretch + span, heads, HEAD), jnp.float32)
    allowed = window_allowed(key_segs, stretch_start, 0, block, span)
    score = jnp.einsum(
        "ihe,jhe->hij", queries, keys, preferred_element_type=jnp.float32
    ) * HEAD ** (-0.5)
    score = jnp.where(allowed[None], score, FLOOR_SCORE)
    prob = jnp.exp(score - log_totals)
    d_prob = jnp.einsum("ihe,jhe->hij", d_out, values, preferred_element_type=jnp.float32)
    d_score = prob * (d_prob - jnp.sum(prob * d_prob, axis=2, keepdims=True)) * HEAD ** (-0.5)
    d_queries = jnp.einsum("hij,jhe->ihe", d_score, keys.astype(jnp.float32), precision=HIGH)
    d_keys = d_keys.at[0 : block + span].add(
        jnp.einsum("hij,ihe->jhe", d_score, queries.astype(jnp.float32), precision=HIGH)
    )
    d_values = d_values.at[0 : block + span].add(
        jnp.einsum(
            "hij,ihe->jhe", prob.astype(jnp.bfloat16), d_out, preferred_element_type=jnp.float32
        )
    )
    back_key, back_value = (
        from_behind(d_keys[:span].astype(jnp.bfloat16), "seq", -1).astype(jnp.float32),
        from_behind(d_values[:span].astype(jnp.bfloat16), "seq", -1).astype(jnp.float32),
    )
    own_keys = d_keys[span:].at[stretch - span :].add(back_key)
    own_values = d_values[span:].at[stretch - span :].add(back_value)
    return (
        d_queries.reshape(stretch, heads * HEAD).astype(jnp.bfloat16),
        own_keys.reshape(stretch, heads * HEAD).astype(jnp.bfloat16),
        own_values.reshape(stretch, heads * HEAD).astype(jnp.bfloat16),
    )


def norm_forward(values, gain):
    inverse = lax.rsqrt(jnp.mean(values * values, axis=-1, keepdims=True) + EPS)
    scaled = values * inverse
    return ((scaled * gain).astype(jnp.bfloat16), scaled, inverse)


def norm_backward(grad, scaled, inverse, gain):
    d_scaled = grad * gain
    d_values = inverse * (d_scaled - scaled * jnp.mean(d_scaled * scaled, axis=-1, keepdims=True))
    return (d_values, jnp.sum(grad * scaled, axis=0))


MESH = pl.DeviceIdType.MESH
LOW = jnp.bfloat16
FULL = jnp.float32
VMEM = pl.BlockSpec(memory_space=pltpu.VMEM)
VMEM_BYTES = 56 * 1024 * 1024


class Group:
    def __init__(self):
        index = lax.axis_index("tensor")
        self.index = index
        self.low = lax.rem(index, 2)
        self.high = index // 2
        self.pair = {"tensor": index + 1 - 2 * self.low}
        self.partner = {"tensor": lax.rem(index + 2, 4)}

    def own(self, chunk):
        return self.low + 2 * chunk

    def other(self, chunk):
        return 1 - self.low + 2 * chunk

    def greet(self):
        barrier = pltpu.get_barrier_semaphore()
        pl.semaphore_signal(barrier, inc=1, device_id=self.pair, device_id_type=MESH)
        pl.semaphore_signal(barrier, inc=1, device_id=self.partner, device_id_type=MESH)
        pl.semaphore_wait(barrier, 2)


def remote(src, dst, send, recv, device):
    copy = pltpu.make_async_remote_copy(
        src_ref=src,
        dst_ref=dst,
        send_sem=send,
        recv_sem=recv,
        device_id=device,
        device_id_type=MESH,
    )
    copy.start()
    return copy


class Total:
    def __init__(self, group, buffers, sems):
        self.group = group
        self.pair_out, self.pair_in, self.out, self.into = buffers
        self.sems = sems
        self.copies = {}

    def give(self, chunk, part):
        self.pair_out[chunk] = part.astype(LOW)
        self.copies["pair", chunk] = remote(
            self.pair_out.at[chunk],
            self.pair_in.at[chunk],
            self.sems.at[0, chunk],
            self.sems.at[1, chunk],
            self.group.pair,
        )

    def pair_sum(self, chunk, part):
        self.copies["pair", chunk].wait_recv()
        return part + self.pair_in[chunk].astype(FULL)

    def swap(self, chunk, part):
        self.out[chunk] = self.pair_sum(chunk, part).astype(LOW)
        self.copies["far", chunk] = remote(
            self.out.at[chunk],
            self.into.at[chunk],
            self.sems.at[2, chunk],
            self.sems.at[3, chunk],
            self.group.partner,
        )

    def take(self, chunk):
        self.copies["far", chunk].wait_recv()
        return self.out[chunk].astype(FULL) + self.into[chunk].astype(FULL)

    def close(self):
        for copy in self.copies.values():
            copy.wait_send()


def total_scratch(rows, width):
    return [pltpu.VMEM((2, rows, width), LOW)] * 4 + [pltpu.SemaphoreType.DMA((4, 2))]


class Share:
    def __init__(self, group, full, sems):
        self.group = group
        self.full = full
        self.sems = sems
        self.copies = {}

    def give(self, chunk, block):
        mine = self.group.own(chunk)
        self.full[mine] = block
        self.copies[chunk] = remote(
            self.full.at[mine],
            self.full.at[mine],
            self.sems.at[0, chunk],
            self.sems.at[1, chunk],
            self.group.pair,
        )

    def await_other(self, chunk):
        self.copies[chunk].wait_recv()

    def close(self):
        for copy in self.copies.values():
            copy.wait_send()


def share_scratch(rows, width):
    return [pltpu.VMEM((4, rows, width), LOW), pltpu.SemaphoreType.DMA((2, 2))]


def norm_apply(values, gain):
    inverse = lax.rsqrt(jnp.mean(values * values, axis=-1, keepdims=True) + EPS)
    return (values * inverse * gain).astype(LOW)


def norm_back(grad, values, gain):
    inverse = lax.rsqrt(jnp.mean(values * values, axis=-1, keepdims=True) + EPS)
    scaled = values * inverse
    d_scaled = grad * gain
    d_values = inverse * (d_scaled - scaled * jnp.mean(d_scaled * scaled, axis=-1, keepdims=True))
    return d_values, grad * scaled


def gate_forward(gate, up_val):
    return (gate * up_val / (1.0 + jnp.exp(-gate))).astype(LOW)


def gate_backward(d_hidden, gate, up_val):
    sigma = 1.0 / (1.0 + jnp.exp(-gate))
    d_gate = (d_hidden * up_val * sigma * (1.0 + gate * (1.0 - sigma))).astype(LOW)
    d_up = (d_hidden * gate * sigma).astype(LOW)
    return d_gate, d_up


def enter_kernel(
    inputs, cotangent, gains, w_query, w_key, w_value,
    start_out, normed_out, grad_out, query_out, key_out, value_out,
    rows_in, cot_in, full, full_sems, cot_full, cot_sems, sems,
):
    group = Group()
    group.greet()
    far = remote(inputs, rows_in, sems.at[0], sems.at[1], group.partner)
    far_cot = remote(cotangent, cot_in, sems.at[2], sems.at[3], group.partner)
    share = Share(group, full, full_sems)
    cot_share = Share(group, cot_full, cot_sems)

    def project(block):
        rows = normed_out[block]
        query_out[block] = plain(rows, w_query[...]).astype(LOW)
        key_out[block] = plain(rows, w_key[...]).astype(LOW)
        value_out[block] = plain(rows, w_value[...]).astype(LOW)

    def hand(step, block, raw):
        values = raw.astype(FULL)
        start_out[block // 2] = values
        normed = norm_apply(values, gains[0:1])
        normed_out[block] = normed
        full[block] = normed
        share.copies[step] = remote(
            full.at[block], full.at[block], full_sems.at[0, step], full_sems.at[1, step], group.pair
        )

    def hand_cot(step, block, raw):
        grad_out[block] = raw
        cot_full[block] = raw
        cot_share.copies[step] = remote(
            cot_full.at[block], cot_full.at[block], cot_sems.at[0, step], cot_sems.at[1, step], group.pair
        )

    mine = group.index
    mate = mine + 1 - 2 * group.low
    theirs = lax.rem(mine + 2, 4)
    theirs_mate = lax.rem(mate + 2, 4)
    hand(0, mine, inputs[...])
    hand_cot(0, mine, cotangent[...])
    project(mine)
    share.await_other(0)
    normed_out[mate] = full[mate]
    project(mate)
    far.wait_recv()
    hand(1, theirs, rows_in[...])
    project(theirs)
    share.await_other(1)
    normed_out[theirs_mate] = full[theirs_mate]
    project(theirs_mate)
    far_cot.wait_recv()
    hand_cot(1, theirs, cot_in[...])
    cot_share.await_other(0)
    grad_out[mate] = cot_full[mate]
    cot_share.await_other(1)
    grad_out[theirs_mate] = cot_full[theirs_mate]
    far.wait_send()
    far_cot.wait_send()
    share.close()
    cot_share.close()


def forward_kernel(
    mixed, w_out, start, gains, w_gate, w_up, w_down, w_query, w_key, w_value,
    middle_out, after_out, normed_mlp_out, normed_out, gate_out, up_out, hidden_out, query_out, key_out, value_out,
    *scratch,
):
    group = Group()
    group.greet()
    first = Total(group, scratch[0:4], scratch[4])
    second = Total(group, scratch[5:9], scratch[9])
    share_mlp = Share(group, *scratch[10:12])
    share = Share(group, *scratch[12:14])

    def mlp_rows(block):
        rows = share_mlp.full[block]
        normed_mlp_out[block] = rows
        gate = plain(rows, w_gate[...])
        up_val = plain(rows, w_up[...])
        gate_out[block] = gate
        up_out[block] = up_val
        hidden = gate_forward(gate, up_val)
        hidden_out[block] = hidden
        return plain(hidden, w_down[...])

    def project(block):
        rows = share.full[block]
        normed_out[block] = rows
        query_out[block] = plain(rows, w_query[...]).astype(LOW)
        key_out[block] = plain(rows, w_key[...]).astype(LOW)
        value_out[block] = plain(rows, w_value[...]).astype(LOW)

    for chunk in range(2):
        first.give(chunk, plain(mixed[group.other(chunk)], w_out[...]))
    for chunk in range(2):
        first.swap(chunk, plain(mixed[group.own(chunk)], w_out[...]))
    for chunk in range(2):
        middle = start[chunk] + first.take(chunk)
        middle_out[chunk] = middle
        share_mlp.give(chunk, norm_apply(middle, gains[1:2]))
        part = mlp_rows(group.own(chunk))
        share_mlp.await_other(chunk)
        second.give(chunk, mlp_rows(group.other(chunk)))
        second.swap(chunk, part)
    for chunk in range(2):
        after = middle_out[chunk] + second.take(chunk)
        after_out[chunk] = after
        share.give(chunk, norm_apply(after, gains[2:3]))
        project(group.own(chunk))
        share.await_other(chunk)
        project(group.other(chunk))
    for item in (first, second, share_mlp, share):
        item.close()


def turn_kernel(
    mixed, w_out, after, gains, w_gate, w_up, w_down, cot,
    result_out, grad_out, grad_low_out, d_mixed_out, normed_out, hidden_out, d_gate_out, d_up_out, gain_out,
    *scratch,
):
    group = Group()
    group.greet()
    first = Total(group, scratch[0:4], scratch[4])
    second = Total(group, scratch[5:9], scratch[9])
    last = Total(group, scratch[10:14], scratch[14])
    share_mlp = Share(group, *scratch[15:17])
    share = Share(group, *scratch[17:19])
    middle_keep = scratch[19]
    gain = gains[3:4]

    def mlp_rows(block):
        rows = share_mlp.full[block]
        normed_out[block] = rows
        gate = plain(rows, w_gate[...])
        up_val = plain(rows, w_up[...])
        d_hidden = through(cot[block], w_down[...])
        hidden_out[block] = gate_forward(gate, up_val)
        d_gate, d_up = gate_backward(d_hidden, gate, up_val)
        d_gate_out[block] = d_gate
        d_up_out[block] = d_up
        return through(d_gate, w_gate[...]) + through(d_up, w_up[...])

    for chunk in range(2):
        first.give(chunk, plain(mixed[group.other(chunk)], w_out[...]))
    for chunk in range(2):
        first.swap(chunk, plain(mixed[group.own(chunk)], w_out[...]))
    for chunk in range(2):
        middle = after[chunk] + first.take(chunk)
        middle_keep[chunk] = middle
        share_mlp.give(chunk, norm_apply(middle, gain))
        part = mlp_rows(group.own(chunk))
        share_mlp.await_other(chunk)
        second.give(chunk, mlp_rows(group.other(chunk)))
        second.swap(chunk, part)
    for chunk in range(2):
        last.give(chunk, plain(hidden_out[group.other(chunk)], w_down[...]))
    for chunk in range(2):
        last.out[chunk] = last.pair_sum(chunk, plain(hidden_out[group.own(chunk)], w_down[...])).astype(LOW)
    mine, theirs = group.high, 1 - group.high
    last.copies["far", 0] = remote(
        last.out.at[theirs], last.into.at[0], last.sems.at[2, 0], last.sems.at[3, 0], group.partner
    )
    gain_out[...] = jnp.zeros_like(gain_out)
    for chunk in range(2):
        own = group.own(chunk)
        d_values, d_gain = norm_back(second.take(chunk), middle_keep[chunk], gain)
        grad = cot[own].astype(FULL) + d_values
        grad_out[chunk] = grad
        gain_out[...] += jnp.where(group.high == chunk, 1.0, 0.0) * jnp.sum(d_gain, axis=0, keepdims=True)
        share.give(chunk, grad.astype(LOW))
        grad_low_out[own] = share.full[own]
        d_mixed_out[own] = through(share.full[own], w_out[...]).astype(LOW)
        share.await_other(chunk)
        other = group.other(chunk)
        grad_low_out[other] = share.full[other]
        d_mixed_out[other] = through(share.full[other], w_out[...]).astype(LOW)
    last.copies["far", 0].wait_recv()
    result_out[...] = (
        middle_keep[mine] + last.out[mine].astype(FULL) + last.into[0].astype(FULL)
    ).astype(LOW)
    for item in (first, second, last, share_mlp, share):
        item.close()


def backward_kernel(
    d_query, d_key, d_value, w_query, w_key, w_value, after, middle, grad_in, gains,
    gate_in, up_in, w_gate, w_up, w_down, w_out,
    grad_out, mlp_grad_out, grad_low_out, d_gate_out, d_up_out, d_mixed_out, gain_out,
    *scratch,
):
    group = Group()
    group.greet()
    first = Total(group, scratch[0:4], scratch[4])
    second = Total(group, scratch[5:9], scratch[9])
    share_mlp = Share(group, *scratch[10:12])
    share = Share(group, *scratch[12:14])

    def normed_rows(block):
        return (
            through(d_query[block], w_query[...])
            + through(d_key[block], w_key[...])
            + through(d_value[block], w_value[...])
        )

    def mlp_rows(block):
        rows = share_mlp.full[block]
        mlp_grad_out[block] = rows
        d_hidden = through(rows, w_down[...])
        d_gate, d_up = gate_backward(d_hidden, gate_in[block], up_in[block])
        d_gate_out[block] = d_gate
        d_up_out[block] = d_up
        return through(d_gate, w_gate[...]) + through(d_up, w_up[...])

    def back(total, chunk, values, gain, row):
        d_values, d_gain = norm_back(total.take(chunk), values, gain)
        kept = jnp.where(group.high == chunk, 1.0, 0.0) * jnp.sum(d_gain, axis=0, keepdims=True)
        gain_out[row : row + 1] = kept if chunk == 0 else gain_out[row : row + 1] + kept
        return d_values

    for chunk in range(2):
        first.give(chunk, normed_rows(group.other(chunk)))
    for chunk in range(2):
        first.swap(chunk, normed_rows(group.own(chunk)))
    for chunk in range(2):
        grad = grad_in[chunk] + back(first, chunk, after[chunk], gains[2:3], 1)
        grad_out[chunk] = grad
        share_mlp.give(chunk, grad.astype(LOW))
        part = mlp_rows(group.own(chunk))
        share_mlp.await_other(chunk)
        second.give(chunk, mlp_rows(group.other(chunk)))
        second.swap(chunk, part)
    for chunk in range(2):
        own = group.own(chunk)
        grad = grad_out[chunk] + back(second, chunk, middle[chunk], gains[1:2], 0)
        grad_out[chunk] = grad
        share.give(chunk, grad.astype(LOW))
        grad_low_out[own] = share.full[own]
        d_mixed_out[own] = through(share.full[own], w_out[...]).astype(LOW)
        share.await_other(chunk)
        other = group.other(chunk)
        grad_low_out[other] = share.full[other]
        d_mixed_out[other] = through(share.full[other], w_out[...]).astype(LOW)
    for item in (first, second, share_mlp, share):
        item.close()


def leave_kernel(
    d_query, d_key, d_value, w_query, w_key, w_value, start, grad_in, gains,
    grad_out, gain_out, *scratch,
):
    group = Group()
    group.greet()
    last = Total(group, scratch[0:4], scratch[4])

    def normed_rows(block):
        return (
            through(d_query[block], w_query[...])
            + through(d_key[block], w_key[...])
            + through(d_value[block], w_value[...])
        )

    mine, theirs = group.high, 1 - group.high
    for chunk, place in ((0, theirs), (1, mine)):
        last.give(chunk, normed_rows(group.other(place)))
        part = normed_rows(group.own(place))
        if chunk == 0:
            last.swap(0, part)
        else:
            kept = last.pair_sum(1, part)
    last.copies["far", 0].wait_recv()
    d_values, d_gain = norm_back(kept + last.into[0].astype(FULL), start[mine], gains[0:1])
    grad_out[...] = grad_in[mine] + d_values
    gain_out[...] = jnp.sum(d_gain, axis=0, keepdims=True)
    last.close()


def run_kernel(kernel, ident, outs, scratch, args, flops):
    shapes = tuple(jax.ShapeDtypeStruct(shape, dtype) for shape, dtype in outs)
    moved = sum(a.size * a.dtype.itemsize for a in args) + sum(
        math.prod(a.shape) * a.dtype.itemsize for a in shapes
    )
    return pl.pallas_call(
        kernel,
        out_shape=shapes,
        in_specs=[VMEM] * len(args),
        out_specs=tuple([VMEM] * len(outs)),
        scratch_shapes=scratch,
        cost_estimate=pl.CostEstimate(flops=flops, bytes_accessed=moved, transcendentals=0),
        compiler_params=pltpu.CompilerParams(
            collective_id=ident, has_side_effects=True, vmem_limit_bytes=VMEM_BYTES
        ),
    )(*args)


def blocks(array):
    return array.reshape((4, array.shape[0] // 4) + array.shape[1:])


def flat(array):
    return array.reshape((array.shape[0] * array.shape[1],) + array.shape[2:])


def halve(array, axis):
    size = lax.axis_size(axis)
    index = lax.axis_index(axis)
    pieces = array.reshape((size, array.shape[0] // size) + array.shape[1:])
    distance = 1
    while distance < size:
        bit = (index // distance) % 2
        pairs = pieces.reshape((pieces.shape[0] // 2, 2) + pieces.shape[1:])
        keep = lax.dynamic_index_in_dim(pairs, bit, axis=1, keepdims=False)
        give = lax.dynamic_index_in_dim(pairs, 1 - bit, axis=1, keepdims=False)
        got = lax.ppermute(give, axis, [(i, i ^ distance) for i in range(size)])
        pieces = (keep.astype(FULL) + got.astype(FULL)).astype(array.dtype)
        distance *= 2
    return pieces[0]


def scatter_sums(parts):
    whole = jnp.concatenate([part.astype(LOW) for part in parts], axis=1)
    mine = halve(whole, "seq").astype(FULL)
    out = []
    first = 0
    for part in parts:
        out.append(mine[:, first : first + part.shape[1]])
        first += part.shape[1]
    return out


def scatter_gains(gains):
    count = lax.axis_size("tensor")
    n_seq = lax.axis_size("seq")
    shaped = gains.reshape(4, n_seq, -1).transpose(1, 0, 2)
    mine = halve(shaped, "seq")
    distance = 1
    while distance < count:
        mine = mine + lax.ppermute(mine, "tensor", [(i, i ^ distance) for i in range(count)])
        distance *= 2
    width = mine.shape[-1] // count
    return lax.dynamic_slice_in_dim(mine[0] if mine.ndim == 3 else mine, lax.axis_index("tensor") * width, width, 1)


def on_device(
    inputs,
    cotangent,
    seq_lengths,
    norm_gains,
    query_one,
    key_one,
    value_one,
    out_one,
    gate_one,
    up_one,
    down_one,
    query_two,
    key_two,
    value_two,
    out_two,
    gate_two,
    up_two,
    down_two,
):
    rows = inputs.shape[0]
    stretch = rows * lax.axis_size("tensor")
    n_seq = lax.axis_size("seq")
    position = lax.axis_index("seq")
    stretch_start = position * stretch
    flags = start_flags(seq_lengths, stretch, n_seq)
    place = (seq_lengths, stretch_start, stretch, position, n_seq, flags)
    width = inputs.shape[1]
    units = gate_one.shape[1]
    cols = value_one.shape[1]
    small = query_one.shape[1]
    wide = (4, rows, width)
    own = (2, rows, width)
    total = total_scratch(rows, width)
    share = share_scratch(rows, width)
    one_flops = 2 * stretch * width

    start, normed_one, cot, query1, key1, value1 = run_kernel(
        enter_kernel,
        0,
        [(own, FULL), (wide, LOW), (wide, LOW)] + [((4, rows, n), LOW) for n in (small, small, cols)],
        [pltpu.VMEM((rows, width), LOW)] * 2 + share + share + [pltpu.SemaphoreType.DMA((4,))],
        (inputs, cotangent, norm_gains, query_one, key_one, value_one),
        one_flops * (2 * small + cols),
    )
    query1, key1, value1 = flat(query1), flat(key1), flat(value1)
    mixed, saved_one = taylor_forward(query1, key1, value1, place)
    mixed_one = mixed.astype(LOW)
    middle_one, after_one, normed_two, normed_three, gate1, up1, hidden_one, query2, key2, value2 = run_kernel(
        forward_kernel,
        1,
        [(own, FULL), (own, FULL), (wide, LOW), (wide, LOW)]
        + [((4, rows, units), kind) for kind in (FULL, FULL, LOW)]
        + [((4, rows, cols), LOW)] * 3,
        total + total + share + share,
        (blocks(mixed_one), out_one, start, norm_gains, gate_one, up_one, down_one, query_two, key_two, value_two),
        one_flops * (4 * cols + 3 * units),
    )
    query2, key2, value2 = flat(query2), flat(key2), flat(value2)
    mixed, saved_two = window_forward(query2, key2, value2, place)
    mixed_two = mixed.astype(LOW)
    result, grad, grad_three, d_mixed_two, normed_four, hidden_two, d_gate2, d_up2, gain_four = run_kernel(
        turn_kernel,
        2,
        [((rows, width), LOW), (own, FULL), (wide, LOW), ((4, rows, cols), LOW), (wide, LOW)]
        + [((4, rows, units), LOW)] * 3
        + [((1, width), FULL)],
        total + total + total + share + share + [pltpu.VMEM(own, FULL)],
        (blocks(mixed_two), out_two, after_one, norm_gains, gate_two, up_two, down_two, cot),
        one_flops * (2 * cols + 6 * units),
    )
    feed_two = scatter_sums(
        (
            inner(flat(normed_four), flat(d_gate2)),
            inner(flat(normed_four), flat(d_up2)),
            inner(flat(cot), flat(hidden_two)),
        )
    )
    d_query2, d_key2, d_value2 = window_backward(flat(d_mixed_two), query2, key2, value2, saved_two, place)
    attn_two = scatter_sums(
        (
            inner(flat(normed_three), d_query2),
            inner(flat(normed_three), d_key2),
            inner(flat(normed_three), d_value2),
            inner(flat(grad_three), mixed_two),
        )
    )
    grad, grad_two, grad_one, d_gate1, d_up1, d_mixed_one, gains_mid = run_kernel(
        backward_kernel,
        3,
        [(own, FULL), (wide, LOW), (wide, LOW)]
        + [((4, rows, units), LOW)] * 2
        + [((4, rows, cols), LOW), ((2, width), FULL)],
        total + total + share + share,
        (blocks(d_query2), blocks(d_key2), blocks(d_value2), query_two, key_two, value_two)
        + (after_one, middle_one, grad, norm_gains, gate1, up1, gate_one, up_one, down_one, out_one),
        one_flops * (4 * cols + 3 * units),
    )
    feed_one = scatter_sums(
        (
            inner(flat(normed_two), flat(d_gate1)),
            inner(flat(normed_two), flat(d_up1)),
            inner(flat(grad_two), flat(hidden_one)),
        )
    )
    d_query1, d_key1, d_value1 = taylor_backward(flat(d_mixed_one), query1, key1, value1, saved_one, place)
    attn_one = scatter_sums(
        (
            inner(flat(normed_one), d_query1),
            inner(flat(normed_one), d_key1),
            inner(flat(normed_one), d_value1),
            inner(flat(grad_one), mixed_one),
        )
    )
    grad, gain_one = run_kernel(
        leave_kernel,
        4,
        [((rows, width), FULL), ((1, width), FULL)],
        total,
        (blocks(d_query1), blocks(d_key1), blocks(d_value1), query_one, key_one, value_one, start, grad, norm_gains),
        one_flops * (2 * small + cols),
    )
    gains = scatter_gains(jnp.concatenate([gain_one, gains_mid, gain_four]))
    return (
        result,
        grad,
        gains,
        attn_one[0],
        attn_one[1],
        attn_one[2],
        attn_one[3].T,
        feed_one[0],
        feed_one[1],
        feed_one[2].T,
        attn_two[0],
        attn_two[1],
        attn_two[2],
        attn_two[3].T,
        feed_two[0],
        feed_two[1],
        feed_two[2].T,
    )


def solution(mesh):
    return jax.shard_map(
        on_device,
        mesh=mesh,
        in_specs=(
            P(("seq", "tensor"), None),
            P(("seq", "tensor"), None),
            P(),
            P(),
            P(None, "tensor"),
            P(None, "tensor"),
            P(None, "tensor"),
            P("tensor", None),
            P(None, "tensor"),
            P(None, "tensor"),
            P("tensor", None),
            P(None, "tensor"),
            P(None, "tensor"),
            P(None, "tensor"),
            P("tensor", None),
            P(None, "tensor"),
            P(None, "tensor"),
            P("tensor", None),
        ),
        out_specs=(
            P(("seq", "tensor"), None),
            P(("seq", "tensor"), None),
            P(None, ("seq", "tensor")),
            P("seq", "tensor"),
            P("seq", "tensor"),
            P("seq", "tensor"),
            P("tensor", "seq"),
            P("seq", "tensor"),
            P("seq", "tensor"),
            P("tensor", "seq"),
            P("seq", "tensor"),
            P("seq", "tensor"),
            P("seq", "tensor"),
            P("tensor", "seq"),
            P("seq", "tensor"),
            P("seq", "tensor"),
            P("tensor", "seq"),
        ),
        check_vma=False,
    )
```

```python
import functools
import math
import types

import jax
import jax.numpy as jnp
import numpy as np
from jax import lax
from jax.experimental import pallas as pl
from jax.experimental.pallas import tpu as pltpu
from jax.sharding import PartitionSpec as P

FEAT = 16
HEAD = 64
WINDOW = 64
BLOCK = 128
EPS = 1e-05
FLOOR_SCORE = -1e30
MESH = pl.DeviceIdType.MESH
LOW = jnp.bfloat16
FULL = jnp.float32
VMEM_BYTES = 60 * 1024 * 1024
HALF = BLOCK // 2
CHUNKS = 4
PAIRS = [(a, b) for a in range(FEAT + 1) for b in range(a, FEAT + 1)]
FEATS = -(-len(PAIRS) // 16) * 16
NORM_ROWS = 16


def plain(left, right):
    return jnp.dot(left, right, preferred_element_type=FULL)


def inner(left, right):
    return lax.dot_general(left, right, (((0,), (0,)), ((), ())), preferred_element_type=FULL)


def through(left, right):
    return lax.dot_general(left, right, (((1,), (1,)), ((), ())), preferred_element_type=FULL)


def flat(array):
    return array.reshape((math.prod(array.shape[:-1]), array.shape[-1]))


class Group:
    def __init__(self):
        index = lax.axis_index("tensor")
        self.index = index
        self.low = lax.rem(index, 2)
        self.high = index // 2
        self.pair = dict(tensor=index + 1 - 2 * self.low)
        self.partner = dict(tensor=lax.rem(index + 2, 4))

    def mine(self, chunk):
        return jnp.where(self.high == chunk // 2, 1.0, 0.0)

    def split(self, part, count, by_rows=False):
        if by_rows:
            zero, one = part.reshape(2, count, HALF, -1)
        else:
            whole = part.reshape(count, 2, HALF, -1)
            zero, one = whole[:, 0], whole[:, 1]
        even = self.low == 0
        return jnp.where(even, zero, one), jnp.where(even, one, zero)

    def own_rows(self, ref, chunk, count):
        return ref.at[self.low + 2 * (chunk // 2), pl.ds(chunk % 2, count)]

    def own_chunks(self, ref, chunk, count):
        return ref.at[pl.ds(chunk, count), self.low]


def chunk_rows(ref, chunk, count=1):
    first, half = 2 * (chunk // 2), chunk % 2
    if len(ref.shape) == 4:
        return flat(ref[first : first + 2, half : half + count])
    starts = [block * BLOCK + half * HALF for block in (first, first + 1)]
    return jnp.concatenate([ref[start : start + count * HALF] for start in starts], axis=0)


def put_rows(ref, chunk, value, ahead=0):
    for side in range(2):
        start = ahead + (2 * (chunk // 2) + side) * BLOCK + chunk % 2 * HALF
        ref[start : start + HALF] = value[side * HALF : (side + 1) * HALF]


class Line:
    def __init__(self, size):
        self.size = size
        self.index = lax.axis_index("seq")
        self.after = dict(seq=lax.rem(self.index + 1, size))
        self.before = dict(seq=lax.rem(self.index + size - 1, size))

    def flip(self, relative):
        found = 0
        bit = 1
        while bit < self.size:
            found = found + bit * lax.rem(self.index // bit + relative // bit, 2)
            bit *= 2
        return found


def greet(peers, everyone=None):
    barrier = pltpu.get_barrier_semaphore()
    for peer in peers:
        pl.semaphore_signal(barrier, inc=1, device_id=peer, device_id_type=MESH)
    count = len(peers)
    if everyone is not None:

        def call(step, carry):
            peer = dict(seq=lax.rem(everyone.index + step, everyone.size))
            pl.semaphore_signal(barrier, inc=1, device_id=peer, device_id_type=MESH)
            return carry

        lax.fori_loop(1, everyone.size, call, 0)
        count += everyone.size - 1
    pl.semaphore_wait(barrier, count)


def remote(src, dst, send, recv, device):
    return pltpu.make_async_remote_copy(
        src_ref=src, dst_ref=dst, send_sem=send, recv_sem=recv, device_id=device, device_id_type=MESH
    )


def send(src, dst, send_sem, recv_sem, device):
    copy = remote(src, dst, send_sem, recv_sem, device)
    copy.start()
    return copy


class Total:
    def __init__(self, group, keep, buffers):
        self.group = group
        self.keep = keep
        self.pair_out, self.pair_in, self.out, self.into, self.sems = buffers
        self.pairs = {}
        self.fars = {}
        self.arriving = {}
        self.arrived = set()

    @staticmethod
    def scratch(width):
        return [pltpu.VMEM((CHUNKS, HALF, width), LOW)] * 4 + [pltpu.SemaphoreType.DMA((4, CHUNKS))]

    def give(self, chunk, part, count=1, by_rows=False):
        own, other = self.group.split(part, count, by_rows)
        place = pl.ds(chunk, count)
        self.keep[place] = own
        self.pair_out[place] = other.astype(LOW)
        self.pairs[chunk] = send(
            self.pair_out.at[place],
            self.pair_in.at[place],
            self.sems.at[0, chunk],
            self.sems.at[1, chunk],
            self.group.pair,
        )
        self.arriving.update({chunk + step: chunk for step in range(count)})

    def pair_sum(self, chunk, count=1):
        given = self.arriving[chunk]
        if given not in self.arrived:
            self.arrived.add(given)
            self.pairs[given].wait_recv()
        place = pl.ds(chunk, count)
        return self.keep[place] + self.pair_in[place].astype(FULL)

    def swap(self, chunk, count=1):
        place = pl.ds(chunk, count)
        self.out[place] = self.pair_sum(chunk, count).astype(LOW)
        self.fars[chunk] = send(
            self.out.at[place],
            self.into.at[place],
            self.sems.at[2, chunk],
            self.sems.at[3, chunk],
            self.group.partner,
        )

    def swap_half(self):
        for chunk in range(0, CHUNKS, 2):
            self.out[chunk : chunk + 2] = self.pair_sum(chunk, 2).astype(LOW)
        self.fars[0] = send(
            self.out.at[pl.ds(2 - 2 * self.group.high, 2)],
            self.into.at[pl.ds(0, 2)],
            self.sems.at[2, 0],
            self.sems.at[3, 0],
            self.group.partner,
        )

    def take(self, chunk, count=1):
        self.fars[chunk].wait_recv()
        place = pl.ds(chunk, count)
        return self.out[place].astype(FULL) + self.into[place].astype(FULL)

    def take_half(self):
        self.fars[0].wait_recv()
        return self.out[pl.ds(2 * self.group.high, 2)].astype(FULL) + self.into[0:2].astype(FULL)

    def close(self):
        for copy in list(self.pairs.values()) + list(self.fars.values()):
            copy.wait_send()


class Share:
    def __init__(self, group, full, sems, place):
        self.group = group
        self.full = full
        self.sems = sems
        self.place = place
        self.copies = {}

    def give(self, chunk, value, count=1):
        rows = self.place(self.full, chunk, count)
        rows[...] = value
        self.copies[chunk] = send(
            rows, rows, self.sems.at[0, chunk], self.sems.at[1, chunk], self.group.pair
        )

    def await_other(self, chunk):
        self.copies[chunk].wait_recv()

    def close(self):
        for copy in self.copies.values():
            copy.wait_send()


def share_sems():
    return pltpu.SemaphoreType.DMA((2, CHUNKS))


def relay(first, second, share, enter, work, count=1, order=None, between=lambda: None):
    starts = order or list(range(0, CHUNKS, count))
    for step in range(len(starts) + 1):
        if step < len(starts):
            share.give(starts[step], enter(starts[step], first.take(starts[step], count)), count)
        if step > 1:
            second.swap(starts[step - 2], count)
        if step > 0:
            chunk = starts[step - 1]
            share.await_other(chunk)
            second.give(chunk, work(chunk), count)
        between()
    second.swap(starts[-1], count)


class Later:
    def __init__(self, source, target, sem):
        self.copy = pltpu.make_async_copy(source, target, sem)
        self.copy.start()
        self.target = target
        self.waiting = True

    def __call__(self):
        if self.waiting:
            self.copy.wait()
            self.waiting = False
        return self.target


class Saved:
    def __init__(self, ref, target, sem):
        self.ref = ref
        self.target = target
        self.sem = sem
        self.copy = None

    def store(self):
        self.copy = pltpu.make_async_copy(self.ref, self.target, self.sem)
        self.copy.start()


class Scatter:
    def __init__(self, line, base, give, got, sems, first=0):
        self.line = line
        self.ready, self.base = base
        self.give = give
        self.got = got
        self.sems = sems
        self.first = first

    @staticmethod
    def blocks(size, width):
        return [pltpu.VMEM((size >> (at + 1), width, BLOCK), LOW) for at in range(int(math.log2(size)))]

    @staticmethod
    def signals(size):
        return [pltpu.SemaphoreType.DMA((2, size >> (at + 1))) for at in range(int(math.log2(size)))]

    def part(self, relative, upto):
        total = self.base(self.line.flip(relative))
        for at in range(upto):
            total = total + self.got[at][relative // 2 ** (at + 1)].astype(FULL)
        return total

    def copy(self, at, index):
        return remote(
            self.give[at].at[index],
            self.got[at].at[index],
            self.sems[at].at[0, index],
            self.sems[at].at[1, index],
            dict(seq=self.line.flip(2**at)),
        )

    def each(self, at, body):
        def step(index, carry):
            body(index)
            return carry

        lax.fori_loop(0, self.line.size >> (at + 1), step, 0)

    def start(self, at):
        self.ready()
        if at > self.first:
            self.arrive(at - 1)

        def body(index):
            self.give[at][index] = self.part(2**at * (2 * index + 1), at).astype(self.give[at].dtype)
            self.copy(at, index).start()

        self.each(at, body)

    def arrive(self, at):
        self.each(at, lambda index: self.copy(at, index).wait_recv())

    def finish(self, out=None):
        self.arrive(len(self.got) - 1)
        found = self.part(0, len(self.got))
        if out is None:
            return found
        out[...] = found

    def sent(self, upto=None):
        for at in range(self.first, len(self.sems) if upto is None else upto):
            self.each(at, lambda index, at=at: self.copy(at, index).wait_send())


def product(left, right):
    def base(block):
        columns = pl.ds(pl.multiple_of(block * BLOCK, BLOCK), BLOCK)
        return plain(right()[...], flat(left()[:, :, :, columns]))

    def ready():
        left()
        right()

    return ready, base


def norm_apply(values, gain):
    inverse = lax.rsqrt(jnp.mean(values * values, axis=-1, keepdims=True) + EPS)
    return (values * inverse * gain).astype(LOW)


def norm_back(grad, values, gain):
    inverse = lax.rsqrt(jnp.mean(values * values, axis=-1, keepdims=True) + EPS)
    scaled = values * inverse
    d_scaled = grad * gain
    d_values = inverse * (d_scaled - scaled * jnp.mean(d_scaled * scaled, axis=-1, keepdims=True))
    return d_values, jnp.sum(grad * scaled, axis=0, keepdims=True)


def gate_forward(gate, up_val):
    return gate * up_val / (1.0 + jnp.exp(-gate))


def gate_backward(d_hidden, gate, up_val):
    sigma = 1.0 / (1.0 + jnp.exp(-gate))
    return d_hidden * up_val * sigma * (1.0 + gate * (1.0 - sigma)), d_hidden * gate * sigma


def segment_of(lengths, positions):
    end = 0
    found = jnp.zeros_like(positions)
    for index in range(lengths.shape[0]):
        end = end + lengths[index]
        found = found + jnp.where(positions >= end, 1, 0)
    return found


def ramp(shape, axis, first):
    return lax.broadcasted_iota(jnp.int32, shape, axis) + first


def same(left, right):
    return jnp.where(left == right, 1.0, 0.0)


def feature_tables():
    choice = np.zeros((2, FEAT, FEATS), np.float32)
    rows = np.zeros((8, FEATS), np.float32)
    for index, pair in enumerate(PAIRS):
        for side, entry in enumerate(pair):
            if entry < FEAT:
                choice[side, entry, index] = 1.0
            else:
                rows[side, index] = 1.0
        rows[2, index] = 0.5**0.5 if pair[0] == pair[1] and pair[0] < FEAT else 1.0
    return jnp.asarray(choice, LOW), jnp.asarray(rows, FULL)


class Taylor:
    def __init__(self, line, k, query, key, value):
        self.line = line
        self.k = k
        self.query = query
        self.key = key
        self.value = value
        self.rows = query.shape[0]
        self.count = self.rows // BLOCK
        self.heads = value.shape[1] // HEAD
        start = line.index * self.rows
        self.start = start
        column = segment_of(k.lengths, ramp((self.rows, 1), 0, start))
        last = segment_of(k.lengths, ramp((1, 1), 0, start + self.rows - 1))
        before = segment_of(k.lengths, ramp((1, 1), 0, start - 1))
        self.last = last
        self.before = before
        self.segments = column
        self.across = segment_of(k.lengths, ramp((1, self.rows), 1, start))
        self.tail = same(column, last)
        self.carried = same(column, before)
        self.lane = ramp((1, self.heads * HEAD), 1, 0) // HEAD

    def half(self, array, head, upto=None, only=None):
        first, last = (0, upto or self.count) if only is None else (only, only + 1)
        return array[first * BLOCK : last * BLOCK, head * FEAT : (head + 1) * FEAT] * jnp.asarray(0.5, LOW)

    def factors(self, half):
        rows = self.k.feature_rows
        left = plain(half, self.k.feature_choice[0]) + rows[0:1]
        right = plain(half, self.k.feature_choice[1]) + rows[1:2]
        return left, right

    def features(self, array, head):
        left, right = self.factors(self.half(array, head))
        return left * right * self.k.feature_rows[2:3]

    def features_back(self, grad, array, head):
        left, right = self.factors(self.half(array, head))
        weighted = grad * self.k.feature_rows[2:3]
        return through((weighted * right).astype(LOW), self.k.feature_choice[0]) + through(
            (weighted * left).astype(LOW), self.k.feature_choice[1]
        )

    def of_head(self, head, array):
        return jnp.where(self.lane == head, array, jnp.zeros_like(array))

    def mask(self, block):
        upto = (block + 1) * BLOCK
        rows = ramp((BLOCK, 1), 0, block * BLOCK)
        allowed = (ramp((1, upto), 1, 0) <= rows) & (
            self.across[:, :upto] == self.segments[block * BLOCK : upto]
        )
        return jnp.where(allowed, 1.0, 0.0)

    def send_state(self, forward):
        k, line = self.k, self.line

        def step(other, carry):
            @pl.when((other > line.index) if forward else (other < line.index))
            def _():
                self.state_copy(other).start()

            return carry

        lax.fori_loop(0, line.size, step, 0)

    def state_copy(self, other):
        k = self.k
        return remote(
            k.state_own,
            k.state_slots.at[self.line.index],
            k.state_sems.at[0, other],
            k.state_sems.at[1, self.line.index],
            dict(seq=other),
        )

    def state_arrival(self, other):
        k = self.k
        return remote(
            k.state_own,
            k.state_slots.at[other],
            k.state_sems.at[0, other],
            k.state_sems.at[1, other],
            dict(seq=other),
        )

    def take_state(self, total, forward):
        k, line = self.k, self.line
        total[...] = jnp.zeros_like(total)

        def step(other, carry):
            @pl.when((other < line.index) if forward else (other > line.index))
            def _():
                self.state_arrival(other).wait_recv()
                if forward:
                    edge = segment_of(k.lengths, ramp((1, 1), 0, (other + 1) * self.rows - 1))
                    weight = same(edge, self.before)
                else:
                    edge = segment_of(k.lengths, ramp((1, 1), 0, other * self.rows - 1))
                    weight = same(edge, self.last)
                total[...] += weight * k.state_slots[other].astype(FULL)

            return carry

        lax.fori_loop(0, line.size, step, 0)

    def close(self, forward):
        line = self.line

        def step(other, carry):
            @pl.when((other > line.index) if forward else (other < line.index))
            def _():
                self.state_copy(other).wait_send()

            return carry

        lax.fori_loop(0, line.size, step, 0)

    @staticmethod
    def scratch(size, cols):
        shape = (FEATS + NORM_ROWS, cols)
        return dict(
            state_own=pltpu.VMEM(shape, LOW),
            state_build=pltpu.VMEM(shape, FULL),
            state_slots=pltpu.VMEM((size,) + shape, LOW),
            state_sems=pltpu.SemaphoreType.DMA((2, size)),
        )

    def forward(self):
        k = self.k
        value = self.value[...]
        build = k.state_build
        build[...] = jnp.zeros_like(build)
        state = jnp.zeros((FEATS, value.shape[1]), FULL)
        for head in range(self.heads):
            feats = self.features(self.key, head) * self.tail
            state = state + self.of_head(head, inner(feats.astype(LOW), value))
            build[FEATS + head : FEATS + head + 1, :FEATS] = jnp.sum(feats, axis=0, keepdims=True)
        build[:FEATS] = state
        k.state_own[...] = build[...].astype(LOW)
        self.send_state(True)
        for block in range(self.count):
            allowed = self.mask(block)
            rows = slice(block * BLOCK, (block + 1) * BLOCK)
            for head in range(self.heads):
                places = slice(head * HEAD, (head + 1) * HEAD)
                score = through(self.half(self.query, head, only=block), self.half(self.key, head, block + 1))
                score = allowed * (1.0 + score + 0.5 * score * score)
                k.mixed[rows, places] = plain(score.astype(LOW), value[: (block + 1) * BLOCK, places])
                k.inverse[rows, places] = jnp.broadcast_to(jnp.sum(score, axis=1, keepdims=True), (BLOCK, HEAD))
        self.take_state(k.carry, True)
        state = k.carry[:FEATS].astype(LOW)
        numerator = jnp.zeros((self.rows, value.shape[1]), FULL)
        totals = jnp.zeros((self.rows, value.shape[1]), FULL)
        for head in range(self.heads):
            feats = self.features(self.query, head)
            numerator = numerator + self.of_head(head, plain(feats.astype(LOW), state))
            norm = k.carry[FEATS + head : FEATS + head + 1, :FEATS]
            totals = totals + self.of_head(head, jnp.sum(feats * norm, axis=1, keepdims=True) + jnp.zeros_like(totals))
        inverse = 1.0 / (k.inverse[...] + self.carried * totals)
        mixed = (k.mixed[...] + self.carried * numerator) * inverse
        k.inverse[...] = inverse
        k.mixed[...] = mixed
        k.mixed_low[...] = mixed.astype(LOW)
        k.mixed_turned[...] = mixed.T.astype(LOW)

    def backward(self, d_mixed):
        k = self.k
        value = self.value[...]
        d_out = d_mixed[...].astype(FULL)
        d_numer = d_out * k.inverse[...]
        d_low = d_numer.astype(LOW)
        product = d_numer * k.mixed[...]
        d_totals = [
            -jnp.sum(product[:, head * HEAD : (head + 1) * HEAD], axis=1, keepdims=True) for head in range(self.heads)
        ]
        build = k.state_build
        build[...] = jnp.zeros_like(build)
        state = jnp.zeros((FEATS, value.shape[1]), FULL)
        for head in range(self.heads):
            feats = self.features(self.query, head) * self.carried
            state = state + self.of_head(head, inner(feats.astype(LOW), d_low))
            build[FEATS + head : FEATS + head + 1, :FEATS] = jnp.sum(feats * d_totals[head], axis=0, keepdims=True)
        build[:FEATS] = state
        k.state_own[...] = build[...].astype(LOW)
        self.send_state(False)
        yield
        carry = k.carry[:FEATS].astype(LOW)
        k.d_key_acc[...] = jnp.zeros_like(k.d_key_acc)
        k.d_value_acc[...] = jnp.zeros_like(k.d_value_acc)
        for head in range(self.heads):
            norm = k.carry[FEATS + head : FEATS + head + 1, :FEATS]
            d_feats = self.carried * (through(self.of_head(head, d_low), carry) + d_totals[head] * norm)
            k.d_query_acc[:, head * FEAT : (head + 1) * FEAT] = self.features_back(d_feats, self.query, head)
        for block in range(self.count):
            allowed = self.mask(block)
            upto = (block + 1) * BLOCK
            rows = slice(block * BLOCK, upto)
            for head in range(self.heads):
                places = slice(head * HEAD, (head + 1) * HEAD)
                narrow = slice(head * FEAT, (head + 1) * FEAT)
                query = self.half(self.query, head, only=block)
                key = self.half(self.key, head, block + 1)
                score = through(query, key)
                d_rows = d_low[rows, places]
                d_score = through(d_rows, value[:upto, places]) + d_totals[head][rows]
                d_score = (allowed * d_score * (1.0 + score)).astype(LOW)
                score = (allowed * (1.0 + score + 0.5 * score * score)).astype(LOW)
                k.d_query_acc[rows, narrow] += plain(d_score, key)
                k.d_key_acc[:upto, narrow] += inner(d_score, query)
                k.d_value_acc[:upto, places] += inner(score, d_rows)
            yield
        self.take_state(k.grad_carry, False)
        carry = k.grad_carry[:FEATS].astype(LOW)
        for head in range(self.heads):
            norm = k.grad_carry[FEATS + head : FEATS + head + 1, :FEATS]
            d_feats = self.tail * (through(self.of_head(head, value), carry) + norm)
            k.d_key_acc[:, head * FEAT : (head + 1) * FEAT] += self.features_back(d_feats, self.key, head)
            feats = self.features(self.key, head).astype(LOW)
            k.d_value_acc[...] += self.of_head(head, self.tail * plain(feats, carry))


def window_mask(k, line, block, rows):
    span = BLOCK + WINDOW
    first = line.index * rows + block * BLOCK
    query = ramp((BLOCK, 1), 0, first)
    key = ramp((1, span), 1, first - WINDOW)
    return (
        (key <= query)
        & (key > query - WINDOW)
        & (key >= 0)
        & (segment_of(k.lengths, key) == segment_of(k.lengths, query))
    )


def window_weights(query, key, allowed):
    score = jnp.where(allowed, through(query, key) * HEAD**-0.5, FLOOR_SCORE)
    weight = jnp.exp(score - jnp.max(score, axis=1, keepdims=True))
    return weight / jnp.sum(weight, axis=1, keepdims=True)


def window_forward(k, line, block):
    own = slice(block * BLOCK, (block + 1) * BLOCK)
    allowed = window_mask(k, line, block, k.query2.shape[0])
    span = slice(block * BLOCK, (block + 1) * BLOCK + WINDOW)
    outs = []
    for head in range(k.keys.shape[1] // HEAD):
        places = slice(head * HEAD, (head + 1) * HEAD)
        weight = window_weights(k.query2[own, places], k.keys[span, places], allowed)
        outs.append(plain(weight.astype(LOW), k.values[span, places]))
    whole = jnp.concatenate(outs, axis=1)
    k.window_low[own] = whole.astype(LOW)
    k.window_turned[:, own] = whole.T.astype(LOW)


def window_backward(k, line, block):
    own = slice(block * BLOCK, (block + 1) * BLOCK)
    allowed = window_mask(k, line, block, k.query2.shape[0])
    span = slice(block * BLOCK, (block + 1) * BLOCK + WINDOW)
    grads = []
    for head in range(k.keys.shape[1] // HEAD):
        places = slice(head * HEAD, (head + 1) * HEAD)
        query = k.query2[own, places]
        key = k.keys[span, places]
        d_out = k.d_window[own, places]
        weight = window_weights(query, key, allowed)
        d_weight = through(d_out, k.values[span, places])
        d_score = weight * (d_weight - jnp.sum(weight * d_weight, axis=1, keepdims=True)) * HEAD**-0.5
        d_score = d_score.astype(LOW)
        grads.append(plain(d_score, key))
        k.d_keys[span, places] += inner(d_score, query)
        k.d_values[span, places] += inner(weight.astype(LOW), d_out)
    whole = jnp.concatenate(grads, axis=1)
    k.d_query2[own] = whole.astype(LOW)
    k.d_turned2[: whole.shape[1], own] = whole.T.astype(LOW)


def first_kernel(k, size):
    group, line = Group(), Line(size)
    greet([group.pair, group.partner], line)
    width = k.inputs.shape[1]
    rows = k.query.shape[0]
    cols = k.value.shape[1]
    total_a, total_b, total_c = (Total(group, k.keep, k.totals[i]) for i in range(3))
    closing = [total_a, total_b]

    def offer(step, block, raw):
        values = raw.astype(FULL)
        k.start[pl.ds(2 * (block // 2), 2)] = values.reshape(2, HALF, width)
        k.normed_one[block] = norm_apply(values, k.gains[0:1]).reshape(2, HALF, width)
        place = k.normed_one.at[block]
        copy = send(place, place, k.near_sems.at[0, step], k.near_sems.at[1, step], group.pair)
        copy.wait_recv()
        return copy

    def project_one(pair):
        normed = flat(k.normed_one[pl.ds(2 * pair, 2)])
        place = pl.ds(pl.multiple_of(pair * 2 * BLOCK, 2 * BLOCK), 2 * BLOCK)
        k.key[place] = through(normed, k.w_key_one[...]).astype(LOW)
        k.value[place] = plain(normed, k.w_value_one[...]).astype(LOW)
        k.query[place] = through(normed, k.w_query_one[...]).astype(LOW)

    def offer_cot(step, half, raw):
        place = k.cot.at[pl.ds(2 * half, 2), group.low]
        place[...] = raw.reshape(2, HALF, width)
        return send(place, place, k.near_sems.at[0, 2 + step], k.near_sems.at[1, 2 + step], group.pair)

    far = send(k.inputs, k.rows_in, k.far_sems.at[0, 0], k.far_sems.at[1, 0], group.partner)
    copies = [offer(0, group.index, k.inputs[...])]
    project_one(group.high)
    far.wait_recv()
    far_cot = send(k.cotangent, k.cot_in, k.far_sems.at[0, 1], k.far_sems.at[1, 1], group.partner)
    copies.append(offer(1, lax.rem(group.index + 2, 4), k.rows_in[...]))
    project_one(1 - group.high)
    copies.append(offer_cot(0, group.high, k.cotangent[...]))
    taylor = Taylor(line, k, k.query, k.key, k.value)
    taylor.forward()
    for item in (k.start, k.normed_one, k.query, k.key, k.value, k.mixed, k.inverse, k.mixed_turned, k.carry):
        k.store(item)
    far_cot.wait_recv()
    copies.append(offer_cot(1, 1 - group.high, k.cot_in[...]))

    share = Share(group, k.normed_two, k.share_sems.at[0], group.own_chunks)
    closing.append(share)

    def enter_mlp(chunk, total):
        middle = k.start[chunk : chunk + 1] + total
        k.middle[chunk : chunk + 1] = middle
        return norm_apply(middle, k.gains[1:2])

    def mlp_one(chunk):
        normed = flat(k.normed_two[chunk])
        gate = through(normed, k.w_gate_one()[...])
        up_val = through(normed, k.w_up_one()[...])
        k.gate[chunk] = gate.astype(LOW).reshape(k.gate.shape[1:])
        k.up[chunk] = up_val.astype(LOW).reshape(k.up.shape[1:])
        hidden = gate_forward(gate, up_val)
        k.hidden_one[:, chunk * BLOCK : (chunk + 1) * BLOCK] = hidden.T.astype(LOW)
        return plain(hidden.astype(LOW), k.w_down_one()[...])

    for chunk in range(0, CHUNKS, 2):
        part = plain(chunk_rows(k.mixed_low, chunk, 2), k.w_out_one()[...])
        total_a.give(chunk, part, 2, by_rows=True)
    for chunk in range(CHUNKS):
        total_a.swap(chunk)
    relay(total_a, total_b, share, enter_mlp, mlp_one)
    for item in (k.middle, k.normed_two, k.gate, k.up, k.hidden_one):
        k.store(item)

    share = Share(group, k.normed_three, k.share_sems.at[1], group.own_rows)
    closing.append(share)

    def project_two(chunk):
        normed = chunk_rows(k.normed_three, chunk)
        put_rows(k.keys, chunk, plain(normed, k.w_key_two()[...]).astype(LOW), WINDOW)
        put_rows(k.values, chunk, plain(normed, k.w_value_two()[...]).astype(LOW), WINDOW)
        put_rows(k.query2, chunk, plain(normed, k.w_query_two()[...]).astype(LOW))

    for step in range(CHUNKS + 1):
        if step < CHUNKS:
            after = k.middle[step : step + 1] + total_b.take(step)
            k.after[step : step + 1] = after
            share.give(step, norm_apply(after, k.gains[2:3]))
        if step > 0:
            share.await_other(step - 1)
            project_two(step - 1)
        if step == 2:
            window_forward(k, line, 1)
    k.store(k.after)
    k.store(k.normed_three)
    halo = Halo(k, 0, (k.keys, k.values), slice(rows, rows + WINDOW), line.after)
    for item in closing:
        item.close()
    closing = [halo]
    total_a, total_b = (Total(group, k.keep, k.totals[i]) for i in range(2))
    closing += [total_a, total_b, total_c]
    order = [2, 3, 0, 1]
    for chunk in (2, 0):
        if chunk == 2:
            window_forward(k, line, 2)
            window_forward(k, line, 3)
        else:
            for index, target in enumerate((k.keys, k.values)):
                target[:WINDOW] = halo.take(index)
            window_forward(k, line, 0)
        part = plain(chunk_rows(k.window_low, chunk, 2), k.w_out_two()[...])
        total_a.give(chunk, part, 2, by_rows=True)
        total_a.swap(chunk)
        total_a.swap(chunk + 1)
    k.store(k.window_turned)

    gain = k.gains[3:4]
    share = Share(group, k.normed_four, k.share_sems.at[2], group.own_chunks)
    closing.append(share)
    for copy in copies[2:]:
        copy.wait_recv()
    k.store(k.cot)

    def enter_turn(chunk, total):
        middle = k.after[chunk : chunk + 1] + total
        k.middle_two[chunk : chunk + 1] = middle
        return norm_apply(middle, gain)

    def mlp_two(chunk):
        normed = flat(k.normed_four[chunk])
        gate = through(normed, k.w_gate_two()[...])
        up_val = through(normed, k.w_up_two()[...])
        d_hidden = through(flat(k.cot[chunk]), k.w_down_two()[...])
        d_gate, d_up = gate_backward(d_hidden, gate, up_val)
        back = plain(d_gate.astype(LOW), k.w_gate_two()[...]) + plain(d_up.astype(LOW), k.w_up_two()[...])
        hidden = gate_forward(gate, up_val)
        k.hidden[chunk] = hidden.astype(LOW).reshape(k.hidden.shape[1:])
        columns = slice(chunk * BLOCK, (chunk + 1) * BLOCK)
        k.hidden_two[:, columns] = hidden.T.astype(LOW)
        k.d_gate_two[:, columns] = d_gate.T.astype(LOW)
        k.d_up_two[:, columns] = d_up.T.astype(LOW)
        return back

    relay(total_a, total_b, share, enter_turn, mlp_two, order=order)
    for item in (k.normed_four, k.hidden_two, k.d_gate_two, k.d_up_two):
        k.store(item)
    if k.scatter:
        gate_sum = Scatter(
            line, product(lambda: k.normed_four, lambda: k.d_gate_two), k.give, [k.gate_two_got], [k.give_sems]
        )
        gate_sum.start(0)
    for chunk in range(0, CHUNKS, 2):
        total_c.give(chunk, plain(flat(k.hidden[chunk : chunk + 2]), k.w_down_two()[...]), 2)
    total_c.swap_half()

    share = Share(group, k.grad_three, k.share_sems.at[3], group.own_rows)
    closing.append(share)
    k.gain_grad[...] = jnp.zeros_like(k.gain_grad)
    k.d_keys[...] = jnp.zeros_like(k.d_keys)
    k.d_values[...] = jnp.zeros_like(k.d_values)
    for step in range(CHUNKS + 1):
        if step < CHUNKS:
            chunk = order[step]
            d_values, d_gain = norm_back(total_b.take(chunk)[0], k.middle_two[chunk], gain)
            grad = k.cot[chunk, pl.ds(group.low, 1)].astype(FULL) + d_values[None]
            k.grad[chunk : chunk + 1] = grad
            k.gain_grad[...] += group.mine(chunk) * d_gain
            share.give(chunk, grad.astype(LOW))
        if step > 0:
            chunk = order[step - 1]
            share.await_other(chunk)
            put_rows(k.d_window, chunk, through(chunk_rows(k.grad_three, chunk), k.w_out_two()[...]).astype(LOW))
        if step == 2:
            window_backward(k, line, 2)
            window_backward(k, line, 3)
    k.store(k.grad)
    k.store(k.grad_three)
    window_backward(k, line, 0)
    halo = Halo(k, 1, (k.d_keys, k.d_values), slice(0, WINDOW), line.before)
    closing.append(halo)
    window_backward(k, line, 1)
    k.store(k.d_query2)
    k.result[...] = (flat(k.middle_two[pl.ds(2 * group.high, 2)]) + flat(total_c.take_half())).astype(LOW)
    for index, (target, out) in enumerate(((k.d_keys, k.d_key2), (k.d_values, k.d_value2))):
        target[rows : rows + WINDOW] += halo.take(index).astype(FULL)
        whole = target[WINDOW:]
        out[...] = whole.astype(LOW)
        k.store(out)
        k.d_turned2[(index + 1) * cols : (index + 2) * cols] = whole.T.astype(LOW)
    k.store(k.d_turned2)
    if k.scatter:
        gate_sum.arrive(0)
        gate_sum.sent()
    for item in closing:
        item.close()
    for copy in [far, far_cot] + copies:
        copy.wait_send()
    taylor.close(True)


class Halo:
    def __init__(self, k, turn, sources, rows, peer):
        self.into = k.halo_in.at[turn]
        self.copies = []
        for index, source in enumerate(sources):
            k.halo_out[turn, index] = source[rows].astype(LOW)
            self.copies.append(
                send(
                    k.halo_out.at[turn, index],
                    k.halo_in.at[turn, index],
                    k.halo_sems.at[0, turn, index],
                    k.halo_sems.at[1, turn, index],
                    peer,
                )
            )

    def take(self, index):
        self.copies[index].wait_recv()
        return self.into[index]

    def close(self):
        for copy in self.copies:
            copy.wait_send()


def second_kernel(k, size):
    group, line = Group(), Line(size)
    greet([group.pair, group.partner], line)
    width = k.gains.shape[1]
    total_a, total_b = (Total(group, k.keep, k.totals[i]) for i in range(2))
    share_mlp = Share(group, k.grad_two, k.share_sems.at[0], group.own_chunks)
    share = Share(group, k.grad_one, k.share_sems.at[1], group.own_rows)
    taylor = Taylor(line, k, k.query(), k.key(), k.value())
    background = []
    sums = {}

    def tick(count=1):
        for _ in range(count):
            if background:
                background.pop(0)()

    def normed_rows(chunk):
        return (
            through(chunk_rows(k.d_query2(), chunk, 2), k.w_query_two()[...])
            + through(chunk_rows(k.d_key2(), chunk, 2), k.w_key_two()[...])
            + through(chunk_rows(k.d_value2(), chunk, 2), k.w_value_two()[...])
        )

    def back(chunk, total, values, gain, row):
        d_values, d_gain = norm_back(flat(total), flat(values[chunk : chunk + 2]), gain)
        k.gain_rows[row : row + 1] += group.mine(chunk) * d_gain
        return d_values.reshape(2, HALF, width)

    def enter_mlp(chunk, total):
        grad = k.grad()[chunk : chunk + 2] + back(chunk, total, k.after(), k.gains[2:3], 2)
        k.grad()[chunk : chunk + 2] = grad
        return grad.astype(LOW)

    def mlp(chunk):
        d_hidden = through(flat(k.grad_two[chunk : chunk + 2]), k.w_down_one()[...])
        gate = flat(k.gate()[chunk : chunk + 2]).astype(FULL)
        up_val = flat(k.up()[chunk : chunk + 2]).astype(FULL)
        d_gate, d_up = gate_backward(d_hidden, gate, up_val)
        columns = slice(chunk * BLOCK, (chunk + 2) * BLOCK)
        k.d_gate_one[:, columns] = d_gate.T.astype(LOW)
        k.d_up_one[:, columns] = d_up.T.astype(LOW)
        return plain(d_gate.astype(LOW), k.w_gate_one()[...]) + plain(d_up.astype(LOW), k.w_up_one()[...])

    if k.scatter:
        levels = len(k.sems)

        def add(name, left, right, give, got, sems, first=0):
            sums[name] = Scatter(line, product(left, right), give, got, sems, first)

        at = lambda index: [sem.at[index] for sem in k.sems]
        add(1, k.normed_four, k.d_up_two, k.unit_gives[1], k.unit_gots[1], at(1))
        add(2, k.cot, k.hidden_two, k.unit_gives[2], k.unit_gots[2], at(2))
        add(3, k.grad_three, k.window_turned, k.out_gives[0], k.out_gots[0], at(3))
        add(4, k.normed_three, k.d_turned2, k.three_two_gives, k.three_two_gots, at(4))
        add(5, k.normed_two, lambda: k.d_gate_one, k.unit_gives[0], k.unit_gots[3], at(5))
        add(6, k.normed_two, lambda: k.d_up_one, k.unit_gives[1], k.unit_gots[4], at(6))
        add(7, lambda: k.grad_two, k.hidden_one, k.unit_gives[2], k.unit_gots[5], at(7))
        add(8, k.normed_one, lambda: k.d_turned, k.three_one_gives, k.three_one_gots, at(8))
        add(9, lambda: k.grad_one, k.mixed_turned, k.out_gives[1], k.out_gots[1], at(9))
        sums[10] = Scatter(line, (lambda: None, lambda block: k.gain_rows[:, columns_of(block)]), k.gain_gives, k.gain_gots, at(10))
        before = {5: 0, 6: 1, 7: 2}

        def start(name, level):
            def step():
                if level == 0 and name in before:
                    sums[before[name]].sent()
                sums[name].start(level)

            return step

        def finish(name):
            def step():
                sums[name].finish(k.sums[name])
                k.store(k.sums[name])

            return step

        background += [
            start(0, 2),
            start(2, 0),
            start(1, 1),
            finish(0),
            start(1, 2),
            start(3, 0),
            start(4, 0),
            start(2, 1),
            finish(1),
            start(2, 2),
            start(5, 0),
            start(3, 1),
            start(4, 1),
        ]

    k.gain_rows[...] = jnp.zeros_like(k.gain_rows)
    k.gain_rows[3:4] = k.gain_in[...]
    for chunk in range(0, CHUNKS, 2):
        total_a.give(chunk, normed_rows(chunk), 2, by_rows=True)
    for chunk in range(0, CHUNKS, 2):
        total_a.swap(chunk, 2)
    if k.scatter:
        sums[1].start(0)
        add(0, k.normed_four, k.d_gate_two, k.unit_gives[0], [k.gate_two_got()] + k.unit_gots[0][1:], at(0), 1)
        sums[0].start(1)
    relay(total_a, total_b, share_mlp, enter_mlp, mlp, 2, between=tick)
    for step in range(3):
        if step < 2:
            chunk = 2 * step
            grad = k.grad()[chunk : chunk + 2] + back(chunk, total_b.take(chunk, 2), k.middle(), k.gains[1:2], 1)
            k.grad()[chunk : chunk + 2] = grad
            share.give(chunk, grad.astype(LOW), 2)
        if step > 0:
            chunk = 2 * step - 2
            share.await_other(chunk)
            rows = through(chunk_rows(k.grad_one, chunk, 2), k.w_out_one()[...])
            k.d_mixed[chunk * BLOCK : (chunk + 2) * BLOCK] = rows.astype(LOW)
        tick()

    total_a.close()
    total_c = Total(group, k.keep, k.totals[0])
    k.mixed, k.inverse, k.carry = k.mixed(), k.inverse(), k.carry()
    for _ in taylor.backward(k.d_mixed):
        tick()
    d_query = 0.5 * k.d_query_acc[...]
    d_key = 0.5 * k.d_key_acc[...]
    d_value = k.d_value_acc[...]
    small, cols = d_query.shape[1], d_value.shape[1]
    k.d_query_low[...] = d_query.astype(LOW)
    k.d_key_low[...] = d_key.astype(LOW)
    k.d_value_low[...] = d_value.astype(LOW)
    k.d_turned[:small] = d_query.T.astype(LOW)
    k.d_turned[small : 2 * small] = d_key.T.astype(LOW)
    k.d_turned[2 * small : 2 * small + cols] = d_value.T.astype(LOW)
    for chunk in range(0, CHUNKS, 2):
        part = (
            plain(chunk_rows(k.d_query_low, chunk, 2), k.w_query_one()[...])
            + plain(chunk_rows(k.d_key_low, chunk, 2), k.w_key_one()[...])
            + through(chunk_rows(k.d_value_low, chunk, 2), k.w_value_one()[...])
        )
        total_c.give(chunk, part, 2, by_rows=True)
    total_c.swap_half()
    tick()
    half = pl.ds(2 * group.high, 2)
    d_values, d_gain = norm_back(flat(total_c.take_half()), flat(k.start()[half]), k.gains[0:1])
    k.input_grad[...] = flat(k.grad()[half]) + d_values
    k.gain_rows[0:1] = d_gain

    if k.scatter:
        background += [
            start(6, 0),
            start(10, 0),
            finish(2),
            start(3, 2),
            start(10, 1),
            start(4, 2),
            start(5, 1),
            start(7, 0),
            start(10, 2),
            finish(3),
            finish(4),
            start(5, 2),
            start(6, 1),
            start(8, 0),
            start(9, 0),
            finish(5),
            start(6, 2),
            start(7, 1),
            finish(6),
            start(7, 2),
            start(8, 1),
            start(9, 1),
            finish(7),
            start(8, 2),
            start(9, 2),
        ]
        tick(13)
        copies = []
        k.gain_sum[0] = sums[10].finish()
        for index, peer in enumerate((group.pair, group.partner)):
            copy = send(
                k.gain_sum.at[index], k.gain_in_sum.at[index], k.gain_sems.at[0, index], k.gain_sems.at[1, index], peer
            )
            tick(4)
            copy.wait_recv()
            k.gain_sum[index + 1] = k.gain_sum[index] + k.gain_in_sum[index]
            copies.append(copy)
        total = k.gain_sum[2]
        share_of = BLOCK // 4
        found = jnp.zeros((8, share_of), FULL)
        for index in range(4):
            found = found + jnp.where(group.index == index, 1.0, 0.0) * total[:, index * share_of : (index + 1) * share_of]
        k.gain_out[...] = found
        while background:
            tick()
        finish(8)()
        finish(9)()
        for name in (3, 4, 5, 6, 7, 8, 9, 10):
            sums[name].sent()
        for copy in copies:
            copy.wait_send()
    else:
        for item in (k.d_gate_one, k.d_up_one, k.d_turned, k.grad_one, k.grad_two):
            k.store(item)
        k.gain_out[...] = k.gain_rows[...]
    for item in (total_b, total_c, share_mlp, share):
        item.close()
    taylor.close(False)


def columns_of(block):
    return pl.ds(pl.multiple_of(block * BLOCK, BLOCK), BLOCK)


def finish_kernel(k, small, cols):
    k.result[...] = k.result_in[...]
    k.input_grad[...] = k.input_grad_in[...]
    k.gains[...] = k.gains_in[0:4]
    for source, target in zip(k.sums, k.same):
        target[...] = source[...]
    for source, targets in zip(k.threes, k.turned):
        first = 0
        for target in targets:
            if target.shape[1] == BLOCK:
                target[...] = source[first : first + target.shape[0]]
                first += target.shape[0]
            else:
                target[...] = source[first : first + target.shape[1]].T
                first += target.shape[1]


def run_kernel(kernel, ident, ins, outs, scratch, flops, later=None, saved=None, apart=None, scalars=None, extra=None):
    later, saved, apart, scalars = (found or {} for found in (later, saved, apart, scalars))
    is_shape = lambda leaf: isinstance(leaf, tuple) and isinstance(leaf[0], tuple)

    def buffer(array):
        return pltpu.VMEM(array.shape, array.dtype)

    def held(tree):
        return jax.tree.map(lambda leaf: pltpu.VMEM(*leaf), tree, is_leaf=is_shape)

    def sems(tree):
        return jax.tree.map(lambda leaf: pltpu.SemaphoreType.DMA(()), tree, is_leaf=is_shape)

    arguments = (ins, later, scalars)
    results = (outs, saved, apart)
    own = (
        scratch,
        jax.tree.map(buffer, later),
        jax.tree.map(lambda leaf: pltpu.SemaphoreType.DMA(()), later),
        held(saved),
        sems(saved),
    )
    flat_in, tree_in = jax.tree.flatten(arguments)
    flat_out, tree_out = jax.tree.flatten(results, is_leaf=is_shape)
    flat_own, tree_own = jax.tree.flatten(own)

    def body(*refs):
        in_refs = jax.tree.unflatten(tree_in, refs[: len(flat_in)])
        out_refs = jax.tree.unflatten(tree_out, refs[len(flat_in) : len(flat_in) + len(flat_out)])
        own_refs = jax.tree.unflatten(tree_own, refs[len(flat_in) + len(flat_out) :])
        k = types.SimpleNamespace(**(extra or {}))
        for tree in (in_refs[0], in_refs[2], out_refs[0], out_refs[2], own_refs[0], own_refs[3]):
            k.__dict__.update(tree)
        waited = []
        for name, source in in_refs[1].items():
            waited.append(Later(source, own_refs[1][name], own_refs[2][name]))
            setattr(k, name, waited[-1])
        saves = []
        for name in saved:
            parts = zip(*(jax.tree.leaves(tree[name]) for tree in (own_refs[3], out_refs[1], own_refs[4])))
            saves += [Saved(*part) for part in parts]

        def store(ref):
            for item in saves:
                if item.ref is ref:
                    item.store()

        k.store = store
        kernel(k)
        for item in waited:
            item()
        for item in saves:
            if item.copy is None:
                item.store()
            item.copy.wait()

    shapes = [jax.ShapeDtypeStruct(*leaf) for leaf in flat_out]
    moved = sum(a.size * a.dtype.itemsize for a in flat_in) + sum(
        math.prod(a.shape) * a.dtype.itemsize for a in shapes
    )
    there = pl.BlockSpec(memory_space=pl.ANY)
    here = pl.BlockSpec(memory_space=pltpu.VMEM)
    scalar = pl.BlockSpec(memory_space=pltpu.SMEM)

    def places(trees, kinds):
        return [kind for tree, kind in zip(trees, kinds) for _ in jax.tree.leaves(tree, is_leaf=is_shape)]

    found = pl.pallas_call(
        body,
        out_shape=shapes,
        in_specs=places(arguments, (here, there, scalar)),
        out_specs=places(results, (here, there, there)),
        scratch_shapes=flat_own,
        cost_estimate=pl.CostEstimate(flops=flops, bytes_accessed=moved, transcendentals=0),
        compiler_params=pltpu.CompilerParams(
            collective_id=ident, has_side_effects=ident is not None, vmem_limit_bytes=VMEM_BYTES
        ),
    )(*flat_in)
    found = jax.tree.unflatten(tree_out, found)
    return types.SimpleNamespace(**found[0], **found[1], **found[2])


def halve(array, axis):
    size = lax.axis_size(axis)
    index = lax.axis_index(axis)
    pieces = array.reshape((size, array.shape[0] // size) + array.shape[1:])
    distance = 1
    while distance < size:
        bit = (index // distance) % 2
        pairs = pieces.reshape((pieces.shape[0] // 2, 2) + pieces.shape[1:])
        keep = lax.dynamic_index_in_dim(pairs, bit, axis=1, keepdims=False)
        give = lax.dynamic_index_in_dim(pairs, 1 - bit, axis=1, keepdims=False)
        got = lax.ppermute(give, axis, [(i, i ^ distance) for i in range(size)])
        pieces = (keep.astype(FULL) + got.astype(FULL)).astype(array.dtype)
        distance *= 2
    return pieces[0]


def scatter_plain(left, right):
    return halve(inner(flat(left), right.T).astype(LOW), "seq").astype(FULL).T


def scatter_gains(gains):
    count = lax.axis_size("tensor")
    n_seq = lax.axis_size("seq")
    shaped = gains.reshape(4, n_seq, -1).transpose(1, 0, 2)
    mine = halve(shaped, "seq")[0]
    distance = 1
    while distance < count:
        mine = mine + lax.ppermute(mine, "tensor", [(i, i ^ distance) for i in range(count)])
        distance *= 2
    width = mine.shape[-1] // count
    return lax.dynamic_slice_in_dim(mine, lax.axis_index("tensor") * width, width, 1)


def on_device(
    inputs,
    cotangent,
    seq_lengths,
    norm_gains,
    query_one,
    key_one,
    value_one,
    out_one,
    gate_one,
    up_one,
    down_one,
    query_two,
    key_two,
    value_two,
    out_two,
    gate_two,
    up_two,
    down_two,
):
    rows, width = inputs.shape
    size = lax.axis_size("seq")
    stretch = 4 * rows
    units = gate_one.shape[1]
    cols = value_one.shape[1]
    small = query_one.shape[1]
    scatter = width // size == BLOCK
    count = int(math.log2(size))
    wide = ((4, 2, HALF, width), LOW)
    own = ((CHUNKS, HALF, width), FULL)
    heads = ((stretch, cols), LOW)
    heads_full = ((stretch, cols), FULL)
    narrow = ((stretch, small), LOW)
    unit_rows = ((CHUNKS, 2, HALF, units), LOW)
    turned_units = ((units, stretch), LOW)
    turned_cols = ((cols, stretch), LOW)
    state = ((FEATS + NORM_ROWS, cols), FULL)
    padded = ((stretch + WINDOW, cols), LOW)
    one_flops = 2 * stretch * width
    blocks = functools.partial(Scatter.blocks, size)
    choice, feature_rows = feature_tables()
    tables = dict(feature_choice=choice, feature_rows=feature_rows)
    tensor_sums = dict(
        keep=pltpu.VMEM(*own),
        share_sems=pltpu.SemaphoreType.DMA((4, 2, CHUNKS)),
    )
    got = ((size // 2, units, BLOCK), LOW)
    ahead = run_kernel(
        functools.partial(first_kernel, size=size),
        0,
        dict(
            gains=norm_gains,
            inputs=inputs,
            cotangent=cotangent,
            w_query_one=query_one.T,
            w_key_one=key_one.T,
            w_value_one=value_one,
            **tables,
        ),
        dict(result=((rows, width), LOW), gain_grad=((1, width), FULL)),
        dict(
            **tensor_sums,
            **Taylor.scratch(size, cols),
            totals=[Total.scratch(width) for _ in range(3)],
            rows_in=pltpu.VMEM((rows, width), LOW),
            cot_in=pltpu.VMEM((rows, width), LOW),
            near_sems=pltpu.SemaphoreType.DMA((2, 4)),
            far_sems=pltpu.SemaphoreType.DMA((2, 2)),
            mixed_low=pltpu.VMEM(*heads),
            query2=pltpu.VMEM(*heads),
            keys=pltpu.VMEM(*padded),
            values=pltpu.VMEM(*padded),
            window_low=pltpu.VMEM(*heads),
            d_window=pltpu.VMEM(*heads),
            d_keys=pltpu.VMEM(padded[0], FULL),
            d_values=pltpu.VMEM(padded[0], FULL),
            middle_two=pltpu.VMEM(*own),
            hidden=pltpu.VMEM(*unit_rows),
            halo_out=pltpu.VMEM((2, 2, WINDOW, cols), LOW),
            halo_in=pltpu.VMEM((2, 2, WINDOW, cols), LOW),
            halo_sems=pltpu.SemaphoreType.DMA((2, 2, 2)),
            give=[pltpu.VMEM(*got)],
            give_sems=pltpu.SemaphoreType.DMA((2, size // 2)),
        ),
        one_flops * (8 * cols + 9 * units),
        later=dict(
            w_out_one=out_one,
            w_gate_one=gate_one.T,
            w_up_one=up_one.T,
            w_down_one=down_one,
            w_key_two=key_two,
            w_value_two=value_two,
            w_query_two=query_two,
            w_out_two=out_two,
            w_gate_two=gate_two.T,
            w_up_two=up_two.T,
            w_down_two=down_two,
        ),
        saved=dict(
            start=own,
            middle=own,
            after=own,
            grad=own,
            normed_one=wide,
            normed_two=wide,
            normed_three=wide,
            normed_four=wide,
            cot=wide,
            grad_three=wide,
            query=narrow,
            key=narrow,
            value=heads,
            mixed=heads_full,
            inverse=heads_full,
            mixed_turned=turned_cols,
            carry=state,
            gate=unit_rows,
            up=unit_rows,
            hidden_one=turned_units,
            hidden_two=turned_units,
            d_gate_two=turned_units,
            d_up_two=turned_units,
            window_turned=turned_cols,
            d_query2=heads,
            d_key2=heads,
            d_value2=heads,
            d_turned2=((3 * cols, stretch), LOW),
        ),
        apart=dict(gate_two_got=got) if scatter else None,
        scalars=dict(lengths=seq_lengths),
        extra=dict(scatter=scatter),
    )
    widths = [units, units, units, cols, 3 * cols, units, units, units, 2 * small + cols, cols]
    carried = dict(
        d_query2=ahead.d_query2,
        d_key2=ahead.d_key2,
        d_value2=ahead.d_value2,
        w_query_two=query_two,
        w_key_two=key_two,
        w_value_two=value_two,
    )
    summed = dict(
        normed_four=ahead.normed_four,
        d_up_two=ahead.d_up_two,
        d_gate_two=ahead.d_gate_two,
        cot=ahead.cot,
        hidden_two=ahead.hidden_two,
        grad_three=ahead.grad_three,
        window_turned=ahead.window_turned,
        normed_three=ahead.normed_three,
        d_turned2=ahead.d_turned2,
        normed_two=ahead.normed_two,
        hidden_one=ahead.hidden_one,
        normed_one=ahead.normed_one,
        mixed_turned=ahead.mixed_turned,
    )
    chain = dict(
        after=ahead.after,
        grad=ahead.grad,
        w_down_one=down_one,
        gate=ahead.gate,
        up=ahead.up,
        w_gate_one=gate_one.T,
        w_up_one=up_one.T,
        middle=ahead.middle,
        w_out_one=out_one,
        query=ahead.query,
        key=ahead.key,
        value=ahead.value,
        mixed=ahead.mixed,
        inverse=ahead.inverse,
        carry=ahead.carry,
        w_query_one=query_one.T,
        w_key_one=key_one.T,
        w_value_one=value_one,
        start=ahead.start,
    )
    early = ("normed_four", "d_up_two", "d_gate_two")
    made = dict(
        d_gate_one=turned_units,
        d_up_one=turned_units,
        d_turned=((2 * small + cols, stretch), LOW),
        grad_two=wide,
        grad_one=wide,
    )
    if scatter:
        gain_blocks = [pltpu.VMEM((size >> (at + 1), 8, BLOCK), FULL) for at in range(count)]
        buffers = dict(
            unit_gives=[blocks(units) for _ in range(3)],
            unit_gots=[blocks(units) for _ in range(6)],
            out_gives=[blocks(cols) for _ in range(2)],
            out_gots=[blocks(cols) for _ in range(2)],
            three_two_gives=blocks(3 * cols),
            three_two_gots=blocks(3 * cols),
            three_one_gives=blocks(2 * small + cols),
            three_one_gots=blocks(2 * small + cols),
            gain_gives=gain_blocks,
            gain_gots=gain_blocks,
            sems=[pltpu.SemaphoreType.DMA((11, 2, size >> (at + 1))) for at in range(count)],
            gain_sum=pltpu.VMEM((3, 8, BLOCK), FULL),
            gain_in_sum=pltpu.VMEM((2, 8, BLOCK), FULL),
            gain_sems=pltpu.SemaphoreType.DMA((2, 2)),
            **{name: pltpu.VMEM(*leaf) for name, leaf in made.items()},
        )
        buffers["unit_gots"][0][0] = None
        inputs_later = dict(
            **carried,
            **{name: summed[name] for name in early},
            gate_two_got=ahead.gate_two_got,
            **chain,
            **{name: array for name, array in summed.items() if name not in early},
        )
        kept = dict(sums=[((wide_, BLOCK), FULL) for wide_ in widths])
    else:
        buffers = {}
        inputs_later = dict(**carried, **chain)
        kept = made
    behind = run_kernel(
        functools.partial(second_kernel, size=size),
        1,
        dict(gains=norm_gains, gain_in=ahead.gain_grad, **tables),
        dict(input_grad=((rows, width), FULL), gain_out=((8, BLOCK // 4 if scatter else width), FULL)),
        dict(
            **tensor_sums,
            **Taylor.scratch(size, cols),
            totals=[Total.scratch(width) for _ in range(2)],
            d_mixed=pltpu.VMEM(*heads),
            gain_rows=pltpu.VMEM((8, width), FULL),
            grad_carry=pltpu.VMEM(*state),
            d_query_acc=pltpu.VMEM((stretch, small), FULL),
            d_key_acc=pltpu.VMEM((stretch, small), FULL),
            d_value_acc=pltpu.VMEM((stretch, cols), FULL),
            d_query_low=pltpu.VMEM(*narrow),
            d_key_low=pltpu.VMEM(*narrow),
            d_value_low=pltpu.VMEM(*heads),
            **buffers,
        ),
        one_flops * (6 * cols + 9 * units),
        later=inputs_later,
        saved=kept,
        scalars=dict(lengths=seq_lengths),
        extra=dict(scatter=scatter),
    )
    if not scatter:
        sums = [
            scatter_plain(left, right)
            for left, right in (
                (ahead.normed_four, ahead.d_gate_two),
                (ahead.normed_four, ahead.d_up_two),
                (ahead.cot, ahead.hidden_two),
                (ahead.grad_three, ahead.window_turned),
                (ahead.normed_three, ahead.d_turned2),
                (ahead.normed_two, behind.d_gate_one),
                (ahead.normed_two, behind.d_up_one),
                (behind.grad_two, ahead.hidden_one),
                (ahead.normed_one, behind.d_turned),
                (behind.grad_one, ahead.mixed_turned),
            )
        ]
        gains = scatter_gains(behind.gain_out[:4])
        three_one, three_two = sums[8], sums[4]
        return (
            (ahead.result, behind.input_grad, gains)
            + (three_one[:small].T, three_one[small : 2 * small].T, three_one[2 * small :].T)
            + (sums[9], sums[5].T, sums[6].T, sums[7])
            + tuple(three_two[first : first + cols].T for first in range(0, 3 * cols, cols))
            + (sums[3], sums[0].T, sums[1].T, sums[2])
        )
    block = ((BLOCK, cols), FULL)
    unit = ((units, BLOCK), FULL)
    done = run_kernel(
        functools.partial(finish_kernel, small=small, cols=cols),
        None,
        dict(
            result_in=ahead.result,
            input_grad_in=behind.input_grad,
            gains_in=behind.gain_out,
            sums=[behind.sums[name] for name in (0, 1, 2, 3, 5, 6, 7, 9)],
            threes=[behind.sums[8], behind.sums[4]],
        ),
        dict(
            result=((rows, width), LOW),
            input_grad=((rows, width), FULL),
            gains=((4, BLOCK // 4), FULL),
            same=[unit, unit, unit, ((cols, BLOCK), FULL), unit, unit, unit, ((cols, BLOCK), FULL)],
            turned=[[((small, BLOCK), FULL), ((small, BLOCK), FULL), block], [block, block, block]],
        ),
        {},
        stretch,
    )
    same, turned = done.same, done.turned
    return (
        (done.result, done.input_grad, done.gains)
        + (turned[0][0].T, turned[0][1].T, turned[0][2])
        + (same[7], same[4].T, same[5].T, same[6])
        + tuple(turned[1])
        + (same[3], same[0].T, same[1].T, same[2])
    )


def solution(mesh):
    both = P(("seq", "tensor"), None)
    split = P(None, "tensor")
    stacked = P("tensor", None)
    columns_out = P("seq", "tensor")
    rows_out = P("tensor", "seq")
    layer_in = (split, split, split, stacked, split, split, stacked)
    layer_out = (columns_out, columns_out, columns_out, rows_out, columns_out, columns_out, rows_out)
    return jax.shard_map(
        on_device,
        mesh=mesh,
        in_specs=(both, both, P(), P()) + layer_in + layer_in,
        out_specs=(both, both, P(None, ("seq", "tensor"))) + layer_out + layer_out,
        check_vma=False,
    )
```

```python
import functools
import math
import types

import jax
import jax.numpy as jnp
import numpy as np
from jax import lax
from jax.experimental import pallas as pl
from jax.experimental.pallas import tpu as pltpu
from jax.sharding import PartitionSpec as P

FEAT = 16
HEAD = 64
WINDOW = 64
BLOCK = 128
EPS = 1e-05
FLOOR_SCORE = -1e30
MESH = pl.DeviceIdType.MESH
LOW = jnp.bfloat16
FULL = jnp.float32
VMEM_BYTES = 60 * 1024 * 1024
HALF = BLOCK // 2
CHUNKS = 4
PAIRS = [(a, b) for a in range(FEAT + 1) for b in range(a, FEAT + 1)]
FEATS = -(-len(PAIRS) // 16) * 16
NORM_ROWS = 16


def plain(left, right):
    return jnp.dot(left, right, preferred_element_type=FULL)


def inner(left, right):
    return lax.dot_general(left, right, (((0,), (0,)), ((), ())), preferred_element_type=FULL)


def through(left, right):
    return lax.dot_general(left, right, (((1,), (1,)), ((), ())), preferred_element_type=FULL)


def flat(array):
    return array.reshape((math.prod(array.shape[:-1]), array.shape[-1]))


class Group:
    def __init__(self):
        index = lax.axis_index("tensor")
        self.index = index
        self.low = lax.rem(index, 2)
        self.high = index // 2
        self.pair = dict(tensor=index + 1 - 2 * self.low)
        self.partner = dict(tensor=lax.rem(index + 2, 4))

    def mine(self, chunk):
        return jnp.where(self.high == chunk // 2, 1.0, 0.0)

    def split(self, part, count, by_rows=False):
        if by_rows:
            zero, one = part.reshape(2, count, HALF, -1)
        else:
            whole = part.reshape(count, 2, HALF, -1)
            zero, one = whole[:, 0], whole[:, 1]
        even = self.low == 0
        return jnp.where(even, zero, one), jnp.where(even, one, zero)

    def own_rows(self, ref, chunk, count):
        return ref.at[self.low + 2 * (chunk // 2), pl.ds(chunk % 2, count)]

    def own_chunks(self, ref, chunk, count):
        return ref.at[pl.ds(chunk, count), self.low]


def chunk_rows(ref, chunk, count=1):
    first, half = 2 * (chunk // 2), chunk % 2
    if len(ref.shape) == 4:
        return flat(ref[first : first + 2, half : half + count])
    starts = [block * BLOCK + half * HALF for block in (first, first + 1)]
    return jnp.concatenate([ref[start : start + count * HALF] for start in starts], axis=0)


def put_rows(ref, chunk, value, ahead=0):
    for side in range(2):
        start = ahead + (2 * (chunk // 2) + side) * BLOCK + chunk % 2 * HALF
        ref[start : start + HALF] = value[side * HALF : (side + 1) * HALF]


class Line:
    def __init__(self, size):
        self.size = size
        self.index = lax.axis_index("seq")
        self.after = dict(seq=lax.rem(self.index + 1, size))
        self.before = dict(seq=lax.rem(self.index + size - 1, size))

    def flip(self, relative):
        found = 0
        bit = 1
        while bit < self.size:
            found = found + bit * lax.rem(self.index // bit + relative // bit, 2)
            bit *= 2
        return found


def greet(peers, everyone=None):
    barrier = pltpu.get_barrier_semaphore()
    for peer in peers:
        pl.semaphore_signal(barrier, inc=1, device_id=peer, device_id_type=MESH)
    count = len(peers)
    if everyone is not None:

        def call(step, carry):
            peer = dict(seq=lax.rem(everyone.index + step, everyone.size))
            pl.semaphore_signal(barrier, inc=1, device_id=peer, device_id_type=MESH)
            return carry

        lax.fori_loop(1, everyone.size, call, 0)
        count += everyone.size - 1
    pl.semaphore_wait(barrier, count)


def remote(src, dst, send, recv, device):
    return pltpu.make_async_remote_copy(
        src_ref=src, dst_ref=dst, send_sem=send, recv_sem=recv, device_id=device, device_id_type=MESH
    )


def send(src, dst, send_sem, recv_sem, device):
    copy = remote(src, dst, send_sem, recv_sem, device)
    copy.start()
    return copy


class Total:
    def __init__(self, group, keep, buffers):
        self.group = group
        self.keep = keep
        self.pair_out, self.pair_in, self.out, self.into, self.sems = buffers
        self.pairs = {}
        self.fars = {}
        self.arriving = {}
        self.arrived = set()

    @staticmethod
    def scratch(width):
        return [pltpu.VMEM((CHUNKS, HALF, width), LOW)] * 4 + [pltpu.SemaphoreType.DMA((4, CHUNKS))]

    def give(self, chunk, part, count=1, by_rows=False):
        own, other = self.group.split(part, count, by_rows)
        place = pl.ds(chunk, count)
        self.keep[place] = own
        self.pair_out[place] = other.astype(LOW)
        self.pairs[chunk] = send(
            self.pair_out.at[place],
            self.pair_in.at[place],
            self.sems.at[0, chunk],
            self.sems.at[1, chunk],
            self.group.pair,
        )
        self.arriving.update({chunk + step: chunk for step in range(count)})

    def pair_sum(self, chunk, count=1):
        given = self.arriving[chunk]
        if given not in self.arrived:
            self.arrived.add(given)
            self.pairs[given].wait_recv()
        place = pl.ds(chunk, count)
        return self.keep[place] + self.pair_in[place].astype(FULL)

    def swap(self, chunk, count=1):
        place = pl.ds(chunk, count)
        self.out[place] = self.pair_sum(chunk, count).astype(LOW)
        self.fars[chunk] = send(
            self.out.at[place],
            self.into.at[place],
            self.sems.at[2, chunk],
            self.sems.at[3, chunk],
            self.group.partner,
        )

    def swap_half(self):
        for chunk in range(0, CHUNKS, 2):
            self.out[chunk : chunk + 2] = self.pair_sum(chunk, 2).astype(LOW)
        self.fars[0] = send(
            self.out.at[pl.ds(2 - 2 * self.group.high, 2)],
            self.into.at[pl.ds(0, 2)],
            self.sems.at[2, 0],
            self.sems.at[3, 0],
            self.group.partner,
        )

    def take(self, chunk, count=1):
        self.fars[chunk].wait_recv()
        place = pl.ds(chunk, count)
        return self.out[place].astype(FULL) + self.into[place].astype(FULL)

    def take_half(self):
        self.fars[0].wait_recv()
        return self.out[pl.ds(2 * self.group.high, 2)].astype(FULL) + self.into[0:2].astype(FULL)

    def close(self):
        for copy in list(self.pairs.values()) + list(self.fars.values()):
            copy.wait_send()


class Share:
    def __init__(self, group, full, sems, place):
        self.group = group
        self.full = full
        self.sems = sems
        self.place = place
        self.copies = {}

    def give(self, chunk, value, count=1):
        rows = self.place(self.full, chunk, count)
        rows[...] = value
        self.copies[chunk] = send(
            rows, rows, self.sems.at[0, chunk], self.sems.at[1, chunk], self.group.pair
        )

    def await_other(self, chunk):
        self.copies[chunk].wait_recv()

    def close(self):
        for copy in self.copies.values():
            copy.wait_send()


def share_sems():
    return pltpu.SemaphoreType.DMA((2, CHUNKS))


def relay(first, second, share, enter, work, count=1, order=None, between=lambda: None):
    starts = order or list(range(0, CHUNKS, count))
    for step in range(len(starts) + 1):
        if step < len(starts):
            share.give(starts[step], enter(starts[step], first.take(starts[step], count)), count)
        if step > 1:
            second.swap(starts[step - 2], count)
        if step > 0:
            chunk = starts[step - 1]
            share.await_other(chunk)
            second.give(chunk, work(chunk), count)
        between()
    second.swap(starts[-1], count)


class Later:
    def __init__(self, source, target, sem):
        self.copy = pltpu.make_async_copy(source, target, sem)
        self.copy.start()
        self.target = target
        self.waiting = True

    def __call__(self):
        if self.waiting:
            self.copy.wait()
            self.waiting = False
        return self.target


class Saved:
    def __init__(self, ref, target, sem):
        self.ref = ref
        self.target = target
        self.sem = sem
        self.copy = None

    def store(self):
        self.copy = pltpu.make_async_copy(self.ref, self.target, self.sem)
        self.copy.start()


class Scatter:
    def __init__(self, line, source, order, give, got, sems, begun=0):
        self.line = line
        self.ready, self.base = source
        self.order = order
        self.give = give
        self.got = got
        self.sems = sems
        self.begun = begun

    @staticmethod
    def blocks(size, width):
        return [pltpu.VMEM((size >> (at + 1), width, BLOCK), LOW) for at in range(int(math.log2(size)))]

    def copy(self, at, index):
        return remote(
            self.give[at].at[index],
            self.got[at].at[index],
            self.sems[at].at[0, index],
            self.sems[at].at[1, index],
            dict(seq=self.line.flip(self.order[at])),
        )

    def part(self, place, upto):
        relative = sum(bit for at, bit in enumerate(self.order) if place >> at & 1)
        total = self.base(self.line.flip(relative))
        for at in range(upto):
            index = place >> (at + 1)
            if at >= self.begun:
                self.copy(at, index).wait_recv()
            total = total + self.got[at][index].astype(FULL)
        return total

    def places(self, at):
        return sorted(range(self.line.size >> (at + 1)), key=lambda index: (index & -index) or self.line.size)

    def start(self, at):
        self.ready()
        for index in self.places(at):
            self.give[at][index] = self.part(2**at * (2 * index + 1), at).astype(self.give[at].dtype)
            self.copy(at, index).start()

    def finish(self):
        return self.part(0, len(self.order))

    def arrive(self, at):
        for index in self.places(at):
            self.copy(at, index).wait_recv()

    def sent(self):
        for at in range(self.begun, len(self.sems)):
            for index in self.places(at):
                self.copy(at, index).wait_send()


def columns_of(block):
    return pl.ds(pl.multiple_of(block * BLOCK, BLOCK), BLOCK)


def product(left, right):
    def base(block):
        return plain(held(right)[...], flat(held(left)[:, :, :, columns_of(block)]))

    def ready():
        held(left)
        held(right)

    return ready, base


def held(item):
    return item() if isinstance(item, Later) else item


def norm_apply(values, gain):
    inverse = lax.rsqrt(jnp.mean(values * values, axis=-1, keepdims=True) + EPS)
    return (values * inverse * gain).astype(LOW)


def norm_back(grad, values, gain):
    inverse = lax.rsqrt(jnp.mean(values * values, axis=-1, keepdims=True) + EPS)
    scaled = values * inverse
    d_scaled = grad * gain
    d_values = inverse * (d_scaled - scaled * jnp.mean(d_scaled * scaled, axis=-1, keepdims=True))
    return d_values, jnp.sum(grad * scaled, axis=0, keepdims=True)


def gate_forward(gate, up_val):
    return gate * up_val / (1.0 + jnp.exp(-gate))


def gate_backward(d_hidden, gate, up_val):
    sigma = 1.0 / (1.0 + jnp.exp(-gate))
    return d_hidden * up_val * sigma * (1.0 + gate * (1.0 - sigma)), d_hidden * gate * sigma


def segment_of(lengths, positions):
    end = 0
    found = jnp.zeros_like(positions)
    for index in range(lengths.shape[0]):
        end = end + lengths[index]
        found = found + jnp.where(positions >= end, 1, 0)
    return found


def ramp(shape, axis, first):
    return lax.broadcasted_iota(jnp.int32, shape, axis) + first


def same(left, right):
    return jnp.where(left == right, 1.0, 0.0)


def feature_tables():
    choice = np.zeros((2, FEAT, FEATS), np.float32)
    rows = np.zeros((8, FEATS), np.float32)
    for index, pair in enumerate(PAIRS):
        for side, entry in enumerate(pair):
            if entry < FEAT:
                choice[side, entry, index] = 1.0
            else:
                rows[side, index] = 1.0
        rows[2, index] = 0.5**0.5 if pair[0] == pair[1] and pair[0] < FEAT else 1.0
    return jnp.asarray(choice, LOW), jnp.asarray(rows, FULL)


class Taylor:
    def __init__(self, line, k, query, key, value):
        self.line = line
        self.k = k
        self.query = query
        self.key = key
        self.value = value
        self.rows = query.shape[0]
        self.count = self.rows // BLOCK
        self.heads = value.shape[1] // HEAD
        start = line.index * self.rows
        self.start = start
        column = segment_of(k.lengths, ramp((self.rows, 1), 0, start))
        last = segment_of(k.lengths, ramp((1, 1), 0, start + self.rows - 1))
        before = segment_of(k.lengths, ramp((1, 1), 0, start - 1))
        self.last = last
        self.before = before
        self.segments = column
        self.across = segment_of(k.lengths, ramp((1, self.rows), 1, start))
        self.tail = same(column, last)
        self.carried = same(column, before)
        self.lane = ramp((1, self.heads * HEAD), 1, 0) // HEAD

    def half(self, array, head, upto=None, only=None):
        first, last = (0, upto or self.count) if only is None else (only, only + 1)
        return array[first * BLOCK : last * BLOCK, head * FEAT : (head + 1) * FEAT] * jnp.asarray(0.5, LOW)

    def factors(self, half):
        rows = self.k.feature_rows
        left = plain(half, self.k.feature_choice[0]) + rows[0:1]
        right = plain(half, self.k.feature_choice[1]) + rows[1:2]
        return left, right

    def features(self, array, head):
        left, right = self.factors(self.half(array, head))
        return left * right * self.k.feature_rows[2:3]

    def features_back(self, grad, array, head):
        left, right = self.factors(self.half(array, head))
        weighted = grad * self.k.feature_rows[2:3]
        return through((weighted * right).astype(LOW), self.k.feature_choice[0]) + through(
            (weighted * left).astype(LOW), self.k.feature_choice[1]
        )

    def of_head(self, head, array):
        return jnp.where(self.lane == head, array, jnp.zeros_like(array))

    def mask(self, block):
        upto = (block + 1) * BLOCK
        rows = ramp((BLOCK, 1), 0, block * BLOCK)
        allowed = (ramp((1, upto), 1, 0) <= rows) & (
            self.across[:, :upto] == self.segments[block * BLOCK : upto]
        )
        return jnp.where(allowed, 1.0, 0.0)

    def send_state(self, forward):
        k, line = self.k, self.line

        def step(other, carry):
            @pl.when((other > line.index) if forward else (other < line.index))
            def _():
                self.state_copy(other).start()

            return carry

        lax.fori_loop(0, line.size, step, 0)

    def state_copy(self, other):
        k = self.k
        return remote(
            k.state_own,
            k.state_slots.at[self.line.index],
            k.state_sems.at[0, other],
            k.state_sems.at[1, self.line.index],
            dict(seq=other),
        )

    def state_arrival(self, other):
        k = self.k
        return remote(
            k.state_own,
            k.state_slots.at[other],
            k.state_sems.at[0, other],
            k.state_sems.at[1, other],
            dict(seq=other),
        )

    def take_state(self, total, forward):
        k, line = self.k, self.line
        total[...] = jnp.zeros_like(total)

        def step(other, carry):
            @pl.when((other < line.index) if forward else (other > line.index))
            def _():
                self.state_arrival(other).wait_recv()
                if forward:
                    edge = segment_of(k.lengths, ramp((1, 1), 0, (other + 1) * self.rows - 1))
                    weight = same(edge, self.before)
                else:
                    edge = segment_of(k.lengths, ramp((1, 1), 0, other * self.rows - 1))
                    weight = same(edge, self.last)
                total[...] += weight * k.state_slots[other].astype(FULL)

            return carry

        lax.fori_loop(0, line.size, step, 0)

    def close(self, forward):
        line = self.line

        def step(other, carry):
            @pl.when((other > line.index) if forward else (other < line.index))
            def _():
                self.state_copy(other).wait_send()

            return carry

        lax.fori_loop(0, line.size, step, 0)

    @staticmethod
    def scratch(size, cols):
        shape = (FEATS + NORM_ROWS, cols)
        return dict(
            state_own=pltpu.VMEM(shape, LOW),
            state_build=pltpu.VMEM(shape, FULL),
            state_slots=pltpu.VMEM((size,) + shape, LOW),
            state_sems=pltpu.SemaphoreType.DMA((2, size)),
        )

    def forward(self, meanwhile):
        k = self.k
        value = self.value[...]
        build = k.state_build
        build[...] = jnp.zeros_like(build)
        state = jnp.zeros((FEATS, value.shape[1]), FULL)
        for head in range(self.heads):
            feats = self.features(self.key, head) * self.tail
            state = state + self.of_head(head, inner(feats.astype(LOW), value))
            build[FEATS + head : FEATS + head + 1, :FEATS] = jnp.sum(feats, axis=0, keepdims=True)
        build[:FEATS] = state
        k.state_own[...] = build[...].astype(LOW)
        self.send_state(True)
        for block in range(self.count):
            allowed = self.mask(block)
            rows = slice(block * BLOCK, (block + 1) * BLOCK)
            for head in range(self.heads):
                places = slice(head * HEAD, (head + 1) * HEAD)
                score = through(self.half(self.query, head, only=block), self.half(self.key, head, block + 1))
                score = allowed * (1.0 + score + 0.5 * score * score)
                k.mixed[rows, places] = plain(score.astype(LOW), value[: (block + 1) * BLOCK, places])
                k.inverse[rows, places] = jnp.broadcast_to(jnp.sum(score, axis=1, keepdims=True), (BLOCK, HEAD))
        meanwhile()
        self.take_state(k.carry, True)
        state = k.carry[:FEATS].astype(LOW)
        numerator = jnp.zeros((self.rows, value.shape[1]), FULL)
        totals = jnp.zeros((self.rows, value.shape[1]), FULL)
        for head in range(self.heads):
            feats = self.features(self.query, head)
            numerator = numerator + self.of_head(head, plain(feats.astype(LOW), state))
            norm = k.carry[FEATS + head : FEATS + head + 1, :FEATS]
            totals = totals + self.of_head(head, jnp.sum(feats * norm, axis=1, keepdims=True) + jnp.zeros_like(totals))
        inverse = 1.0 / (k.inverse[...] + self.carried * totals)
        mixed = (k.mixed[...] + self.carried * numerator) * inverse
        k.inverse[...] = inverse
        k.mixed[...] = mixed
        k.mixed_low[...] = mixed.astype(LOW)
        k.mixed_turned[...] = mixed.T.astype(LOW)

    def backward(self, d_mixed):
        k = self.k
        value = self.value[...]
        d_out = d_mixed[...].astype(FULL)
        d_numer = d_out * k.inverse[...]
        d_low = d_numer.astype(LOW)
        product = d_numer * k.mixed[...]
        d_totals = [
            -jnp.sum(product[:, head * HEAD : (head + 1) * HEAD], axis=1, keepdims=True) for head in range(self.heads)
        ]
        build = k.state_build
        build[...] = jnp.zeros_like(build)
        state = jnp.zeros((FEATS, value.shape[1]), FULL)
        for head in range(self.heads):
            feats = self.features(self.query, head) * self.carried
            state = state + self.of_head(head, inner(feats.astype(LOW), d_low))
            build[FEATS + head : FEATS + head + 1, :FEATS] = jnp.sum(feats * d_totals[head], axis=0, keepdims=True)
        build[:FEATS] = state
        k.state_own[...] = build[...].astype(LOW)
        self.send_state(False)
        yield
        carry = k.carry[:FEATS].astype(LOW)
        k.d_key_acc[...] = jnp.zeros_like(k.d_key_acc)
        k.d_value_acc[...] = jnp.zeros_like(k.d_value_acc)
        for head in range(self.heads):
            norm = k.carry[FEATS + head : FEATS + head + 1, :FEATS]
            d_feats = self.carried * (through(self.of_head(head, d_low), carry) + d_totals[head] * norm)
            k.d_query_acc[:, head * FEAT : (head + 1) * FEAT] = self.features_back(d_feats, self.query, head)
        for block in range(self.count):
            allowed = self.mask(block)
            upto = (block + 1) * BLOCK
            rows = slice(block * BLOCK, upto)
            for head in range(self.heads):
                places = slice(head * HEAD, (head + 1) * HEAD)
                narrow = slice(head * FEAT, (head + 1) * FEAT)
                query = self.half(self.query, head, only=block)
                key = self.half(self.key, head, block + 1)
                score = through(query, key)
                d_rows = d_low[rows, places]
                d_score = through(d_rows, value[:upto, places]) + d_totals[head][rows]
                d_score = (allowed * d_score * (1.0 + score)).astype(LOW)
                score = (allowed * (1.0 + score + 0.5 * score * score)).astype(LOW)
                k.d_query_acc[rows, narrow] += plain(d_score, key)
                k.d_key_acc[:upto, narrow] += inner(d_score, query)
                k.d_value_acc[:upto, places] += inner(score, d_rows)
            yield
        self.take_state(k.grad_carry, False)
        carry = k.grad_carry[:FEATS].astype(LOW)
        for head in range(self.heads):
            norm = k.grad_carry[FEATS + head : FEATS + head + 1, :FEATS]
            d_feats = self.tail * (through(self.of_head(head, value), carry) + norm)
            k.d_key_acc[:, head * FEAT : (head + 1) * FEAT] += self.features_back(d_feats, self.key, head)
            feats = self.features(self.key, head).astype(LOW)
            k.d_value_acc[...] += self.of_head(head, self.tail * plain(feats, carry))


def window_mask(k, line, block, rows):
    span = BLOCK + WINDOW
    first = line.index * rows + block * BLOCK
    query = ramp((BLOCK, 1), 0, first)
    key = ramp((1, span), 1, first - WINDOW)
    return (
        (key <= query)
        & (key > query - WINDOW)
        & (key >= 0)
        & (segment_of(k.lengths, key) == segment_of(k.lengths, query))
    )


def window_weights(query, key, allowed):
    score = jnp.where(allowed, through(query, key) * HEAD**-0.5, FLOOR_SCORE)
    weight = jnp.exp(score - jnp.max(score, axis=1, keepdims=True))
    return weight / jnp.sum(weight, axis=1, keepdims=True)


def window_forward(k, line, block):
    own = slice(block * BLOCK, (block + 1) * BLOCK)
    allowed = window_mask(k, line, block, k.query2.shape[0])
    span = slice(block * BLOCK, (block + 1) * BLOCK + WINDOW)
    outs = []
    for head in range(k.keys.shape[1] // HEAD):
        places = slice(head * HEAD, (head + 1) * HEAD)
        weight = window_weights(k.query2[own, places], k.keys[span, places], allowed)
        outs.append(plain(weight.astype(LOW), k.values[span, places]))
    whole = jnp.concatenate(outs, axis=1)
    k.window_low[own] = whole.astype(LOW)
    k.window_turned[:, own] = whole.T.astype(LOW)


def window_backward(k, line, block):
    own = slice(block * BLOCK, (block + 1) * BLOCK)
    allowed = window_mask(k, line, block, k.query2.shape[0])
    span = slice(block * BLOCK, (block + 1) * BLOCK + WINDOW)
    grads = []
    for head in range(k.keys.shape[1] // HEAD):
        places = slice(head * HEAD, (head + 1) * HEAD)
        query = k.query2[own, places]
        key = k.keys[span, places]
        d_out = k.d_window[own, places]
        weight = window_weights(query, key, allowed)
        d_weight = through(d_out, k.values[span, places])
        d_score = weight * (d_weight - jnp.sum(weight * d_weight, axis=1, keepdims=True)) * HEAD**-0.5
        d_score = d_score.astype(LOW)
        grads.append(plain(d_score, key))
        k.d_keys[span, places] += inner(d_score, query)
        k.d_values[span, places] += inner(weight.astype(LOW), d_out)
    whole = jnp.concatenate(grads, axis=1)
    k.d_query2[own] = whole.astype(LOW)
    k.d_turned2[: whole.shape[1], own] = whole.T.astype(LOW)


X_FIRST, Z_FIRST = (1, 2, 4), (2, 4, 1)
ORDERS = [X_FIRST, X_FIRST, Z_FIRST, Z_FIRST, X_FIRST, X_FIRST, X_FIRST, X_FIRST, X_FIRST, X_FIRST, X_FIRST]
PLAN = [[(2, 1), (4, 0), (0, 1), (1, 0), (4, 1)], [(0, 2), (3, 0)], [], [(4, 2)], [(5, 0), (1, 1)], [], [(2, 2)], [], [(3, 1), (5, 1)], [(1, 2)], [(7, 0), (5, 2), (7, 1), (6, 0)], [], [(7, 2), (1, 3), (6, 1)], [(10, 0)], [(8, 0), (7, 3), (9, 0), (6, 2), (4, 3), (5, 3), (3, 2), (10, 1), (8, 1), (10, 2), (9, 1), (8, 2), (11, 0), (11, 1), (2, 3), (3, 3), (11, 2), (9, 2), (0, 3), (6, 3), (8, 3), (9, 3)]]


def first_kernel(k, size):
    group, line = Group(), Line(size)
    greet([group.pair, group.partner], line)
    width = k.inputs.shape[1]
    rows = k.query.shape[0]
    cols = k.value.shape[1]
    total_a, total_b, total_c = (Total(group, k.keep, k.totals[i]) for i in range(3))
    closing = [total_a, total_b]

    def offer(step, block, raw):
        values = raw.astype(FULL)
        k.start[pl.ds(2 * (block // 2), 2)] = values.reshape(2, HALF, width)
        k.normed_one[block] = norm_apply(values, k.gains[0:1]).reshape(2, HALF, width)
        place = k.normed_one.at[block]
        copy = send(place, place, k.near_sems.at[0, step], k.near_sems.at[1, step], group.pair)
        copy.wait_recv()
        return copy

    def project_one(pair):
        normed = flat(k.normed_one[pl.ds(2 * pair, 2)])
        place = pl.ds(pl.multiple_of(pair * 2 * BLOCK, 2 * BLOCK), 2 * BLOCK)
        k.key[place] = through(normed, k.w_key_one[...]).astype(LOW)
        k.value[place] = plain(normed, k.w_value_one[...]).astype(LOW)
        k.query[place] = through(normed, k.w_query_one[...]).astype(LOW)

    def offer_cot(step, half, raw):
        place = k.cot.at[pl.ds(2 * half, 2), group.low]
        place[...] = raw.reshape(2, HALF, width)
        return send(place, place, k.near_sems.at[0, 2 + step], k.near_sems.at[1, 2 + step], group.pair)

    far = send(k.inputs, k.rows_in, k.far_sems.at[0, 0], k.far_sems.at[1, 0], group.partner)
    copies = [offer(0, group.index, k.inputs[...])]
    project_one(group.high)
    far.wait_recv()
    far_cot = send(k.cotangent, k.cot_in, k.far_sems.at[0, 1], k.far_sems.at[1, 1], group.partner)
    copies.append(offer(1, lax.rem(group.index + 2, 4), k.rows_in[...]))
    project_one(1 - group.high)
    copies.append(offer_cot(0, group.high, k.cotangent[...]))
    taylor = Taylor(line, k, k.query, k.key, k.value)

    def turn_ahead():
        far_cot.wait_recv()
        copies.append(offer_cot(1, 1 - group.high, k.cot_in[...]))
        for copy in copies[2:]:
            copy.wait_recv()
        k.store(k.cot)
        for chunk in range(0, CHUNKS, 2):
            found = through(flat(k.cot[chunk : chunk + 2]), k.w_down_two()[...])
            k.d_hidden[chunk : chunk + 2] = found.reshape(2, 2 * HALF, -1)

    taylor.forward(turn_ahead)
    for item in (k.start, k.normed_one, k.query, k.key, k.value, k.mixed, k.inverse, k.mixed_turned, k.carry):
        k.store(item)

    share = Share(group, k.normed_two, k.share_sems.at[0], group.own_chunks)
    closing.append(share)

    def enter_mlp(chunk, total):
        middle = k.start[chunk : chunk + 1] + total
        k.middle[chunk : chunk + 1] = middle
        return norm_apply(middle, k.gains[1:2])

    def mlp_one(chunk):
        normed = flat(k.normed_two[chunk])
        gate = through(normed, k.w_gate_one()[...])
        up_val = through(normed, k.w_up_one()[...])
        k.gate[chunk] = gate.astype(LOW).reshape(k.gate.shape[1:])
        k.up[chunk] = up_val.astype(LOW).reshape(k.up.shape[1:])
        hidden = gate_forward(gate, up_val)
        k.hidden_one[:, chunk * BLOCK : (chunk + 1) * BLOCK] = hidden.T.astype(LOW)
        return plain(hidden.astype(LOW), k.w_down_one()[...])

    order = [2, 3, 0, 1]
    for chunk in (2, 0):
        part = plain(chunk_rows(k.mixed_low, chunk, 2), k.w_out_one()[...])
        total_a.give(chunk, part, 2, by_rows=True)
    for chunk in order:
        total_a.swap(chunk)
    relay(total_a, total_b, share, enter_mlp, mlp_one, order=order)
    for item in (k.middle, k.normed_two, k.gate, k.up, k.hidden_one):
        k.store(item)

    share = Share(group, k.normed_three, k.share_sems.at[1], group.own_rows)
    closing.append(share)

    def project_two(chunk):
        normed = chunk_rows(k.normed_three, chunk)
        put_rows(k.keys, chunk, plain(normed, k.w_key_two()[...]).astype(LOW), WINDOW)
        put_rows(k.values, chunk, plain(normed, k.w_value_two()[...]).astype(LOW), WINDOW)
        put_rows(k.query2, chunk, plain(normed, k.w_query_two()[...]).astype(LOW))

    for step in range(CHUNKS + 1):
        if step < CHUNKS:
            chunk = order[step]
            after = k.middle[chunk : chunk + 1] + total_b.take(chunk)
            k.after[chunk : chunk + 1] = after
            share.give(chunk, norm_apply(after, k.gains[2:3]))
        if step > 0:
            chunk = order[step - 1]
            share.await_other(chunk)
            project_two(chunk)
        if step == 2:
            halo = Halo(k, 0, (k.keys, k.values), slice(rows, rows + WINDOW), line.after)
    for item in closing:
        item.close()
    closing = [halo]
    total_a, total_b = (Total(group, k.keep, k.totals[i]) for i in range(2))
    closing += [total_a, total_b, total_c]
    for index, target in enumerate((k.keys, k.values)):
        target[:WINDOW] = halo.take(index)
    for chunk in (0, 2):
        window_forward(k, line, chunk)
        window_forward(k, line, chunk + 1)
        part = plain(chunk_rows(k.window_low, chunk, 2), k.w_out_two()[...])
        total_a.give(chunk, part, 2, by_rows=True)
        total_a.swap(chunk)
        total_a.swap(chunk + 1)
    k.store(k.after)
    k.store(k.normed_three)
    k.store(k.window_turned)

    gain = k.gains[3:4]
    share = Share(group, k.normed_four, k.share_sems.at[2], group.own_chunks)
    closing.append(share)

    def enter_turn(chunk, total):
        middle = k.after[chunk : chunk + 1] + total
        k.middle_two[chunk : chunk + 1] = middle
        return norm_apply(middle, gain)

    def mlp_two(chunk):
        normed = flat(k.normed_four[chunk])
        gate = through(normed, k.w_gate_two()[...])
        up_val = through(normed, k.w_up_two()[...])
        d_gate, d_up = gate_backward(k.d_hidden[chunk], gate, up_val)
        d_gate, d_up = d_gate.astype(LOW), d_up.astype(LOW)
        back = plain(d_gate, k.w_gate_two()[...]) + plain(d_up, k.w_up_two()[...])
        k.gate_two[chunk] = gate
        k.up_two[chunk] = up_val
        k.d_gate_low[chunk] = d_gate
        k.d_up_low[chunk] = d_up
        return back

    relay(total_a, total_b, share, enter_turn, mlp_two)
    for chunk in range(CHUNKS):
        columns = slice(chunk * BLOCK, (chunk + 1) * BLOCK)
        k.d_gate_two[:, columns] = k.d_gate_low[chunk].T
        k.d_up_two[:, columns] = k.d_up_low[chunk].T
        hidden = gate_forward(k.gate_two[chunk], k.up_two[chunk])
        k.hidden[chunk] = hidden.astype(LOW)
        k.hidden_two[:, columns] = hidden.T.astype(LOW)
    for item in (k.normed_four, k.hidden_two, k.d_gate_two, k.d_up_two):
        k.store(item)
    begun = []
    if k.scatter:
        begun = [
            Scatter(line, product(left, right), order, [k.gives[i]], [k.begun[i]], [k.give_sems.at[i]])
            for i, (left, right, order) in enumerate(
                ((k.normed_four, k.d_gate_two, X_FIRST), (k.cot, k.hidden_two, Z_FIRST))
            )
        ]
    for item in begun:
        item.start(0)
    for chunk in range(0, CHUNKS, 2):
        total_c.give(chunk, plain(flat(k.hidden[chunk : chunk + 2]), k.w_down_two()[...]), 2)
    total_c.swap_half()

    share = Share(group, k.grad_three, k.share_sems.at[3], group.own_rows)
    closing.append(share)
    k.gain_grad[...] = jnp.zeros_like(k.gain_grad)
    k.d_keys[...] = jnp.zeros_like(k.d_keys)
    k.d_values[...] = jnp.zeros_like(k.d_values)
    for step in range(CHUNKS + 1):
        if step < CHUNKS:
            chunk = step
            d_values, d_gain = norm_back(total_b.take(chunk)[0], k.middle_two[chunk], gain)
            grad = k.cot[chunk, pl.ds(group.low, 1)].astype(FULL) + d_values[None]
            k.grad[chunk : chunk + 1] = grad
            k.gain_grad[...] += group.mine(chunk) * d_gain
            share.give(chunk, grad.astype(LOW))
        if step > 0:
            chunk = step - 1
            share.await_other(chunk)
            put_rows(k.d_window, chunk, through(chunk_rows(k.grad_three, chunk), k.w_out_two()[...]).astype(LOW))
        if step == 2:
            window_backward(k, line, 0)
            halo = Halo(k, 1, (k.d_keys, k.d_values), slice(0, WINDOW), line.before)
            closing.append(halo)
            window_backward(k, line, 1)
    k.store(k.grad)
    k.store(k.grad_three)
    window_backward(k, line, 2)
    window_backward(k, line, 3)
    k.store(k.d_query2)
    k.result[...] = (flat(k.middle_two[pl.ds(2 * group.high, 2)]) + flat(total_c.take_half())).astype(LOW)
    for index, (target, out) in enumerate(((k.d_keys, k.d_key2), (k.d_values, k.d_value2))):
        target[rows : rows + WINDOW] += halo.take(index).astype(FULL)
        whole = target[WINDOW:]
        out[...] = whole.astype(LOW)
        k.store(out)
        k.d_turned2[(index + 1) * cols : (index + 2) * cols] = whole.T.astype(LOW)
    k.store(k.d_turned2)
    for item in begun:
        item.arrive(0)
        item.sent()
    for item in closing:
        item.close()
    for copy in [far, far_cot] + copies:
        copy.wait_send()
    taylor.close(True)


class Halo:
    def __init__(self, k, turn, sources, rows, peer):
        self.into = k.halo_in.at[turn]
        self.copies = []
        for index, source in enumerate(sources):
            k.halo_out[turn, index] = source[rows].astype(LOW)
            self.copies.append(
                send(
                    k.halo_out.at[turn, index],
                    k.halo_in.at[turn, index],
                    k.halo_sems.at[0, turn, index],
                    k.halo_sems.at[1, turn, index],
                    peer,
                )
            )

    def take(self, index):
        self.copies[index].wait_recv()
        return self.into[index]

    def close(self):
        for copy in self.copies:
            copy.wait_send()


def second_kernel(k, size):
    group, line = Group(), Line(size)
    greet([group.pair, group.partner], line)
    width = k.gains.shape[1]
    total_a, total_b = (Total(group, k.keep, k.totals[i]) for i in range(2))
    share_mlp = Share(group, k.grad_two, k.share_sems.at[0], group.own_chunks)
    share = Share(group, k.grad_one, k.share_sems.at[1], group.own_rows)
    taylor = Taylor(line, k, k.query(), k.key(), k.value())
    background = list(PLAN)
    sums = {}

    def tick():
        if k.scatter:
            for name, level in background.pop(0):
                act(name, level)

    def normed_rows(chunk):
        return (
            through(chunk_rows(k.d_query2(), chunk, 2), k.w_query_two()[...])
            + through(chunk_rows(k.d_key2(), chunk, 2), k.w_key_two()[...])
            + through(chunk_rows(k.d_value2(), chunk, 2), k.w_value_two()[...])
        )

    def back(chunk, total, values, gain, row):
        d_values, d_gain = norm_back(flat(total), flat(values[chunk : chunk + 2]), gain)
        k.gain_rows[row : row + 1] += group.mine(chunk) * d_gain
        return d_values.reshape(2, HALF, width)

    def enter_mlp(chunk, total):
        grad = k.grad()[chunk : chunk + 2] + back(chunk, total, k.after(), k.gains[2:3], 2)
        k.grad()[chunk : chunk + 2] = grad
        return grad.astype(LOW)

    def mlp(chunk):
        d_hidden = through(flat(k.grad_two[chunk : chunk + 2]), k.w_down_one()[...])
        gate = flat(k.gate()[chunk : chunk + 2]).astype(FULL)
        up_val = flat(k.up()[chunk : chunk + 2]).astype(FULL)
        d_gate, d_up = gate_backward(d_hidden, gate, up_val)
        columns = slice(chunk * BLOCK, (chunk + 2) * BLOCK)
        k.d_gate_one[:, columns] = d_gate.T.astype(LOW)
        k.d_up_one[:, columns] = d_up.T.astype(LOW)
        return plain(d_gate.astype(LOW), k.w_gate_one()[...]) + plain(d_up.astype(LOW), k.w_up_one()[...])

    if k.scatter:
        pieces = [
            (k.normed_four, k.d_gate_two),
            (k.normed_four, k.d_up_two),
            (k.cot, k.hidden_two),
            (k.grad_three, k.window_turned),
            (k.normed_three, k.d_turned2),
            (k.normed_two, k.d_gate_one),
            (k.normed_two, k.d_up_one),
            (k.grad_two, k.hidden_one),
            (k.normed_one, k.d_turned),
            (k.grad_one, k.mixed_turned),
        ]
        sources = [product(left, right) for left, right in pieces]
        sources.append((lambda: None, lambda block: k.gain_rows[:, columns_of(block)]))
        begun = {0: 0, 2: 1}
        before = {5: 0, 6: 1, 7: 2}

        gain_copies = []

        def gain_step(step):
            if step:
                gain_copies[-1].wait_recv()
                k.gain_sum[step] = k.gain_sum[step - 1] + k.gain_in_sum[step - 1]
            else:
                k.gain_sum[0] = sums[10].finish()
            if step < 2:
                signals = k.gain_sems.at[0, step], k.gain_sems.at[1, step]
                peer = (group.pair, group.partner)[step]
                gain_copies.append(send(k.gain_sum.at[step], k.gain_in_sum.at[step], *signals, peer))
                return
            share_of = BLOCK // 4
            found = jnp.zeros((8, share_of), FULL)
            for index in range(4):
                part = k.gain_sum[2][:, index * share_of : (index + 1) * share_of]
                found = found + jnp.where(group.index == index, 1.0, 0.0) * part
            k.gain_out[...] = found

        def act(name, level):
            if name == 11:
                return gain_step(level)
            if name not in sums:
                got = list(k.gots[name])
                if name in begun:
                    got[0] = k.begun[begun[name]]()
                if name in before:
                    sums[before[name]].sent()
                sems = [sem.at[name] for sem in k.sems]
                give = k.gives[before.get(name, name)]
                order = ORDERS[name]
                sums[name] = Scatter(line, sources[name], order, give, got, sems, 1 if name in begun else 0)
            if level < len(ORDERS[name]):
                sums[name].start(level)
            else:
                k.sums[name][...] = sums[name].finish()
                k.store(k.sums[name])

    k.gain_rows[...] = jnp.zeros_like(k.gain_rows)
    k.gain_rows[3:4] = k.gain_in[...]
    for chunk in range(0, CHUNKS, 2):
        total_a.give(chunk, normed_rows(chunk), 2, by_rows=True)
    for chunk in range(0, CHUNKS, 2):
        total_a.swap(chunk, 2)
    tick()
    relay(total_a, total_b, share_mlp, enter_mlp, mlp, 2, between=tick)
    for step in range(3):
        if step < 2:
            chunk = 2 * step
            grad = k.grad()[chunk : chunk + 2] + back(chunk, total_b.take(chunk, 2), k.middle(), k.gains[1:2], 1)
            k.grad()[chunk : chunk + 2] = grad
            share.give(chunk, grad.astype(LOW), 2)
        if step > 0:
            chunk = 2 * step - 2
            share.await_other(chunk)
            rows = through(chunk_rows(k.grad_one, chunk, 2), k.w_out_one()[...])
            k.d_mixed[chunk * BLOCK : (chunk + 2) * BLOCK] = rows.astype(LOW)
        tick()

    total_a.close()
    total_c = Total(group, k.keep, k.totals[0])
    k.mixed, k.inverse, k.carry = k.mixed(), k.inverse(), k.carry()
    for _ in taylor.backward(k.d_mixed):
        tick()
    d_query = 0.5 * k.d_query_acc[...]
    d_key = 0.5 * k.d_key_acc[...]
    d_value = k.d_value_acc[...]
    small, cols = d_query.shape[1], d_value.shape[1]
    k.d_query_low[...] = d_query.astype(LOW)
    k.d_key_low[...] = d_key.astype(LOW)
    k.d_value_low[...] = d_value.astype(LOW)
    k.d_turned[:small] = d_query.T.astype(LOW)
    k.d_turned[small : 2 * small] = d_key.T.astype(LOW)
    k.d_turned[2 * small : 2 * small + cols] = d_value.T.astype(LOW)
    for chunk in range(0, CHUNKS, 2):
        part = (
            plain(chunk_rows(k.d_query_low, chunk, 2), k.w_query_one()[...])
            + plain(chunk_rows(k.d_key_low, chunk, 2), k.w_key_one()[...])
            + through(chunk_rows(k.d_value_low, chunk, 2), k.w_value_one()[...])
        )
        total_c.give(chunk, part, 2, by_rows=True)
    total_c.swap_half()
    tick()
    half = pl.ds(2 * group.high, 2)
    d_values, d_gain = norm_back(flat(total_c.take_half()), flat(k.start()[half]), k.gains[0:1])
    k.input_grad[...] = flat(k.grad()[half]) + d_values
    k.gain_rows[0:1] = d_gain

    tick()
    if k.scatter:
        while background:
            tick()
        for name in set(sums) - set(before.values()):
            sums[name].sent()
        for copy in gain_copies:
            copy.wait_send()
    else:
        for item in (k.d_gate_one, k.d_up_one, k.d_turned, k.grad_one, k.grad_two):
            k.store(item)
        k.gain_out[...] = k.gain_rows[...]
    for item in (total_b, total_c, share_mlp, share):
        item.close()
    taylor.close(False)


def finish_kernel(k, small, cols):
    k.result[...] = k.result_in[...]
    k.input_grad[...] = k.input_grad_in[...]
    k.gains[...] = k.gains_in[0:4]
    for source, target in zip(k.sums, k.same):
        target[...] = source[...]
    for source, targets in zip(k.threes, k.turned):
        first = 0
        for target in targets:
            if target.shape[1] == BLOCK:
                target[...] = source[first : first + target.shape[0]]
                first += target.shape[0]
            else:
                target[...] = source[first : first + target.shape[1]].T
                first += target.shape[1]


def run_kernel(kernel, ident, ins, outs, scratch, flops, later=None, saved=None, apart=None, scalars=None, extra=None):
    later, saved, apart, scalars = (found or {} for found in (later, saved, apart, scalars))
    is_shape = lambda leaf: isinstance(leaf, tuple) and isinstance(leaf[0], tuple)

    def buffer(array):
        return pltpu.VMEM(array.shape, array.dtype)

    def held(tree):
        return jax.tree.map(lambda leaf: pltpu.VMEM(*leaf), tree, is_leaf=is_shape)

    def sems(tree):
        return jax.tree.map(lambda leaf: pltpu.SemaphoreType.DMA(()), tree, is_leaf=is_shape)

    arguments = (ins, later, scalars)
    results = (outs, saved, apart)
    own = (
        scratch,
        jax.tree.map(buffer, later),
        jax.tree.map(lambda leaf: pltpu.SemaphoreType.DMA(()), later),
        held(saved),
        sems(saved),
    )
    flat_in, tree_in = jax.tree.flatten(arguments)
    flat_out, tree_out = jax.tree.flatten(results, is_leaf=is_shape)
    flat_own, tree_own = jax.tree.flatten(own)

    def body(*refs):
        in_refs = jax.tree.unflatten(tree_in, refs[: len(flat_in)])
        out_refs = jax.tree.unflatten(tree_out, refs[len(flat_in) : len(flat_in) + len(flat_out)])
        own_refs = jax.tree.unflatten(tree_own, refs[len(flat_in) + len(flat_out) :])
        k = types.SimpleNamespace(**(extra or {}))
        for tree in (in_refs[0], in_refs[2], out_refs[0], out_refs[2], own_refs[0], own_refs[3]):
            k.__dict__.update(tree)
        waited = []
        for name, source in in_refs[1].items():
            parts = zip(*(jax.tree.leaves(tree) for tree in (source, own_refs[1][name], own_refs[2][name])))
            found = [Later(*part) for part in parts]
            waited += found
            setattr(k, name, found if isinstance(source, list) else found[0])
        saves = []
        for name in saved:
            parts = zip(*(jax.tree.leaves(tree[name]) for tree in (own_refs[3], out_refs[1], own_refs[4])))
            saves += [Saved(*part) for part in parts]

        def store(ref):
            for item in saves:
                if item.ref is ref:
                    item.store()

        k.store = store
        kernel(k)
        for item in waited:
            item()
        for item in saves:
            if item.copy is None:
                item.store()
        for item in saves:
            item.copy.wait()

    shapes = [jax.ShapeDtypeStruct(*leaf) for leaf in flat_out]
    moved = sum(a.size * a.dtype.itemsize for a in flat_in) + sum(
        math.prod(a.shape) * a.dtype.itemsize for a in shapes
    )
    there = pl.BlockSpec(memory_space=pl.ANY)
    here = pl.BlockSpec(memory_space=pltpu.VMEM)
    scalar = pl.BlockSpec(memory_space=pltpu.SMEM)

    def places(trees, kinds):
        return [kind for tree, kind in zip(trees, kinds) for _ in jax.tree.leaves(tree, is_leaf=is_shape)]

    found = pl.pallas_call(
        body,
        out_shape=shapes,
        in_specs=places(arguments, (here, there, scalar)),
        out_specs=places(results, (here, there, there)),
        scratch_shapes=flat_own,
        cost_estimate=pl.CostEstimate(flops=flops, bytes_accessed=moved, transcendentals=0),
        compiler_params=pltpu.CompilerParams(
            collective_id=ident, has_side_effects=ident is not None, vmem_limit_bytes=VMEM_BYTES
        ),
    )(*flat_in)
    found = jax.tree.unflatten(tree_out, found)
    return types.SimpleNamespace(**found[0], **found[1], **found[2])


def halve(array, axis):
    size = lax.axis_size(axis)
    index = lax.axis_index(axis)
    pieces = array.reshape((size, array.shape[0] // size) + array.shape[1:])
    distance = 1
    while distance < size:
        bit = (index // distance) % 2
        pairs = pieces.reshape((pieces.shape[0] // 2, 2) + pieces.shape[1:])
        keep = lax.dynamic_index_in_dim(pairs, bit, axis=1, keepdims=False)
        give = lax.dynamic_index_in_dim(pairs, 1 - bit, axis=1, keepdims=False)
        got = lax.ppermute(give, axis, [(i, i ^ distance) for i in range(size)])
        pieces = (keep.astype(FULL) + got.astype(FULL)).astype(array.dtype)
        distance *= 2
    return pieces[0]


def scatter_plain(left, right):
    return halve(inner(flat(left), right.T).astype(LOW), "seq").astype(FULL).T


def scatter_gains(gains):
    count = lax.axis_size("tensor")
    n_seq = lax.axis_size("seq")
    shaped = gains.reshape(4, n_seq, -1).transpose(1, 0, 2)
    mine = halve(shaped, "seq")[0]
    distance = 1
    while distance < count:
        mine = mine + lax.ppermute(mine, "tensor", [(i, i ^ distance) for i in range(count)])
        distance *= 2
    width = mine.shape[-1] // count
    return lax.dynamic_slice_in_dim(mine, lax.axis_index("tensor") * width, width, 1)


def on_device(
    inputs,
    cotangent,
    seq_lengths,
    norm_gains,
    query_one,
    key_one,
    value_one,
    out_one,
    gate_one,
    up_one,
    down_one,
    query_two,
    key_two,
    value_two,
    out_two,
    gate_two,
    up_two,
    down_two,
):
    rows, width = inputs.shape
    size = lax.axis_size("seq")
    stretch = 4 * rows
    units = gate_one.shape[1]
    cols = value_one.shape[1]
    small = query_one.shape[1]
    scatter = width // size == BLOCK
    count = int(math.log2(size))
    wide = ((4, 2, HALF, width), LOW)
    own = ((CHUNKS, HALF, width), FULL)
    heads = ((stretch, cols), LOW)
    heads_full = ((stretch, cols), FULL)
    narrow = ((stretch, small), LOW)
    unit_rows = ((CHUNKS, 2, HALF, units), LOW)
    turned_units = ((units, stretch), LOW)
    turned_cols = ((cols, stretch), LOW)
    state = ((FEATS + NORM_ROWS, cols), FULL)
    padded = ((stretch + WINDOW, cols), LOW)
    one_flops = 2 * stretch * width
    blocks = functools.partial(Scatter.blocks, size)
    choice, feature_rows = feature_tables()
    tables = dict(feature_choice=choice, feature_rows=feature_rows)
    tensor_sums = dict(
        keep=pltpu.VMEM(*own),
        share_sems=pltpu.SemaphoreType.DMA((4, 2, CHUNKS)),
    )
    got = ((size // 2, units, BLOCK), LOW)
    ahead = run_kernel(
        functools.partial(first_kernel, size=size),
        0,
        dict(
            gains=norm_gains,
            inputs=inputs,
            cotangent=cotangent,
            w_query_one=query_one.T,
            w_key_one=key_one.T,
            w_value_one=value_one,
            **tables,
        ),
        dict(result=((rows, width), LOW), gain_grad=((1, width), FULL)),
        dict(
            **tensor_sums,
            **Taylor.scratch(size, cols),
            totals=[Total.scratch(width) for _ in range(3)],
            rows_in=pltpu.VMEM((rows, width), LOW),
            cot_in=pltpu.VMEM((rows, width), LOW),
            near_sems=pltpu.SemaphoreType.DMA((2, 4)),
            far_sems=pltpu.SemaphoreType.DMA((2, 2)),
            mixed_low=pltpu.VMEM(*heads),
            query2=pltpu.VMEM(*heads),
            keys=pltpu.VMEM(*padded),
            values=pltpu.VMEM(*padded),
            window_low=pltpu.VMEM(*heads),
            d_window=pltpu.VMEM(*heads),
            d_keys=pltpu.VMEM(padded[0], FULL),
            d_values=pltpu.VMEM(padded[0], FULL),
            middle_two=pltpu.VMEM(*own),
            hidden=pltpu.VMEM((CHUNKS, 2 * HALF, units), LOW),
            d_hidden=pltpu.VMEM((CHUNKS, 2 * HALF, units), FULL),
            gate_two=pltpu.VMEM((CHUNKS, 2 * HALF, units), FULL),
            up_two=pltpu.VMEM((CHUNKS, 2 * HALF, units), FULL),
            d_gate_low=pltpu.VMEM((CHUNKS, 2 * HALF, units), LOW),
            d_up_low=pltpu.VMEM((CHUNKS, 2 * HALF, units), LOW),
            halo_out=pltpu.VMEM((2, 2, WINDOW, cols), LOW),
            halo_in=pltpu.VMEM((2, 2, WINDOW, cols), LOW),
            halo_sems=pltpu.SemaphoreType.DMA((2, 2, 2)),
            gives=[pltpu.VMEM(*got), pltpu.VMEM(*got)],
            give_sems=pltpu.SemaphoreType.DMA((2, 2, size // 2)),
        ),
        one_flops * (8 * cols + 9 * units),
        later=dict(
            w_out_one=out_one,
            w_gate_one=gate_one.T,
            w_up_one=up_one.T,
            w_down_one=down_one,
            w_key_two=key_two,
            w_value_two=value_two,
            w_query_two=query_two,
            w_out_two=out_two,
            w_gate_two=gate_two.T,
            w_up_two=up_two.T,
            w_down_two=down_two,
        ),
        saved=dict(
            start=own,
            middle=own,
            after=own,
            grad=own,
            normed_one=wide,
            normed_two=wide,
            normed_three=wide,
            normed_four=wide,
            cot=wide,
            grad_three=wide,
            query=narrow,
            key=narrow,
            value=heads,
            mixed=heads_full,
            inverse=heads_full,
            mixed_turned=turned_cols,
            carry=state,
            gate=unit_rows,
            up=unit_rows,
            hidden_one=turned_units,
            hidden_two=turned_units,
            d_gate_two=turned_units,
            d_up_two=turned_units,
            window_turned=turned_cols,
            d_query2=heads,
            d_key2=heads,
            d_value2=heads,
            d_turned2=((3 * cols, stretch), LOW),
        ),
        apart=dict(begun=[got, got]) if scatter else None,
        scalars=dict(lengths=seq_lengths),
        extra=dict(scatter=scatter),
    )
    widths = [units, units, units, cols, 3 * cols, units, units, units, 2 * small + cols, cols]
    carried = dict(
        d_query2=ahead.d_query2,
        d_key2=ahead.d_key2,
        d_value2=ahead.d_value2,
        w_query_two=query_two,
        w_key_two=key_two,
        w_value_two=value_two,
    )
    summed = dict(
        normed_four=ahead.normed_four,
        d_up_two=ahead.d_up_two,
        d_gate_two=ahead.d_gate_two,
        cot=ahead.cot,
        hidden_two=ahead.hidden_two,
        grad_three=ahead.grad_three,
        window_turned=ahead.window_turned,
        normed_three=ahead.normed_three,
        d_turned2=ahead.d_turned2,
        normed_two=ahead.normed_two,
        hidden_one=ahead.hidden_one,
        normed_one=ahead.normed_one,
        mixed_turned=ahead.mixed_turned,
    )
    chain = dict(
        after=ahead.after,
        grad=ahead.grad,
        w_down_one=down_one,
        gate=ahead.gate,
        up=ahead.up,
        w_gate_one=gate_one.T,
        w_up_one=up_one.T,
        middle=ahead.middle,
        w_out_one=out_one,
        query=ahead.query,
        key=ahead.key,
        value=ahead.value,
        mixed=ahead.mixed,
        inverse=ahead.inverse,
        carry=ahead.carry,
        w_query_one=query_one.T,
        w_key_one=key_one.T,
        w_value_one=value_one,
        start=ahead.start,
    )
    early = ("normed_four", "d_up_two", "d_gate_two")
    made = dict(
        d_gate_one=turned_units,
        d_up_one=turned_units,
        d_turned=((2 * small + cols, stretch), LOW),
        grad_two=wide,
        grad_one=wide,
    )
    if scatter:
        gain_blocks = [pltpu.VMEM((size >> (at + 1), 8, BLOCK), FULL) for at in range(count)]
        buffers = dict(
            gives=[[] if name in (5, 6, 7) else blocks(wide_) for name, wide_ in enumerate(widths)] + [gain_blocks],
            gots=[blocks(wide_) for wide_ in widths] + [gain_blocks],
            sems=[pltpu.SemaphoreType.DMA((11, 2, size >> (at + 1))) for at in range(count)],
            gain_sum=pltpu.VMEM((3, 8, BLOCK), FULL),
            gain_in_sum=pltpu.VMEM((2, 8, BLOCK), FULL),
            gain_sems=pltpu.SemaphoreType.DMA((2, 2)),
            **{name: pltpu.VMEM(*leaf) for name, leaf in made.items()},
        )
        for name in (0, 2):
            buffers["gots"][name][0] = None
        inputs_later = dict(
            **carried,
            **{name: summed[name] for name in early},
            begun=ahead.begun,
            **chain,
            **{name: array for name, array in summed.items() if name not in early},
        )
        kept = dict(sums=[((wide_, BLOCK), FULL) for wide_ in widths])
    else:
        buffers = {}
        inputs_later = dict(**carried, **chain)
        kept = made
    behind = run_kernel(
        functools.partial(second_kernel, size=size),
        1,
        dict(gains=norm_gains, gain_in=ahead.gain_grad, **tables),
        dict(input_grad=((rows, width), FULL), gain_out=((8, BLOCK // 4 if scatter else width), FULL)),
        dict(
            **tensor_sums,
            **Taylor.scratch(size, cols),
            totals=[Total.scratch(width) for _ in range(2)],
            d_mixed=pltpu.VMEM(*heads),
            gain_rows=pltpu.VMEM((8, width), FULL),
            grad_carry=pltpu.VMEM(*state),
            d_query_acc=pltpu.VMEM((stretch, small), FULL),
            d_key_acc=pltpu.VMEM((stretch, small), FULL),
            d_value_acc=pltpu.VMEM((stretch, cols), FULL),
            d_query_low=pltpu.VMEM(*narrow),
            d_key_low=pltpu.VMEM(*narrow),
            d_value_low=pltpu.VMEM(*heads),
            **buffers,
        ),
        one_flops * (6 * cols + 9 * units),
        later=inputs_later,
        saved=kept,
        scalars=dict(lengths=seq_lengths),
        extra=dict(scatter=scatter),
    )
    if not scatter:
        sums = [
            scatter_plain(left, right)
            for left, right in (
                (ahead.normed_four, ahead.d_gate_two),
                (ahead.normed_four, ahead.d_up_two),
                (ahead.cot, ahead.hidden_two),
                (ahead.grad_three, ahead.window_turned),
                (ahead.normed_three, ahead.d_turned2),
                (ahead.normed_two, behind.d_gate_one),
                (ahead.normed_two, behind.d_up_one),
                (behind.grad_two, ahead.hidden_one),
                (ahead.normed_one, behind.d_turned),
                (behind.grad_one, ahead.mixed_turned),
            )
        ]
        gains = scatter_gains(behind.gain_out[:4])
        three_one, three_two = sums[8], sums[4]
        return (
            (ahead.result, behind.input_grad, gains)
            + (three_one[:small].T, three_one[small : 2 * small].T, three_one[2 * small :].T)
            + (sums[9], sums[5].T, sums[6].T, sums[7])
            + tuple(three_two[first : first + cols].T for first in range(0, 3 * cols, cols))
            + (sums[3], sums[0].T, sums[1].T, sums[2])
        )
    block = ((BLOCK, cols), FULL)
    unit = ((units, BLOCK), FULL)
    done = run_kernel(
        functools.partial(finish_kernel, small=small, cols=cols),
        None,
        dict(
            result_in=ahead.result,
            input_grad_in=behind.input_grad,
            gains_in=behind.gain_out,
            sums=[behind.sums[name] for name in (0, 1, 2, 3, 5, 6, 7, 9)],
            threes=[behind.sums[8], behind.sums[4]],
        ),
        dict(
            result=((rows, width), LOW),
            input_grad=((rows, width), FULL),
            gains=((4, BLOCK // 4), FULL),
            same=[unit, unit, unit, ((cols, BLOCK), FULL), unit, unit, unit, ((cols, BLOCK), FULL)],
            turned=[[((small, BLOCK), FULL), ((small, BLOCK), FULL), block], [block, block, block]],
        ),
        {},
        stretch,
    )
    same, turned = done.same, done.turned
    return (
        (done.result, done.input_grad, done.gains)
        + (turned[0][0].T, turned[0][1].T, turned[0][2])
        + (same[7], same[4].T, same[5].T, same[6])
        + tuple(turned[1])
        + (same[3], same[0].T, same[1].T, same[2])
    )


def solution(mesh):
    both = P(("seq", "tensor"), None)
    split = P(None, "tensor")
    stacked = P("tensor", None)
    columns_out = P("seq", "tensor")
    rows_out = P("tensor", "seq")
    layer_in = (split, split, split, stacked, split, split, stacked)
    layer_out = (columns_out, columns_out, columns_out, rows_out, columns_out, columns_out, rows_out)
    return jax.shard_map(
        on_device,
        mesh=mesh,
        in_specs=(both, both, P(), P()) + layer_in + layer_in,
        out_specs=(both, both, P(None, ("seq", "tensor"))) + layer_out + layer_out,
        check_vma=False,
    )
```

```python
import functools
import math
import types

import jax
import jax.numpy as jnp
import numpy as np
from jax import lax
from jax.experimental import pallas as pl
from jax.experimental.pallas import tpu as pltpu
from jax.sharding import PartitionSpec as P

FEAT = 16
HEAD = 64
WINDOW = 64
BLOCK = 128
EPS = 1e-05
FLOOR_SCORE = -1e30
MESH = pl.DeviceIdType.MESH
LOW = jnp.bfloat16
FULL = jnp.float32
VMEM_BYTES = 60 * 1024 * 1024
HALF = BLOCK // 2
CHUNKS = 4
PAIRS = [(a, b) for a in range(FEAT + 1) for b in range(a, FEAT + 1)]
FEATS = -(-len(PAIRS) // 16) * 16
NORM_ROWS = 16


def plain(left, right):
    return jnp.dot(left, right, preferred_element_type=FULL)


def inner(left, right):
    return lax.dot_general(left, right, (((0,), (0,)), ((), ())), preferred_element_type=FULL)


def through(left, right):
    return lax.dot_general(left, right, (((1,), (1,)), ((), ())), preferred_element_type=FULL)


def flat(array):
    return array.reshape((math.prod(array.shape[:-1]), array.shape[-1]))


class Group:
    def __init__(self):
        index = lax.axis_index("tensor")
        self.index = index
        self.low = lax.rem(index, 2)
        self.high = index // 2
        self.pair = dict(tensor=index + 1 - 2 * self.low)
        self.partner = dict(tensor=lax.rem(index + 2, 4))

    def mine(self, chunk):
        return jnp.where(self.high == chunk // 2, 1.0, 0.0)

    def split(self, part, count, by_rows=False):
        if by_rows:
            zero, one = part.reshape(2, count, HALF, -1)
        else:
            whole = part.reshape(count, 2, HALF, -1)
            zero, one = whole[:, 0], whole[:, 1]
        even = self.low == 0
        return jnp.where(even, zero, one), jnp.where(even, one, zero)

    def own_rows(self, ref, chunk, count):
        return ref.at[self.low + 2 * (chunk // 2), pl.ds(chunk % 2, count)]

    def own_chunks(self, ref, chunk, count):
        return ref.at[pl.ds(chunk, count), self.low]


def chunk_rows(ref, chunk, count=1):
    first, half = 2 * (chunk // 2), chunk % 2
    if len(ref.shape) == 4:
        return flat(ref[first : first + 2, half : half + count])
    starts = [block * BLOCK + half * HALF for block in (first, first + 1)]
    return jnp.concatenate([ref[start : start + count * HALF] for start in starts], axis=0)


def put_rows(ref, chunk, value, ahead=0):
    for side in range(2):
        start = ahead + (2 * (chunk // 2) + side) * BLOCK + chunk % 2 * HALF
        ref[start : start + HALF] = value[side * HALF : (side + 1) * HALF]


class Line:
    def __init__(self, size):
        self.size = size
        self.index = lax.axis_index("seq")
        self.after = dict(seq=lax.rem(self.index + 1, size))
        self.before = dict(seq=lax.rem(self.index + size - 1, size))

    def flip(self, relative):
        found = 0
        bit = 1
        while bit < self.size:
            found = found + bit * lax.rem(self.index // bit + relative // bit, 2)
            bit *= 2
        return found


def greet(peers, everyone=None):
    barrier = pltpu.get_barrier_semaphore()
    for peer in peers:
        pl.semaphore_signal(barrier, inc=1, device_id=peer, device_id_type=MESH)
    count = len(peers)
    if everyone is not None:

        def call(step, carry):
            peer = dict(seq=lax.rem(everyone.index + step, everyone.size))
            pl.semaphore_signal(barrier, inc=1, device_id=peer, device_id_type=MESH)
            return carry

        lax.fori_loop(1, everyone.size, call, 0)
        count += everyone.size - 1
    return lambda: pl.semaphore_wait(barrier, count)


def remote(src, dst, send, recv, device):
    return pltpu.make_async_remote_copy(
        src_ref=src, dst_ref=dst, send_sem=send, recv_sem=recv, device_id=device, device_id_type=MESH
    )


def send(src, dst, send_sem, recv_sem, device):
    copy = remote(src, dst, send_sem, recv_sem, device)
    copy.start()
    return copy


class Total:
    def __init__(self, group, keep, buffers):
        self.group = group
        self.keep = keep
        self.pair_out, self.pair_in, self.out, self.into, self.sems = buffers
        self.pairs = {}
        self.fars = {}
        self.arriving = {}
        self.arrived = set()

    @staticmethod
    def scratch(width):
        return [pltpu.VMEM((CHUNKS, HALF, width), LOW)] * 4 + [pltpu.SemaphoreType.DMA((4, CHUNKS))]

    def give(self, chunk, part, count=1, by_rows=False):
        own, other = self.group.split(part, count, by_rows)
        place = pl.ds(chunk, count)
        self.keep[place] = own
        self.pair_out[place] = other.astype(LOW)
        self.pairs[chunk] = send(
            self.pair_out.at[place],
            self.pair_in.at[place],
            self.sems.at[0, chunk],
            self.sems.at[1, chunk],
            self.group.pair,
        )
        self.arriving.update({chunk + step: chunk for step in range(count)})

    def pair_sum(self, chunk, count=1):
        given = self.arriving[chunk]
        if given not in self.arrived:
            self.arrived.add(given)
            self.pairs[given].wait_recv()
        place = pl.ds(chunk, count)
        return self.keep[place] + self.pair_in[place].astype(FULL)

    def swap(self, chunk, count=1):
        place = pl.ds(chunk, count)
        self.out[place] = self.pair_sum(chunk, count).astype(LOW)
        self.fars[chunk] = send(
            self.out.at[place],
            self.into.at[place],
            self.sems.at[2, chunk],
            self.sems.at[3, chunk],
            self.group.partner,
        )

    def swap_half(self):
        for chunk in range(0, CHUNKS, 2):
            self.out[chunk : chunk + 2] = self.pair_sum(chunk, 2).astype(LOW)
        self.fars[0] = send(
            self.out.at[pl.ds(2 - 2 * self.group.high, 2)],
            self.into.at[pl.ds(0, 2)],
            self.sems.at[2, 0],
            self.sems.at[3, 0],
            self.group.partner,
        )

    def take(self, chunk, count=1):
        self.fars[chunk].wait_recv()
        place = pl.ds(chunk, count)
        return self.out[place].astype(FULL) + self.into[place].astype(FULL)

    def take_half(self):
        self.fars[0].wait_recv()
        return self.out[pl.ds(2 * self.group.high, 2)].astype(FULL) + self.into[0:2].astype(FULL)

    def close(self):
        for copy in list(self.pairs.values()) + list(self.fars.values()):
            copy.wait_send()


class Share:
    def __init__(self, group, full, sems, place):
        self.group = group
        self.full = full
        self.sems = sems
        self.place = place
        self.copies = {}

    def give(self, chunk, value, count=1):
        rows = self.place(self.full, chunk, count)
        rows[...] = value
        self.copies[chunk] = send(
            rows, rows, self.sems.at[0, chunk], self.sems.at[1, chunk], self.group.pair
        )

    def await_other(self, chunk):
        self.copies[chunk].wait_recv()

    def close(self):
        for copy in self.copies.values():
            copy.wait_send()


def share_sems():
    return pltpu.SemaphoreType.DMA((2, CHUNKS))


def relay(first, second, share, enter, work, count=1, order=None, between=lambda: None):
    starts = order or list(range(0, CHUNKS, count))
    for step in range(len(starts) + 1):
        if step < len(starts):
            share.give(starts[step], enter(starts[step], first.take(starts[step], count)), count)
        if step > 1:
            second.swap(starts[step - 2], count)
        if step > 0:
            chunk = starts[step - 1]
            share.await_other(chunk)
            second.give(chunk, work(chunk), count)
        between()
    second.swap(starts[-1], count)


class Later:
    def __init__(self, source, target, sem):
        self.copy = pltpu.make_async_copy(source, target, sem)
        self.copy.start()
        self.target = target
        self.waiting = True

    def __call__(self):
        if self.waiting:
            self.copy.wait()
            self.waiting = False
        return self.target


class Saved:
    def __init__(self, ref, target, sem):
        self.ref = ref
        self.target = target
        self.sem = sem
        self.copy = None

    def store(self):
        self.copy = pltpu.make_async_copy(self.ref, self.target, self.sem)
        self.copy.start()


class Scatter:
    def __init__(self, line, source, order, give, got, sems, begun=0):
        self.line = line
        self.ready, self.base = source
        self.order = order
        self.give = give
        self.got = got
        self.sems = sems
        self.begun = begun

    @staticmethod
    def blocks(size, width):
        return [pltpu.VMEM((size >> (at + 1), width, BLOCK), LOW) for at in range(int(math.log2(size)))]

    def copy(self, at, index):
        return remote(
            self.give[at].at[index],
            self.got[at].at[index],
            self.sems[at].at[0, index],
            self.sems[at].at[1, index],
            dict(seq=self.line.flip(self.order[at])),
        )

    def part(self, place, upto):
        relative = sum(bit for at, bit in enumerate(self.order) if place >> at & 1)
        total = self.base(self.line.flip(relative))
        for at in range(upto):
            index = place >> (at + 1)
            if at >= self.begun:
                self.copy(at, index).wait_recv()
            total = total + self.got[at][index].astype(FULL)
        return total

    def places(self, at):
        return sorted(range(self.line.size >> (at + 1)), key=lambda index: (index & -index) or self.line.size)

    def prepare(self, at, index):
        self.ready()
        self.give[at][index] = self.part(2**at * (2 * index + 1), at).astype(self.give[at].dtype)

    def start(self, at, prepared=False):
        for index in self.places(at):
            if not prepared:
                self.prepare(at, index)
            self.copy(at, index).start()

    def finish(self):
        return self.part(0, len(self.order))

    def arrive(self, at):
        for index in self.places(at):
            self.copy(at, index).wait_recv()

    def sent(self):
        for at in range(self.begun, len(self.sems)):
            for index in self.places(at):
                self.copy(at, index).wait_send()


def columns_of(block):
    return pl.ds(pl.multiple_of(block * BLOCK, BLOCK), BLOCK)


def product(left, right):
    def base(block):
        return plain(held(right)[...], flat(held(left)[:, :, :, columns_of(block)]))

    def ready():
        held(left)
        held(right)

    return ready, base


def held(item):
    return item() if isinstance(item, Later) else item


def norm_apply(values, gain):
    inverse = lax.rsqrt(jnp.mean(values * values, axis=-1, keepdims=True) + EPS)
    return (values * inverse * gain).astype(LOW)


def norm_back(grad, values, gain):
    inverse = lax.rsqrt(jnp.mean(values * values, axis=-1, keepdims=True) + EPS)
    scaled = values * inverse
    d_scaled = grad * gain
    d_values = inverse * (d_scaled - scaled * jnp.mean(d_scaled * scaled, axis=-1, keepdims=True))
    return d_values, jnp.sum(grad * scaled, axis=0, keepdims=True)


def gate_forward(gate, up_val):
    return gate * up_val / (1.0 + jnp.exp(-gate))


def gate_backward(d_hidden, gate, up_val):
    sigma = 1.0 / (1.0 + jnp.exp(-gate))
    return d_hidden * up_val * sigma * (1.0 + gate * (1.0 - sigma)), d_hidden * gate * sigma


def segment_of(lengths, positions):
    end = 0
    found = jnp.zeros_like(positions)
    for index in range(lengths.shape[0]):
        end = end + lengths[index]
        found = found + jnp.where(positions >= end, 1, 0)
    return found


def ramp(shape, axis, first):
    return lax.broadcasted_iota(jnp.int32, shape, axis) + first


def same(left, right):
    return jnp.where(left == right, 1.0, 0.0)


def feature_tables():
    choice = np.zeros((2, FEAT, FEATS), np.float32)
    rows = np.zeros((8, FEATS), np.float32)
    for index, pair in enumerate(PAIRS):
        for side, entry in enumerate(pair):
            if entry < FEAT:
                choice[side, entry, index] = 1.0
            else:
                rows[side, index] = 1.0
        rows[2, index] = 0.5**0.5 if pair[0] == pair[1] and pair[0] < FEAT else 1.0
    return jnp.asarray(choice, LOW), jnp.asarray(rows, FULL)


class Taylor:
    def __init__(self, line, k, query, key, value):
        self.line = line
        self.k = k
        self.query = query
        self.key = key
        self.value = value
        self.rows = query.shape[0]
        self.count = self.rows // BLOCK
        self.heads = value.shape[1] // HEAD
        start = line.index * self.rows
        self.start = start
        column = segment_of(k.lengths, ramp((self.rows, 1), 0, start))
        last = segment_of(k.lengths, ramp((1, 1), 0, start + self.rows - 1))
        before = segment_of(k.lengths, ramp((1, 1), 0, start - 1))
        self.last = last
        self.before = before
        self.segments = column
        self.across = segment_of(k.lengths, ramp((1, self.rows), 1, start))
        self.tail = same(column, last)
        self.carried = same(column, before)
        self.lane = ramp((1, self.heads * HEAD), 1, 0) // HEAD

    def half(self, array, head, upto=None, only=None):
        first, last = (0, upto or self.count) if only is None else (only, only + 1)
        return array[first * BLOCK : last * BLOCK, head * FEAT : (head + 1) * FEAT] * jnp.asarray(0.5, LOW)

    def factors(self, half):
        rows = self.k.feature_rows
        left = plain(half, self.k.feature_choice[0]) + rows[0:1]
        right = plain(half, self.k.feature_choice[1]) + rows[1:2]
        return left, right

    def features(self, array, head):
        left, right = self.factors(self.half(array, head))
        return left * right * self.k.feature_rows[2:3]

    def features_back(self, grad, array, head):
        left, right = self.factors(self.half(array, head))
        weighted = grad * self.k.feature_rows[2:3]
        return through((weighted * right).astype(LOW), self.k.feature_choice[0]) + through(
            (weighted * left).astype(LOW), self.k.feature_choice[1]
        )

    def of_head(self, head, array):
        return jnp.where(self.lane == head, array, jnp.zeros_like(array))

    def mask(self, block):
        upto = (block + 1) * BLOCK
        rows = ramp((BLOCK, 1), 0, block * BLOCK)
        allowed = (ramp((1, upto), 1, 0) <= rows) & (
            self.across[:, :upto] == self.segments[block * BLOCK : upto]
        )
        return jnp.where(allowed, 1.0, 0.0)

    def far_first(self, step, forward):
        return self.line.size - 1 - step if forward else step

    def send_state(self, forward):
        line = self.line

        def step(index, carry):
            other = self.far_first(index, forward)

            @pl.when((other > line.index) if forward else (other < line.index))
            def _():
                self.state_copy(other).start()

            return carry

        lax.fori_loop(0, line.size, step, 0)

    def state_copy(self, other):
        k = self.k
        return remote(
            k.state_own,
            k.state_slots.at[self.line.index],
            k.state_sems.at[0, other],
            k.state_sems.at[1, self.line.index],
            dict(seq=other),
        )

    def state_arrival(self, other):
        k = self.k
        return remote(
            k.state_own,
            k.state_slots.at[other],
            k.state_sems.at[0, other],
            k.state_sems.at[1, other],
            dict(seq=other),
        )

    def take_state(self, total, forward):
        k, line = self.k, self.line
        total[...] = jnp.zeros_like(total)

        def step(index, carry):
            other = self.far_first(index, forward)

            @pl.when((other < line.index) if forward else (other > line.index))
            def _():
                self.state_arrival(other).wait_recv()
                if forward:
                    edge = segment_of(k.lengths, ramp((1, 1), 0, (other + 1) * self.rows - 1))
                    weight = same(edge, self.before)
                else:
                    edge = segment_of(k.lengths, ramp((1, 1), 0, other * self.rows - 1))
                    weight = same(edge, self.last)
                total[...] += weight * k.state_slots[other].astype(FULL)

            return carry

        lax.fori_loop(0, line.size, step, 0)

    def close(self, forward):
        line = self.line

        def step(other, carry):
            @pl.when((other > line.index) if forward else (other < line.index))
            def _():
                self.state_copy(other).wait_send()

            return carry

        lax.fori_loop(0, line.size, step, 0)

    @staticmethod
    def scratch(size, cols):
        shape = (FEATS + NORM_ROWS, cols)
        return dict(
            state_own=pltpu.VMEM(shape, LOW),
            state_build=pltpu.VMEM(shape, FULL),
            state_slots=pltpu.VMEM((size,) + shape, LOW),
            state_sems=pltpu.SemaphoreType.DMA((2, size)),
        )

    def forward(self, meanwhile):
        k = self.k
        value = self.value[...]
        build = k.state_build
        build[...] = jnp.zeros_like(build)
        state = jnp.zeros((FEATS, value.shape[1]), FULL)
        for head in range(self.heads):
            feats = self.features(self.key, head) * self.tail
            state = state + self.of_head(head, inner(feats.astype(LOW), value))
            build[FEATS + head : FEATS + head + 1, :FEATS] = jnp.sum(feats, axis=0, keepdims=True)
        build[:FEATS] = state
        k.state_own[...] = build[...].astype(LOW)
        self.send_state(True)
        for block in range(self.count):
            allowed = self.mask(block)
            rows = slice(block * BLOCK, (block + 1) * BLOCK)
            for head in range(self.heads):
                places = slice(head * HEAD, (head + 1) * HEAD)
                score = through(self.half(self.query, head, only=block), self.half(self.key, head, block + 1))
                score = allowed * (1.0 + score + 0.5 * score * score)
                k.mixed[rows, places] = plain(score.astype(LOW), value[: (block + 1) * BLOCK, places])
                k.inverse[rows, places] = jnp.broadcast_to(jnp.sum(score, axis=1, keepdims=True), (BLOCK, HEAD))
        for head in range(self.heads):
            k.query_feats[head] = self.features(self.query, head).astype(LOW)
        meanwhile()
        self.take_state(k.carry, True)
        state = k.carry[:FEATS].astype(LOW)
        numerator = jnp.zeros((self.rows, value.shape[1]), FULL)
        totals = jnp.zeros((self.rows, value.shape[1]), FULL)
        for head in range(self.heads):
            feats = k.query_feats[head]
            numerator = numerator + self.of_head(head, plain(feats, state))
            norm = k.carry[FEATS + head : FEATS + head + 1, :FEATS]
            totals = totals + self.of_head(head, jnp.sum(feats * norm, axis=1, keepdims=True) + jnp.zeros_like(totals))
        inverse = 1.0 / (k.inverse[...] + self.carried * totals)
        mixed = (k.mixed[...] + self.carried * numerator) * inverse
        k.inverse[...] = inverse
        k.mixed[...] = mixed
        k.mixed_low[...] = mixed.astype(LOW)
        k.mixed_turned[...] = mixed.T.astype(LOW)

    def backward(self, d_mixed):
        k = self.k
        value = self.value[...]
        d_out = d_mixed[...].astype(FULL)
        d_numer = d_out * k.inverse[...]
        d_low = d_numer.astype(LOW)
        product = d_numer * k.mixed[...]
        d_totals = [
            -jnp.sum(product[:, head * HEAD : (head + 1) * HEAD], axis=1, keepdims=True) for head in range(self.heads)
        ]
        build = k.state_build
        build[...] = jnp.zeros_like(build)
        state = jnp.zeros((FEATS, value.shape[1]), FULL)
        for head in range(self.heads):
            feats = self.features(self.query, head) * self.carried
            state = state + self.of_head(head, inner(feats.astype(LOW), d_low))
            build[FEATS + head : FEATS + head + 1, :FEATS] = jnp.sum(feats * d_totals[head], axis=0, keepdims=True)
        build[:FEATS] = state
        k.state_own[...] = build[...].astype(LOW)
        self.send_state(False)
        yield
        carry = k.carry[:FEATS].astype(LOW)
        k.d_key_acc[...] = jnp.zeros_like(k.d_key_acc)
        k.d_value_acc[...] = jnp.zeros_like(k.d_value_acc)
        for head in range(self.heads):
            norm = k.carry[FEATS + head : FEATS + head + 1, :FEATS]
            d_feats = self.carried * (through(self.of_head(head, d_low), carry) + d_totals[head] * norm)
            k.d_query_acc[:, head * FEAT : (head + 1) * FEAT] = self.features_back(d_feats, self.query, head)
        for block in range(self.count):
            allowed = self.mask(block)
            upto = (block + 1) * BLOCK
            rows = slice(block * BLOCK, upto)
            for head in range(self.heads):
                places = slice(head * HEAD, (head + 1) * HEAD)
                narrow = slice(head * FEAT, (head + 1) * FEAT)
                query = self.half(self.query, head, only=block)
                key = self.half(self.key, head, block + 1)
                score = through(query, key)
                d_rows = d_low[rows, places]
                d_score = through(d_rows, value[:upto, places]) + d_totals[head][rows]
                d_score = (allowed * d_score * (1.0 + score)).astype(LOW)
                score = (allowed * (1.0 + score + 0.5 * score * score)).astype(LOW)
                k.d_query_acc[rows, narrow] += plain(d_score, key)
                k.d_key_acc[:upto, narrow] += inner(d_score, query)
                k.d_value_acc[:upto, places] += inner(score, d_rows)
            yield
        self.take_state(k.grad_carry, False)
        carry = k.grad_carry[:FEATS].astype(LOW)
        for head in range(self.heads):
            norm = k.grad_carry[FEATS + head : FEATS + head + 1, :FEATS]
            d_feats = self.tail * (through(self.of_head(head, value), carry) + norm)
            k.d_key_acc[:, head * FEAT : (head + 1) * FEAT] += self.features_back(d_feats, self.key, head)
            feats = self.features(self.key, head).astype(LOW)
            k.d_value_acc[...] += self.of_head(head, self.tail * plain(feats, carry))


def window_mask(k, line, first, count):
    start = line.index * k.query2.shape[0] + first
    query = ramp((count, 1), 0, start)
    key = ramp((1, count + WINDOW), 1, start - WINDOW)
    return (
        (key <= query)
        & (key > query - WINDOW)
        & (key >= 0)
        & (segment_of(k.lengths, key) == segment_of(k.lengths, query))
    )


def window_weights(query, key, allowed):
    score = jnp.where(allowed, through(query, key) * HEAD**-0.5, FLOOR_SCORE)
    weight = jnp.exp(score - jnp.max(score, axis=1, keepdims=True))
    return weight / jnp.sum(weight, axis=1, keepdims=True)


def window_forward(k, line, chunk):
    for side in range(2):
        first = (2 * (chunk // 2) + side) * BLOCK + chunk % 2 * HALF
        own = slice(first, first + HALF)
        span = slice(first, first + HALF + WINDOW)
        allowed = window_mask(k, line, first, HALF)
        outs = []
        for head in range(k.keys.shape[1] // HEAD):
            places = slice(head * HEAD, (head + 1) * HEAD)
            weight = window_weights(k.query2[own, places], k.keys[span, places], allowed)
            outs.append(plain(weight.astype(LOW), k.values[span, places]))
        k.window_low[own] = jnp.concatenate(outs, axis=1).astype(LOW)


def window_backward(k, line, block):
    own = slice(block * BLOCK, (block + 1) * BLOCK)
    allowed = window_mask(k, line, block * BLOCK, BLOCK)
    span = slice(block * BLOCK, (block + 1) * BLOCK + WINDOW)
    grads = []
    for head in range(k.keys.shape[1] // HEAD):
        places = slice(head * HEAD, (head + 1) * HEAD)
        query = k.query2[own, places]
        key = k.keys[span, places]
        d_out = k.d_window[own, places]
        weight = window_weights(query, key, allowed)
        d_weight = through(d_out, k.values[span, places])
        d_score = weight * (d_weight - jnp.sum(weight * d_weight, axis=1, keepdims=True)) * HEAD**-0.5
        d_score = d_score.astype(LOW)
        grads.append(plain(d_score, key))
        k.d_keys[span, places] += inner(d_score, query)
        k.d_values[span, places] += inner(weight.astype(LOW), d_out)
    whole = jnp.concatenate(grads, axis=1)
    k.d_query2[own] = whole.astype(LOW)
    k.d_turned2[: whole.shape[1], own] = whole.T.astype(LOW)


X_FIRST, Z_FIRST = (1, 2, 4), (2, 4, 1)
ORDERS = [X_FIRST, Z_FIRST, X_FIRST, Z_FIRST, X_FIRST, X_FIRST, X_FIRST, X_FIRST, X_FIRST, X_FIRST, X_FIRST]
PLAN = [[(4, 0), (1, 1), (0, 1), (2, 0), (4, 1)], [(0, 2), (3, 0)], [], [(4, 2)], [(5, 0), (2, 1)], [], [(1, 2)], [], [(3, 1), (5, 1)], [(2, 2)], [(7, 0), (5, 2), (7, 1), (6, 0)], [], [(7, 2), (2, 3), (6, 1)], [(10, 0)], [(8, 0), (7, 3), (9, 0), (6, 2), (4, 3), (5, 3), (3, 2), (10, 1), (8, 1), (10, 2), (9, 1), (8, 2), (11, 0), (11, 1), (1, 3), (3, 3), (11, 2), (9, 2), (0, 3), (6, 3), (8, 3), (9, 3)]]


def first_kernel(k, size):
    group, line = Group(), Line(size)
    greet([group.pair, group.partner], line)()
    width = k.inputs.shape[1]
    rows = k.query.shape[0]
    cols = k.value.shape[1]
    total_a, total_b, total_c = (Total(group, k.keep, k.totals[i]) for i in range(3))
    closing = [total_a, total_b]

    def offer(step, block, raw):
        values = raw.astype(FULL)
        k.start[pl.ds(2 * (block // 2), 2)] = values.reshape(2, HALF, width)
        k.normed_one[block] = norm_apply(values, k.gains[0:1]).reshape(2, HALF, width)
        place = k.normed_one.at[block]
        copy = send(place, place, k.near_sems.at[0, step], k.near_sems.at[1, step], group.pair)
        copy.wait_recv()
        return copy

    def project_one(pair):
        normed = flat(k.normed_one[pl.ds(2 * pair, 2)])
        place = pl.ds(pl.multiple_of(pair * 2 * BLOCK, 2 * BLOCK), 2 * BLOCK)
        k.key[place] = through(normed, k.w_key_one[...]).astype(LOW)
        k.value[place] = plain(normed, k.w_value_one[...]).astype(LOW)
        k.query[place] = through(normed, k.w_query_one[...]).astype(LOW)

    def offer_cot(step, half, raw):
        place = k.cot.at[pl.ds(2 * half, 2), group.low]
        place[...] = raw.reshape(2, HALF, width)
        return send(place, place, k.near_sems.at[0, 2 + step], k.near_sems.at[1, 2 + step], group.pair)

    far = send(k.inputs, k.rows_in, k.far_sems.at[0, 0], k.far_sems.at[1, 0], group.partner)
    copies = [offer(0, group.index, k.inputs[...])]
    project_one(group.high)
    far.wait_recv()
    far_cot = send(k.cotangent, k.cot_in, k.far_sems.at[0, 1], k.far_sems.at[1, 1], group.partner)
    copies.append(offer(1, lax.rem(group.index + 2, 4), k.rows_in[...]))
    project_one(1 - group.high)
    copies.append(offer_cot(0, group.high, k.cotangent[...]))
    taylor = Taylor(line, k, k.query, k.key, k.value)

    def turn_ahead():
        far_cot.wait_recv()
        copies.append(offer_cot(1, 1 - group.high, k.cot_in[...]))
        for copy in copies[2:]:
            copy.wait_recv()
        k.store(k.cot)
        for chunk in range(0, CHUNKS, 2):
            found = through(flat(k.cot[chunk : chunk + 2]), k.w_down_two()[...])
            k.d_hidden[chunk : chunk + 2] = found.reshape(2, 2 * HALF, -1)

    taylor.forward(turn_ahead)
    for item in (k.start, k.normed_one, k.query, k.key, k.value, k.mixed, k.inverse, k.mixed_turned, k.carry):
        k.store(item)

    share = Share(group, k.normed_two, k.share_sems.at[0], group.own_chunks)
    closing.append(share)

    def enter_mlp(chunk, total):
        middle = k.start[chunk : chunk + 1] + total
        k.middle[chunk : chunk + 1] = middle
        return norm_apply(middle, k.gains[1:2])

    def mlp_one(chunk):
        normed = flat(k.normed_two[chunk])
        gate = through(normed, k.w_gate_one()[...])
        up_val = through(normed, k.w_up_one()[...])
        k.gate[chunk] = gate.astype(LOW).reshape(k.gate.shape[1:])
        k.up[chunk] = up_val.astype(LOW).reshape(k.up.shape[1:])
        hidden = gate_forward(gate, up_val)
        k.hidden_one[:, chunk * BLOCK : (chunk + 1) * BLOCK] = hidden.T.astype(LOW)
        return plain(hidden.astype(LOW), k.w_down_one()[...])

    order = [2, 3, 0, 1]
    for chunk in (2, 0):
        part = plain(chunk_rows(k.mixed_low, chunk, 2), k.w_out_one()[...])
        total_a.give(chunk, part, 2, by_rows=True)
    for chunk in order:
        total_a.swap(chunk)
    relay(total_a, total_b, share, enter_mlp, mlp_one, order=order)
    for item in (k.middle, k.normed_two, k.gate, k.up, k.hidden_one):
        k.store(item)

    share = Share(group, k.normed_three, k.share_sems.at[1], group.own_rows)
    closing.append(share)

    def project_two(chunk):
        normed = chunk_rows(k.normed_three, chunk)
        put_rows(k.keys, chunk, plain(normed, k.w_key_two()[...]).astype(LOW), WINDOW)
        put_rows(k.values, chunk, plain(normed, k.w_value_two()[...]).astype(LOW), WINDOW)
        put_rows(k.query2, chunk, plain(normed, k.w_query_two()[...]).astype(LOW))

    def attend(chunk):
        window_forward(k, line, chunk)
        total_a.give(chunk, plain(chunk_rows(k.window_low, chunk), k.w_out_two()[...]))

    for step in range(CHUNKS + 1):
        if step < CHUNKS:
            chunk = order[step]
            after = k.middle[chunk : chunk + 1] + total_b.take(chunk)
            k.after[chunk : chunk + 1] = after
            share.give(chunk, norm_apply(after, k.gains[2:3]))
        if step > 0:
            chunk = order[step - 1]
            share.await_other(chunk)
            project_two(chunk)
        if step == 2:
            halo = Halo(k, 0, (k.keys, k.values), slice(rows, rows + WINDOW), line.after)
            total_a.close()
            total_a = Total(group, k.keep, k.totals[0])
            attend(3)
    total_a.swap(3)
    for item in closing[1:]:
        item.close()
    closing = [halo, total_a, total_c]
    attend(1)
    for index, target in enumerate((k.keys, k.values)):
        target[:WINDOW] = halo.take(index)
    total_a.swap(1)
    attend(0)
    total_a.swap(0)
    attend(2)
    total_a.swap(2)
    total_b = Total(group, k.keep, k.totals[1])
    closing.append(total_b)
    k.window_turned[...] = k.window_low[...].T
    k.store(k.after)
    k.store(k.normed_three)
    k.store(k.window_turned)

    gain = k.gains[3:4]
    share = Share(group, k.normed_four, k.share_sems.at[2], group.own_chunks)
    closing.append(share)

    def enter_turn(chunk, total):
        middle = k.after[chunk : chunk + 1] + total
        k.middle_two[chunk : chunk + 1] = middle
        return norm_apply(middle, gain)

    def mlp_two(chunk):
        normed = flat(k.normed_four[chunk])
        gate = through(normed, k.w_gate_two()[...])
        up_val = through(normed, k.w_up_two()[...])
        d_gate, d_up = gate_backward(k.d_hidden[chunk], gate, up_val)
        d_gate, d_up = d_gate.astype(LOW), d_up.astype(LOW)
        back = plain(d_gate, k.w_gate_two()[...]) + plain(d_up, k.w_up_two()[...])
        k.gate_two[chunk] = gate
        k.up_two[chunk] = up_val
        k.d_gate_low[chunk] = d_gate
        k.d_up_low[chunk] = d_up
        return back

    order = [3, 1, 0, 2]
    relay(total_a, total_b, share, enter_turn, mlp_two, order=order)
    begun = []
    if k.scatter:
        begun = [
            Scatter(line, product(left, right), order, [k.gives[i]], [k.begun[i]], [k.give_sems.at[i]])
            for i, (left, right, order) in enumerate(
                ((k.normed_four, k.d_gate_two, X_FIRST), (k.normed_four, k.d_up_two, Z_FIRST))
            )
        ]
    spans = [slice(chunk * BLOCK, (chunk + 1) * BLOCK) for chunk in range(CHUNKS)]
    for chunk in range(CHUNKS):
        k.d_gate_two[:, spans[chunk]] = k.d_gate_low[chunk].T
    for item in begun[:1]:
        item.start(0)
    for chunk in range(CHUNKS):
        k.d_up_two[:, spans[chunk]] = k.d_up_low[chunk].T
    for item in begun[1:]:
        item.start(0)
    for chunk in range(CHUNKS):
        hidden = gate_forward(k.gate_two[chunk], k.up_two[chunk]).astype(LOW)
        k.hidden[chunk] = hidden
        k.hidden_two[:, spans[chunk]] = hidden.T
    for chunk in range(0, CHUNKS, 2):
        total_c.give(chunk, plain(flat(k.hidden[chunk : chunk + 2]), k.w_down_two()[...]), 2)
    total_c.swap_half()
    for item in (k.normed_four, k.hidden_two, k.d_gate_two, k.d_up_two):
        k.store(item)

    share = Share(group, k.grad_three, k.share_sems.at[3], group.own_rows)
    closing.append(share)
    k.gain_grad[...] = jnp.zeros_like(k.gain_grad)
    k.d_keys[...] = jnp.zeros_like(k.d_keys)
    k.d_values[...] = jnp.zeros_like(k.d_values)
    for step in range(CHUNKS + 1):
        if step < CHUNKS:
            chunk = order[step]
            d_values, d_gain = norm_back(total_b.take(chunk)[0], k.middle_two[chunk], gain)
            grad = k.cot[chunk, pl.ds(group.low, 1)].astype(FULL) + d_values[None]
            k.grad[chunk : chunk + 1] = grad
            k.gain_grad[...] += group.mine(chunk) * d_gain
            share.give(chunk, grad.astype(LOW))
        if step > 0:
            chunk = order[step - 1]
            share.await_other(chunk)
            put_rows(k.d_window, chunk, through(chunk_rows(k.grad_three, chunk), k.w_out_two()[...]).astype(LOW))
        if step == 3:
            window_backward(k, line, 0)
            halo = Halo(k, 1, (k.d_keys, k.d_values), slice(0, WINDOW), line.before)
            closing.append(halo)
            window_backward(k, line, 1)
    k.store(k.grad)
    k.store(k.grad_three)
    window_backward(k, line, 2)
    window_backward(k, line, 3)
    k.store(k.d_query2)
    k.result[...] = (flat(k.middle_two[pl.ds(2 * group.high, 2)]) + flat(total_c.take_half())).astype(LOW)
    for index, (target, out) in enumerate(((k.d_keys, k.d_key2), (k.d_values, k.d_value2))):
        target[rows : rows + WINDOW] += halo.take(index).astype(FULL)
        whole = target[WINDOW:]
        out[...] = whole.astype(LOW)
        k.store(out)
        k.d_turned2[(index + 1) * cols : (index + 2) * cols] = whole.T.astype(LOW)
    k.store(k.d_turned2)
    for item in begun:
        item.arrive(0)
        item.sent()
    for item in closing:
        item.close()
    for copy in [far, far_cot] + copies:
        copy.wait_send()
    taylor.close(True)


class Halo:
    def __init__(self, k, turn, sources, rows, peer):
        self.into = k.halo_in.at[turn]
        self.copies = []
        for index, source in enumerate(sources):
            k.halo_out[turn, index] = source[rows].astype(LOW)
            self.copies.append(
                send(
                    k.halo_out.at[turn, index],
                    k.halo_in.at[turn, index],
                    k.halo_sems.at[0, turn, index],
                    k.halo_sems.at[1, turn, index],
                    peer,
                )
            )

    def take(self, index):
        self.copies[index].wait_recv()
        return self.into[index]

    def close(self):
        for copy in self.copies:
            copy.wait_send()


def second_kernel(k, size):
    group, line = Group(), Line(size)
    meet = greet([group.pair, group.partner], line)
    width = k.gains.shape[1]
    total_a, total_b = (Total(group, k.keep, k.totals[i]) for i in range(2))
    share_mlp = Share(group, k.grad_two, k.share_sems.at[0], group.own_chunks)
    share = Share(group, k.grad_one, k.share_sems.at[1], group.own_rows)
    taylor = Taylor(line, k, k.query(), k.key(), k.value())
    background = list(PLAN)
    sums = {}

    def tick():
        if k.scatter:
            for name, level in background.pop(0):
                act(name, level)

    def normed_rows(chunk):
        return (
            through(chunk_rows(k.d_query2(), chunk, 2), k.w_query_two()[...])
            + through(chunk_rows(k.d_key2(), chunk, 2), k.w_key_two()[...])
            + through(chunk_rows(k.d_value2(), chunk, 2), k.w_value_two()[...])
        )

    def back(chunk, total, values, gain, row):
        d_values, d_gain = norm_back(flat(total), flat(values[chunk : chunk + 2]), gain)
        k.gain_rows[row : row + 1] += group.mine(chunk) * d_gain
        return d_values.reshape(2, HALF, width)

    def enter_mlp(chunk, total):
        grad = k.grad()[chunk : chunk + 2] + back(chunk, total, k.after(), k.gains[2:3], 2)
        k.grad()[chunk : chunk + 2] = grad
        return grad.astype(LOW)

    def mlp(chunk):
        d_hidden = through(flat(k.grad_two[chunk : chunk + 2]), k.w_down_one()[...])
        gate = flat(k.gate()[chunk : chunk + 2]).astype(FULL)
        up_val = flat(k.up()[chunk : chunk + 2]).astype(FULL)
        d_gate, d_up = gate_backward(d_hidden, gate, up_val)
        columns = slice(chunk * BLOCK, (chunk + 2) * BLOCK)
        k.d_gate_one[:, columns] = d_gate.T.astype(LOW)
        k.d_up_one[:, columns] = d_up.T.astype(LOW)
        return plain(d_gate.astype(LOW), k.w_gate_one()[...]) + plain(d_up.astype(LOW), k.w_up_one()[...])

    if k.scatter:
        pieces = [
            (k.normed_four, k.d_gate_two),
            (k.normed_four, k.d_up_two),
            (k.cot, k.hidden_two),
            (k.grad_three, k.window_turned),
            (k.normed_three, k.d_turned2),
            (k.normed_two, k.d_gate_one),
            (k.normed_two, k.d_up_one),
            (k.grad_two, k.hidden_one),
            (k.normed_one, k.d_turned),
            (k.grad_one, k.mixed_turned),
        ]
        sources = [product(left, right) for left, right in pieces]
        sources.append((lambda: None, lambda block: k.gain_rows[:, columns_of(block)]))
        begun = {0: 0, 1: 1}
        before = {5: 0, 6: 2, 7: 1}

        gain_copies = []

        def gain_step(step):
            if step:
                gain_copies[-1].wait_recv()
                k.gain_sum[step] = k.gain_sum[step - 1] + k.gain_in_sum[step - 1]
            else:
                k.gain_sum[0] = sums[10].finish()
            if step < 2:
                signals = k.gain_sems.at[0, step], k.gain_sems.at[1, step]
                peer = (group.pair, group.partner)[step]
                gain_copies.append(send(k.gain_sum.at[step], k.gain_in_sum.at[step], *signals, peer))
                return
            share_of = BLOCK // 4
            found = jnp.zeros((8, share_of), FULL)
            for index in range(4):
                part = k.gain_sum[2][:, index * share_of : (index + 1) * share_of]
                found = found + jnp.where(group.index == index, 1.0, 0.0) * part
            k.gain_out[...] = found

        def sum_of(name):
            if name not in sums:
                got = list(k.gots[name])
                if name in begun:
                    got[0] = k.begun[begun[name]]()
                if name in before:
                    sums[before[name]].sent()
                sems = [sem.at[name] for sem in k.sems]
                give = k.gives[before.get(name, name)]
                order = ORDERS[name]
                sums[name] = Scatter(line, sources[name], order, give, got, sems, 1 if name in begun else 0)
            return sums[name]

        def act(name, level):
            if name == 11:
                return gain_step(level)
            sum_of(name)
            if level < len(ORDERS[name]):
                sums[name].start(level)
            else:
                k.sums[name][...] = sums[name].finish()
                k.store(k.sums[name])

    k.gain_rows[...] = jnp.zeros_like(k.gain_rows)
    k.gain_rows[3:4] = k.gain_in[...]
    if k.scatter:
        name, _ = background[0][0]
        for index in sum_of(name).places(0):
            sums[name].prepare(0, index)
        meet()
        sums[name].start(0, prepared=True)
        background[0] = background[0][1:]
    else:
        meet()
    for chunk in range(0, CHUNKS, 2):
        total_a.give(chunk, normed_rows(chunk), 2, by_rows=True)
    for chunk in range(0, CHUNKS, 2):
        total_a.swap(chunk, 2)
    tick()
    relay(total_a, total_b, share_mlp, enter_mlp, mlp, 2, between=tick)
    for step in range(3):
        if step < 2:
            chunk = 2 * step
            grad = k.grad()[chunk : chunk + 2] + back(chunk, total_b.take(chunk, 2), k.middle(), k.gains[1:2], 1)
            k.grad()[chunk : chunk + 2] = grad
            share.give(chunk, grad.astype(LOW), 2)
        if step > 0:
            chunk = 2 * step - 2
            share.await_other(chunk)
            rows = through(chunk_rows(k.grad_one, chunk, 2), k.w_out_one()[...])
            k.d_mixed[chunk * BLOCK : (chunk + 2) * BLOCK] = rows.astype(LOW)
        tick()

    total_a.close()
    total_c = Total(group, k.keep, k.totals[0])
    k.mixed, k.inverse, k.carry = k.mixed(), k.inverse(), k.carry()
    for _ in taylor.backward(k.d_mixed):
        tick()
    d_query = 0.5 * k.d_query_acc[...]
    d_key = 0.5 * k.d_key_acc[...]
    d_value = k.d_value_acc[...]
    small, cols = d_query.shape[1], d_value.shape[1]
    k.d_query_low[...] = d_query.astype(LOW)
    k.d_key_low[...] = d_key.astype(LOW)
    k.d_value_low[...] = d_value.astype(LOW)
    k.d_turned[:small] = d_query.T.astype(LOW)
    k.d_turned[small : 2 * small] = d_key.T.astype(LOW)
    k.d_turned[2 * small : 2 * small + cols] = d_value.T.astype(LOW)
    for chunk in range(0, CHUNKS, 2):
        part = (
            plain(chunk_rows(k.d_query_low, chunk, 2), k.w_query_one()[...])
            + plain(chunk_rows(k.d_key_low, chunk, 2), k.w_key_one()[...])
            + through(chunk_rows(k.d_value_low, chunk, 2), k.w_value_one()[...])
        )
        total_c.give(chunk, part, 2, by_rows=True)
    total_c.swap_half()
    tick()
    half = pl.ds(2 * group.high, 2)
    d_values, d_gain = norm_back(flat(total_c.take_half()), flat(k.start()[half]), k.gains[0:1])
    k.input_grad[...] = flat(k.grad()[half]) + d_values
    k.gain_rows[0:1] = d_gain

    tick()
    if k.scatter:
        while background:
            tick()
        for name in set(sums) - set(before.values()):
            sums[name].sent()
        for copy in gain_copies:
            copy.wait_send()
    else:
        for item in (k.d_gate_one, k.d_up_one, k.d_turned, k.grad_one, k.grad_two):
            k.store(item)
        k.gain_out[...] = k.gain_rows[...]
    for item in (total_b, total_c, share_mlp, share):
        item.close()
    taylor.close(False)


def finish_kernel(k, small, cols):
    k.result[...] = k.result_in[...]
    k.input_grad[...] = k.input_grad_in[...]
    k.gains[...] = k.gains_in[0:4]
    for source, target in zip(k.sums, k.same):
        target[...] = source[...]
    for source, targets in zip(k.threes, k.turned):
        first = 0
        for target in targets:
            if target.shape[1] == BLOCK:
                target[...] = source[first : first + target.shape[0]]
                first += target.shape[0]
            else:
                target[...] = source[first : first + target.shape[1]].T
                first += target.shape[1]


def run_kernel(kernel, ident, ins, outs, scratch, flops, later=None, saved=None, apart=None, scalars=None, extra=None):
    later, saved, apart, scalars = (found or {} for found in (later, saved, apart, scalars))
    is_shape = lambda leaf: isinstance(leaf, tuple) and isinstance(leaf[0], tuple)

    def buffer(array):
        return pltpu.VMEM(array.shape, array.dtype)

    def held(tree):
        return jax.tree.map(lambda leaf: pltpu.VMEM(*leaf), tree, is_leaf=is_shape)

    def sems(tree):
        return jax.tree.map(lambda leaf: pltpu.SemaphoreType.DMA(()), tree, is_leaf=is_shape)

    arguments = (ins, later, scalars)
    results = (outs, saved, apart)
    own = (
        scratch,
        jax.tree.map(buffer, later),
        jax.tree.map(lambda leaf: pltpu.SemaphoreType.DMA(()), later),
        held(saved),
        sems(saved),
    )
    flat_in, tree_in = jax.tree.flatten(arguments)
    flat_out, tree_out = jax.tree.flatten(results, is_leaf=is_shape)
    flat_own, tree_own = jax.tree.flatten(own)

    def body(*refs):
        in_refs = jax.tree.unflatten(tree_in, refs[: len(flat_in)])
        out_refs = jax.tree.unflatten(tree_out, refs[len(flat_in) : len(flat_in) + len(flat_out)])
        own_refs = jax.tree.unflatten(tree_own, refs[len(flat_in) + len(flat_out) :])
        k = types.SimpleNamespace(**(extra or {}))
        for tree in (in_refs[0], in_refs[2], out_refs[0], out_refs[2], own_refs[0], own_refs[3]):
            k.__dict__.update(tree)
        waited = []
        for name in later:
            source = in_refs[1][name]
            parts = zip(*(jax.tree.leaves(tree) for tree in (source, own_refs[1][name], own_refs[2][name])))
            found = [Later(*part) for part in parts]
            waited += found
            setattr(k, name, found if isinstance(source, list) else found[0])
        saves = []
        for name in saved:
            parts = zip(*(jax.tree.leaves(tree[name]) for tree in (own_refs[3], out_refs[1], own_refs[4])))
            saves += [Saved(*part) for part in parts]

        def store(ref):
            for item in saves:
                if item.ref is ref:
                    item.store()

        k.store = store
        kernel(k)
        for item in waited:
            item()
        for item in saves:
            if item.copy is None:
                item.store()
        for item in saves:
            item.copy.wait()

    shapes = [jax.ShapeDtypeStruct(*leaf) for leaf in flat_out]
    moved = sum(a.size * a.dtype.itemsize for a in flat_in) + sum(
        math.prod(a.shape) * a.dtype.itemsize for a in shapes
    )
    there = pl.BlockSpec(memory_space=pl.ANY)
    here = pl.BlockSpec(memory_space=pltpu.VMEM)
    scalar = pl.BlockSpec(memory_space=pltpu.SMEM)

    def places(trees, kinds):
        return [kind for tree, kind in zip(trees, kinds) for _ in jax.tree.leaves(tree, is_leaf=is_shape)]

    found = pl.pallas_call(
        body,
        out_shape=shapes,
        in_specs=places(arguments, (here, there, scalar)),
        out_specs=places(results, (here, there, there)),
        scratch_shapes=flat_own,
        cost_estimate=pl.CostEstimate(flops=flops, bytes_accessed=moved, transcendentals=0),
        compiler_params=pltpu.CompilerParams(
            collective_id=ident, has_side_effects=ident is not None, vmem_limit_bytes=VMEM_BYTES
        ),
    )(*flat_in)
    found = jax.tree.unflatten(tree_out, found)
    return types.SimpleNamespace(**found[0], **found[1], **found[2])


def halve(array, axis):
    size = lax.axis_size(axis)
    index = lax.axis_index(axis)
    pieces = array.reshape((size, array.shape[0] // size) + array.shape[1:])
    distance = 1
    while distance < size:
        bit = (index // distance) % 2
        pairs = pieces.reshape((pieces.shape[0] // 2, 2) + pieces.shape[1:])
        keep = lax.dynamic_index_in_dim(pairs, bit, axis=1, keepdims=False)
        give = lax.dynamic_index_in_dim(pairs, 1 - bit, axis=1, keepdims=False)
        got = lax.ppermute(give, axis, [(i, i ^ distance) for i in range(size)])
        pieces = (keep.astype(FULL) + got.astype(FULL)).astype(array.dtype)
        distance *= 2
    return pieces[0]


def scatter_plain(left, right):
    return halve(inner(flat(left), right.T).astype(LOW), "seq").astype(FULL).T


def scatter_gains(gains):
    count = lax.axis_size("tensor")
    n_seq = lax.axis_size("seq")
    shaped = gains.reshape(4, n_seq, -1).transpose(1, 0, 2)
    mine = halve(shaped, "seq")[0]
    distance = 1
    while distance < count:
        mine = mine + lax.ppermute(mine, "tensor", [(i, i ^ distance) for i in range(count)])
        distance *= 2
    width = mine.shape[-1] // count
    return lax.dynamic_slice_in_dim(mine, lax.axis_index("tensor") * width, width, 1)


def on_device(
    inputs,
    cotangent,
    seq_lengths,
    norm_gains,
    query_one,
    key_one,
    value_one,
    out_one,
    gate_one,
    up_one,
    down_one,
    query_two,
    key_two,
    value_two,
    out_two,
    gate_two,
    up_two,
    down_two,
):
    rows, width = inputs.shape
    size = lax.axis_size("seq")
    stretch = 4 * rows
    units = gate_one.shape[1]
    cols = value_one.shape[1]
    small = query_one.shape[1]
    scatter = width // size == BLOCK
    count = int(math.log2(size))
    wide = ((4, 2, HALF, width), LOW)
    own = ((CHUNKS, HALF, width), FULL)
    heads = ((stretch, cols), LOW)
    heads_full = ((stretch, cols), FULL)
    narrow = ((stretch, small), LOW)
    unit_rows = ((CHUNKS, 2, HALF, units), LOW)
    turned_units = ((units, stretch), LOW)
    turned_cols = ((cols, stretch), LOW)
    state = ((FEATS + NORM_ROWS, cols), FULL)
    padded = ((stretch + WINDOW, cols), LOW)
    one_flops = 2 * stretch * width
    blocks = functools.partial(Scatter.blocks, size)
    choice, feature_rows = feature_tables()
    tables = dict(feature_choice=choice, feature_rows=feature_rows)
    tensor_sums = dict(
        keep=pltpu.VMEM(*own),
        share_sems=pltpu.SemaphoreType.DMA((4, 2, CHUNKS)),
    )
    got = ((size // 2, units, BLOCK), LOW)
    ahead = run_kernel(
        functools.partial(first_kernel, size=size),
        0,
        dict(
            gains=norm_gains,
            inputs=inputs,
            cotangent=cotangent,
            w_query_one=query_one.T,
            w_key_one=key_one.T,
            w_value_one=value_one,
            **tables,
        ),
        dict(result=((rows, width), LOW), gain_grad=((1, width), FULL)),
        dict(
            **tensor_sums,
            **Taylor.scratch(size, cols),
            totals=[Total.scratch(width) for _ in range(3)],
            rows_in=pltpu.VMEM((rows, width), LOW),
            cot_in=pltpu.VMEM((rows, width), LOW),
            near_sems=pltpu.SemaphoreType.DMA((2, 4)),
            far_sems=pltpu.SemaphoreType.DMA((2, 2)),
            mixed_low=pltpu.VMEM(*heads),
            query_feats=pltpu.VMEM((cols // HEAD, stretch, FEATS), LOW),
            query2=pltpu.VMEM(*heads),
            keys=pltpu.VMEM(*padded),
            values=pltpu.VMEM(*padded),
            window_low=pltpu.VMEM(*heads),
            d_window=pltpu.VMEM(*heads),
            d_keys=pltpu.VMEM(padded[0], FULL),
            d_values=pltpu.VMEM(padded[0], FULL),
            middle_two=pltpu.VMEM(*own),
            hidden=pltpu.VMEM((CHUNKS, 2 * HALF, units), LOW),
            d_hidden=pltpu.VMEM((CHUNKS, 2 * HALF, units), FULL),
            gate_two=pltpu.VMEM((CHUNKS, 2 * HALF, units), FULL),
            up_two=pltpu.VMEM((CHUNKS, 2 * HALF, units), FULL),
            d_gate_low=pltpu.VMEM((CHUNKS, 2 * HALF, units), LOW),
            d_up_low=pltpu.VMEM((CHUNKS, 2 * HALF, units), LOW),
            halo_out=pltpu.VMEM((2, 2, WINDOW, cols), LOW),
            halo_in=pltpu.VMEM((2, 2, WINDOW, cols), LOW),
            halo_sems=pltpu.SemaphoreType.DMA((2, 2, 2)),
            gives=[pltpu.VMEM(*got), pltpu.VMEM(*got)],
            give_sems=pltpu.SemaphoreType.DMA((2, 2, size // 2)),
        ),
        one_flops * (8 * cols + 9 * units),
        later=dict(
            w_out_one=out_one,
            w_gate_one=gate_one.T,
            w_up_one=up_one.T,
            w_down_one=down_one,
            w_key_two=key_two,
            w_value_two=value_two,
            w_query_two=query_two,
            w_out_two=out_two,
            w_gate_two=gate_two.T,
            w_up_two=up_two.T,
            w_down_two=down_two,
        ),
        saved=dict(
            start=own,
            middle=own,
            after=own,
            grad=own,
            normed_one=wide,
            normed_two=wide,
            normed_three=wide,
            normed_four=wide,
            cot=wide,
            grad_three=wide,
            query=narrow,
            key=narrow,
            value=heads,
            mixed=heads_full,
            inverse=heads_full,
            mixed_turned=turned_cols,
            carry=state,
            gate=unit_rows,
            up=unit_rows,
            hidden_one=turned_units,
            hidden_two=turned_units,
            d_gate_two=turned_units,
            d_up_two=turned_units,
            window_turned=turned_cols,
            d_query2=heads,
            d_key2=heads,
            d_value2=heads,
            d_turned2=((3 * cols, stretch), LOW),
        ),
        apart=dict(begun=[got, got]) if scatter else None,
        scalars=dict(lengths=seq_lengths),
        extra=dict(scatter=scatter),
    )
    widths = [units, units, units, cols, 3 * cols, units, units, units, 2 * small + cols, cols]
    carried = dict(
        d_query2=ahead.d_query2,
        d_key2=ahead.d_key2,
        d_value2=ahead.d_value2,
        w_query_two=query_two,
        w_key_two=key_two,
        w_value_two=value_two,
    )
    summed = dict(
        normed_four=ahead.normed_four,
        d_up_two=ahead.d_up_two,
        d_gate_two=ahead.d_gate_two,
        cot=ahead.cot,
        hidden_two=ahead.hidden_two,
        grad_three=ahead.grad_three,
        window_turned=ahead.window_turned,
        normed_three=ahead.normed_three,
        d_turned2=ahead.d_turned2,
        normed_two=ahead.normed_two,
        hidden_one=ahead.hidden_one,
        normed_one=ahead.normed_one,
        mixed_turned=ahead.mixed_turned,
    )
    chain = dict(
        after=ahead.after,
        grad=ahead.grad,
        w_down_one=down_one,
        gate=ahead.gate,
        up=ahead.up,
        w_gate_one=gate_one.T,
        w_up_one=up_one.T,
        middle=ahead.middle,
        w_out_one=out_one,
        query=ahead.query,
        key=ahead.key,
        value=ahead.value,
        mixed=ahead.mixed,
        inverse=ahead.inverse,
        carry=ahead.carry,
        w_query_one=query_one.T,
        w_key_one=key_one.T,
        w_value_one=value_one,
        start=ahead.start,
    )
    early = ("normed_three", "d_turned2", "normed_four", "d_up_two", "d_gate_two", "cot", "hidden_two")
    made = dict(
        d_gate_one=turned_units,
        d_up_one=turned_units,
        d_turned=((2 * small + cols, stretch), LOW),
        grad_two=wide,
        grad_one=wide,
    )
    if scatter:
        gain_blocks = [pltpu.VMEM((size >> (at + 1), 8, BLOCK), FULL) for at in range(count)]
        buffers = dict(
            gives=[[] if name in (5, 6, 7) else blocks(wide_) for name, wide_ in enumerate(widths)] + [gain_blocks],
            gots=[blocks(wide_) for wide_ in widths] + [gain_blocks],
            sems=[pltpu.SemaphoreType.DMA((11, 2, size >> (at + 1))) for at in range(count)],
            gain_sum=pltpu.VMEM((3, 8, BLOCK), FULL),
            gain_in_sum=pltpu.VMEM((2, 8, BLOCK), FULL),
            gain_sems=pltpu.SemaphoreType.DMA((2, 2)),
            **{name: pltpu.VMEM(*leaf) for name, leaf in made.items()},
        )
        for name in (0, 1):
            buffers["gots"][name][0] = None
        inputs_later = dict(
            **{name: summed[name] for name in early[:2]},
            **carried,
            **{name: summed[name] for name in early[2:]},
            begun=ahead.begun,
            **chain,
            **{name: array for name, array in summed.items() if name not in early},
        )
        kept = dict(sums=[((wide_, BLOCK), FULL) for wide_ in widths])
    else:
        buffers = {}
        inputs_later = dict(**carried, **chain)
        kept = made
    behind = run_kernel(
        functools.partial(second_kernel, size=size),
        1,
        dict(gains=norm_gains, gain_in=ahead.gain_grad, **tables),
        dict(input_grad=((rows, width), FULL), gain_out=((8, BLOCK // 4 if scatter else width), FULL)),
        dict(
            **tensor_sums,
            **Taylor.scratch(size, cols),
            totals=[Total.scratch(width) for _ in range(2)],
            d_mixed=pltpu.VMEM(*heads),
            gain_rows=pltpu.VMEM((8, width), FULL),
            grad_carry=pltpu.VMEM(*state),
            d_query_acc=pltpu.VMEM((stretch, small), FULL),
            d_key_acc=pltpu.VMEM((stretch, small), FULL),
            d_value_acc=pltpu.VMEM((stretch, cols), FULL),
            d_query_low=pltpu.VMEM(*narrow),
            d_key_low=pltpu.VMEM(*narrow),
            d_value_low=pltpu.VMEM(*heads),
            **buffers,
        ),
        one_flops * (6 * cols + 9 * units),
        later=inputs_later,
        saved=kept,
        scalars=dict(lengths=seq_lengths),
        extra=dict(scatter=scatter),
    )
    if not scatter:
        sums = [
            scatter_plain(left, right)
            for left, right in (
                (ahead.normed_four, ahead.d_gate_two),
                (ahead.normed_four, ahead.d_up_two),
                (ahead.cot, ahead.hidden_two),
                (ahead.grad_three, ahead.window_turned),
                (ahead.normed_three, ahead.d_turned2),
                (ahead.normed_two, behind.d_gate_one),
                (ahead.normed_two, behind.d_up_one),
                (behind.grad_two, ahead.hidden_one),
                (ahead.normed_one, behind.d_turned),
                (behind.grad_one, ahead.mixed_turned),
            )
        ]
        gains = scatter_gains(behind.gain_out[:4])
        three_one, three_two = sums[8], sums[4]
        return (
            (ahead.result, behind.input_grad, gains)
            + (three_one[:small].T, three_one[small : 2 * small].T, three_one[2 * small :].T)
            + (sums[9], sums[5].T, sums[6].T, sums[7])
            + tuple(three_two[first : first + cols].T for first in range(0, 3 * cols, cols))
            + (sums[3], sums[0].T, sums[1].T, sums[2])
        )
    block = ((BLOCK, cols), FULL)
    unit = ((units, BLOCK), FULL)
    done = run_kernel(
        functools.partial(finish_kernel, small=small, cols=cols),
        None,
        dict(
            result_in=ahead.result,
            input_grad_in=behind.input_grad,
            gains_in=behind.gain_out,
            sums=[behind.sums[name] for name in (0, 1, 2, 3, 5, 6, 7, 9)],
            threes=[behind.sums[8], behind.sums[4]],
        ),
        dict(
            result=((rows, width), LOW),
            input_grad=((rows, width), FULL),
            gains=((4, BLOCK // 4), FULL),
            same=[unit, unit, unit, ((cols, BLOCK), FULL), unit, unit, unit, ((cols, BLOCK), FULL)],
            turned=[[((small, BLOCK), FULL), ((small, BLOCK), FULL), block], [block, block, block]],
        ),
        {},
        stretch,
    )
    same, turned = done.same, done.turned
    return (
        (done.result, done.input_grad, done.gains)
        + (turned[0][0].T, turned[0][1].T, turned[0][2])
        + (same[7], same[4].T, same[5].T, same[6])
        + tuple(turned[1])
        + (same[3], same[0].T, same[1].T, same[2])
    )


def solution(mesh):
    both = P(("seq", "tensor"), None)
    split = P(None, "tensor")
    stacked = P("tensor", None)
    columns_out = P("seq", "tensor")
    rows_out = P("tensor", "seq")
    layer_in = (split, split, split, stacked, split, split, stacked)
    layer_out = (columns_out, columns_out, columns_out, rows_out, columns_out, columns_out, rows_out)
    return jax.shard_map(
        on_device,
        mesh=mesh,
        in_specs=(both, both, P(), P()) + layer_in + layer_in,
        out_specs=(both, both, P(None, ("seq", "tensor"))) + layer_out + layer_out,
        check_vma=False,
    )
```

```python
import functools
import math
import types

import jax
import jax.numpy as jnp
import numpy as np
from jax import lax
from jax.experimental import pallas as pl
from jax.experimental.pallas import tpu as pltpu
from jax.sharding import PartitionSpec as P

FEAT = 16
HEAD = 64
WINDOW = 64
BLOCK = 128
EPS = 1e-05
FLOOR_SCORE = -1e30
MESH = pl.DeviceIdType.MESH
LOW = jnp.bfloat16
FULL = jnp.float32
VMEM_BYTES = 60 * 1024 * 1024
HALF = BLOCK // 2
CHUNKS = 4
PAIRS = [(a, b) for a in range(FEAT + 1) for b in range(a, FEAT + 1)]
FEATS = -(-len(PAIRS) // 16) * 16
NORM_ROWS = 16


def plain(left, right):
    return jnp.dot(left, right, preferred_element_type=FULL)


def inner(left, right):
    return lax.dot_general(left, right, (((0,), (0,)), ((), ())), preferred_element_type=FULL)


def through(left, right):
    return lax.dot_general(left, right, (((1,), (1,)), ((), ())), preferred_element_type=FULL)


def flat(array):
    return array.reshape((math.prod(array.shape[:-1]), array.shape[-1]))


class Group:
    def __init__(self):
        index = lax.axis_index("tensor")
        self.index = index
        self.low = lax.rem(index, 2)
        self.high = index // 2
        self.pair = dict(tensor=index + 1 - 2 * self.low)
        self.partner = dict(tensor=lax.rem(index + 2, 4))

    def mine(self, chunk):
        return jnp.where(self.high == chunk // 2, 1.0, 0.0)

    def split(self, part, count, by_rows=False):
        if by_rows:
            zero, one = part.reshape(2, count, HALF, -1)
        else:
            whole = part.reshape(count, 2, HALF, -1)
            zero, one = whole[:, 0], whole[:, 1]
        even = self.low == 0
        return jnp.where(even, zero, one), jnp.where(even, one, zero)

    def own_rows(self, ref, chunk, count):
        return ref.at[self.low + 2 * (chunk // 2), pl.ds(chunk % 2, count)]

    def own_chunks(self, ref, chunk, count):
        return ref.at[pl.ds(chunk, count), self.low]


def chunk_rows(ref, chunk, count=1):
    first, half = 2 * (chunk // 2), chunk % 2
    if len(ref.shape) == 4:
        return flat(ref[first : first + 2, half : half + count])
    starts = [block * BLOCK + half * HALF for block in (first, first + 1)]
    return jnp.concatenate([ref[start : start + count * HALF] for start in starts], axis=0)


def put_rows(ref, chunk, value, ahead=0):
    for side in range(2):
        start = ahead + (2 * (chunk // 2) + side) * BLOCK + chunk % 2 * HALF
        ref[start : start + HALF] = value[side * HALF : (side + 1) * HALF]


class Line:
    def __init__(self, size):
        self.size = size
        self.index = lax.axis_index("seq")
        self.after = dict(seq=lax.rem(self.index + 1, size))
        self.before = dict(seq=lax.rem(self.index + size - 1, size))

    def flip(self, relative):
        found = 0
        bit = 1
        while bit < self.size:
            found = found + bit * lax.rem(self.index // bit + relative // bit, 2)
            bit *= 2
        return found


def greet(peers, everyone=None):
    barrier = pltpu.get_barrier_semaphore()
    for peer in peers:
        pl.semaphore_signal(barrier, inc=1, device_id=peer, device_id_type=MESH)
    count = len(peers)
    if everyone is not None:

        def call(step, carry):
            peer = dict(seq=lax.rem(everyone.index + step, everyone.size))
            pl.semaphore_signal(barrier, inc=1, device_id=peer, device_id_type=MESH)
            return carry

        lax.fori_loop(1, everyone.size, call, 0)
        count += everyone.size - 1
    return lambda: pl.semaphore_wait(barrier, count)


def remote(src, dst, send, recv, device):
    return pltpu.make_async_remote_copy(
        src_ref=src, dst_ref=dst, send_sem=send, recv_sem=recv, device_id=device, device_id_type=MESH
    )


def send(src, dst, send_sem, recv_sem, device):
    copy = remote(src, dst, send_sem, recv_sem, device)
    copy.start()
    return copy


class Total:
    def __init__(self, group, keep, buffers):
        self.group = group
        self.keep = keep
        self.pair_out, self.pair_in, self.out, self.into, self.sems = buffers
        self.pairs = {}
        self.fars = {}
        self.arriving = {}
        self.arrived = set()

    @staticmethod
    def scratch(width):
        return [pltpu.VMEM((CHUNKS, HALF, width), LOW)] * 4 + [pltpu.SemaphoreType.DMA((4, CHUNKS))]

    def give(self, chunk, part, count=1, by_rows=False):
        own, other = self.group.split(part, count, by_rows)
        place = pl.ds(chunk, count)
        self.keep[place] = own
        self.pair_out[place] = other.astype(LOW)
        self.pairs[chunk] = send(
            self.pair_out.at[place],
            self.pair_in.at[place],
            self.sems.at[0, chunk],
            self.sems.at[1, chunk],
            self.group.pair,
        )
        self.arriving.update({chunk + step: chunk for step in range(count)})

    def pair_sum(self, chunk, count=1):
        given = self.arriving[chunk]
        if given not in self.arrived:
            self.arrived.add(given)
            self.pairs[given].wait_recv()
        place = pl.ds(chunk, count)
        return self.keep[place] + self.pair_in[place].astype(FULL)

    def swap(self, chunk, count=1):
        place = pl.ds(chunk, count)
        self.out[place] = self.pair_sum(chunk, count).astype(LOW)
        self.fars[chunk] = send(
            self.out.at[place],
            self.into.at[place],
            self.sems.at[2, chunk],
            self.sems.at[3, chunk],
            self.group.partner,
        )

    def swap_half(self):
        for chunk in range(0, CHUNKS, 2):
            self.out[chunk : chunk + 2] = self.pair_sum(chunk, 2).astype(LOW)
        self.fars[0] = send(
            self.out.at[pl.ds(2 - 2 * self.group.high, 2)],
            self.into.at[pl.ds(0, 2)],
            self.sems.at[2, 0],
            self.sems.at[3, 0],
            self.group.partner,
        )

    def take(self, chunk, count=1):
        self.fars[chunk].wait_recv()
        place = pl.ds(chunk, count)
        return self.out[place].astype(FULL) + self.into[place].astype(FULL)

    def take_half(self):
        self.fars[0].wait_recv()
        return self.out[pl.ds(2 * self.group.high, 2)].astype(FULL) + self.into[0:2].astype(FULL)

    def close(self):
        for copy in list(self.pairs.values()) + list(self.fars.values()):
            copy.wait_send()


class Share:
    def __init__(self, group, full, sems, place):
        self.group = group
        self.full = full
        self.sems = sems
        self.place = place
        self.copies = {}

    def give(self, chunk, value, count=1):
        rows = self.place(self.full, chunk, count)
        rows[...] = value
        self.copies[chunk] = send(
            rows, rows, self.sems.at[0, chunk], self.sems.at[1, chunk], self.group.pair
        )

    def await_other(self, chunk):
        self.copies[chunk].wait_recv()

    def close(self):
        for copy in self.copies.values():
            copy.wait_send()


def share_sems():
    return pltpu.SemaphoreType.DMA((2, CHUNKS))


def relay(first, second, share, enter, work, count=1, order=None, between=lambda: None):
    starts = order or list(range(0, CHUNKS, count))
    for step in range(len(starts) + 1):
        if step < len(starts):
            share.give(starts[step], enter(starts[step], first.take(starts[step], count)), count)
        if step > 1:
            second.swap(starts[step - 2], count)
        if step > 0:
            chunk = starts[step - 1]
            share.await_other(chunk)
            second.give(chunk, work(chunk), count)
        between()
    second.swap(starts[-1], count)


class Later:
    def __init__(self, source, target, sem):
        self.copy = pltpu.make_async_copy(source, target, sem)
        self.copy.start()
        self.target = target
        self.waiting = True

    def __call__(self):
        if self.waiting:
            self.copy.wait()
            self.waiting = False
        return self.target


class Saved:
    def __init__(self, ref, target, sem):
        self.ref = ref
        self.target = target
        self.sem = sem
        self.copy = None

    def store(self):
        self.copy = pltpu.make_async_copy(self.ref, self.target, self.sem)
        self.copy.start()


class Scatter:
    def __init__(self, line, source, order, give, got, sems, begun=0):
        self.line = line
        self.ready, self.base = source
        self.order = order
        self.give = give
        self.got = got
        self.sems = sems
        self.begun = begun

    @staticmethod
    def blocks(size, width):
        return [pltpu.VMEM((size >> (at + 1), width, BLOCK), LOW) for at in range(int(math.log2(size)))]

    def copy(self, at, index):
        return remote(
            self.give[at].at[index],
            self.got[at].at[index],
            self.sems[at].at[0, index],
            self.sems[at].at[1, index],
            dict(seq=self.line.flip(self.order[at])),
        )

    def part(self, place, upto):
        relative = sum(bit for at, bit in enumerate(self.order) if place >> at & 1)
        total = self.base(self.line.flip(relative))
        for at in range(upto):
            index = place >> (at + 1)
            if at >= self.begun:
                self.copy(at, index).wait_recv()
            total = total + self.got[at][index].astype(FULL)
        return total

    def places(self, at):
        return sorted(range(self.line.size >> (at + 1)), key=lambda index: (index & -index) or self.line.size)

    def prepare(self, at, index):
        self.ready()
        self.give[at][index] = self.part(2**at * (2 * index + 1), at).astype(self.give[at].dtype)

    def start(self, at, prepared=False):
        for index in self.places(at):
            if not prepared:
                self.prepare(at, index)
            self.copy(at, index).start()

    def finish(self):
        return self.part(0, len(self.order))

    def arrive(self, at):
        for index in self.places(at):
            self.copy(at, index).wait_recv()

    def sent(self):
        for at in range(self.begun, len(self.sems)):
            for index in self.places(at):
                self.copy(at, index).wait_send()


def columns_of(block):
    return pl.ds(pl.multiple_of(block * BLOCK, BLOCK), BLOCK)


def product(left, right):
    def base(block):
        return plain(held(right)[...], flat(held(left)[:, :, :, columns_of(block)]))

    def ready():
        held(left)
        held(right)

    return ready, base


def held(item):
    return item() if isinstance(item, Later) else item


def norm_apply(values, gain):
    inverse = lax.rsqrt(jnp.mean(values * values, axis=-1, keepdims=True) + EPS)
    return (values * inverse * gain).astype(LOW)


def norm_back(grad, values, gain):
    inverse = lax.rsqrt(jnp.mean(values * values, axis=-1, keepdims=True) + EPS)
    scaled = values * inverse
    d_scaled = grad * gain
    d_values = inverse * (d_scaled - scaled * jnp.mean(d_scaled * scaled, axis=-1, keepdims=True))
    return d_values, jnp.sum(grad * scaled, axis=0, keepdims=True)


def gate_forward(gate, up_val):
    return gate * up_val / (1.0 + jnp.exp(-gate))


def gate_backward(d_hidden, gate, up_val):
    sigma = 1.0 / (1.0 + jnp.exp(-gate))
    return d_hidden * up_val * sigma * (1.0 + gate * (1.0 - sigma)), d_hidden * gate * sigma


def segment_of(lengths, positions):
    end = 0
    found = jnp.zeros_like(positions)
    for index in range(lengths.shape[0]):
        end = end + lengths[index]
        found = found + jnp.where(positions >= end, 1, 0)
    return found


def ramp(shape, axis, first):
    return lax.broadcasted_iota(jnp.int32, shape, axis) + first


def same(left, right):
    return jnp.where(left == right, 1.0, 0.0)


def feature_tables():
    choice = np.zeros((2, FEAT, FEATS), np.float32)
    rows = np.zeros((8, FEATS), np.float32)
    for index, pair in enumerate(PAIRS):
        for side, entry in enumerate(pair):
            if entry < FEAT:
                choice[side, entry, index] = 1.0
            else:
                rows[side, index] = 1.0
        rows[2, index] = 0.5**0.5 if pair[0] == pair[1] and pair[0] < FEAT else 1.0
    return jnp.asarray(choice, LOW), jnp.asarray(rows, FULL)


class Taylor:
    def __init__(self, line, k, query, key, value):
        self.line = line
        self.k = k
        self.query = query
        self.key = key
        self.value = value
        self.rows = query.shape[0]
        self.count = self.rows // BLOCK
        self.heads = value.shape[1] // HEAD
        start = line.index * self.rows
        self.start = start
        column = segment_of(k.lengths, ramp((self.rows, 1), 0, start))
        last = segment_of(k.lengths, ramp((1, 1), 0, start + self.rows - 1))
        before = segment_of(k.lengths, ramp((1, 1), 0, start - 1))
        self.last = last
        self.before = before
        self.segments = column
        self.across = segment_of(k.lengths, ramp((1, self.rows), 1, start))
        self.tail = same(column, last)
        self.carried = same(column, before)
        self.lane = ramp((1, self.heads * HEAD), 1, 0) // HEAD

    def half(self, array, head, upto=None, only=None):
        first, last = (0, upto or self.count) if only is None else (only, only + 1)
        return array[first * BLOCK : last * BLOCK, head * FEAT : (head + 1) * FEAT] * jnp.asarray(0.5, LOW)

    def factors(self, half):
        rows = self.k.feature_rows
        left = plain(half, self.k.feature_choice[0]) + rows[0:1]
        right = plain(half, self.k.feature_choice[1]) + rows[1:2]
        return left, right

    def features(self, array, head):
        left, right = self.factors(self.half(array, head))
        return left * right * self.k.feature_rows[2:3]

    def features_back(self, grad, array, head):
        left, right = self.factors(self.half(array, head))
        weighted = grad * self.k.feature_rows[2:3]
        return through((weighted * right).astype(LOW), self.k.feature_choice[0]) + through(
            (weighted * left).astype(LOW), self.k.feature_choice[1]
        )

    def of_head(self, head, array):
        return jnp.where(self.lane == head, array, jnp.zeros_like(array))

    def mask(self, block):
        upto = (block + 1) * BLOCK
        rows = ramp((BLOCK, 1), 0, block * BLOCK)
        allowed = (ramp((1, upto), 1, 0) <= rows) & (
            self.across[:, :upto] == self.segments[block * BLOCK : upto]
        )
        return jnp.where(allowed, 1.0, 0.0)

    def far_first(self, step, forward):
        return self.line.size - 1 - step if forward else step

    def send_state(self, forward):
        line = self.line

        def step(index, carry):
            other = self.far_first(index, forward)

            @pl.when((other > line.index) if forward else (other < line.index))
            def _():
                self.state_copy(other).start()

            return carry

        lax.fori_loop(0, line.size, step, 0)

    def state_copy(self, other):
        k = self.k
        return remote(
            k.state_own,
            k.state_slots.at[self.line.index],
            k.state_sems.at[0, other],
            k.state_sems.at[1, self.line.index],
            dict(seq=other),
        )

    def state_arrival(self, other):
        k = self.k
        return remote(
            k.state_own,
            k.state_slots.at[other],
            k.state_sems.at[0, other],
            k.state_sems.at[1, other],
            dict(seq=other),
        )

    def take_state(self, total, forward):
        k, line = self.k, self.line
        total[...] = jnp.zeros_like(total)

        def step(index, carry):
            other = self.far_first(index, forward)

            @pl.when((other < line.index) if forward else (other > line.index))
            def _():
                self.state_arrival(other).wait_recv()
                if forward:
                    edge = segment_of(k.lengths, ramp((1, 1), 0, (other + 1) * self.rows - 1))
                    weight = same(edge, self.before)
                else:
                    edge = segment_of(k.lengths, ramp((1, 1), 0, other * self.rows - 1))
                    weight = same(edge, self.last)
                total[...] += weight * k.state_slots[other].astype(FULL)

            return carry

        lax.fori_loop(0, line.size, step, 0)

    def close(self, forward):
        line = self.line

        def step(other, carry):
            @pl.when((other > line.index) if forward else (other < line.index))
            def _():
                self.state_copy(other).wait_send()

            return carry

        lax.fori_loop(0, line.size, step, 0)

    @staticmethod
    def scratch(size, cols):
        shape = (FEATS + NORM_ROWS, cols)
        return dict(
            state_own=pltpu.VMEM(shape, LOW),
            state_build=pltpu.VMEM(shape, FULL),
            state_slots=pltpu.VMEM((size,) + shape, LOW),
            state_sems=pltpu.SemaphoreType.DMA((2, size)),
        )

    def forward(self, meanwhile):
        k = self.k
        value = self.value[...]
        build = k.state_build
        build[...] = jnp.zeros_like(build)
        state = jnp.zeros((FEATS, value.shape[1]), FULL)
        for head in range(self.heads):
            feats = self.features(self.key, head) * self.tail
            state = state + self.of_head(head, inner(feats.astype(LOW), value))
            build[FEATS + head : FEATS + head + 1, :FEATS] = jnp.sum(feats, axis=0, keepdims=True)
        build[:FEATS] = state
        k.state_own[...] = build[...].astype(LOW)
        self.send_state(True)
        for block in range(self.count):
            allowed = self.mask(block)
            rows = slice(block * BLOCK, (block + 1) * BLOCK)
            for head in range(self.heads):
                places = slice(head * HEAD, (head + 1) * HEAD)
                score = through(self.half(self.query, head, only=block), self.half(self.key, head, block + 1))
                score = allowed * (1.0 + score + 0.5 * score * score)
                k.mixed[rows, places] = plain(score.astype(LOW), value[: (block + 1) * BLOCK, places])
                k.inverse[rows, places] = jnp.broadcast_to(jnp.sum(score, axis=1, keepdims=True), (BLOCK, HEAD))
        for head in range(self.heads):
            k.query_feats[head] = self.features(self.query, head).astype(LOW)
        meanwhile()
        self.take_state(k.carry, True)
        state = k.carry[:FEATS].astype(LOW)
        numerator = jnp.zeros((self.rows, value.shape[1]), FULL)
        totals = jnp.zeros((self.rows, value.shape[1]), FULL)
        for head in range(self.heads):
            feats = k.query_feats[head]
            numerator = numerator + self.of_head(head, plain(feats, state))
            norm = k.carry[FEATS + head : FEATS + head + 1, :FEATS]
            totals = totals + self.of_head(head, jnp.sum(feats * norm, axis=1, keepdims=True) + jnp.zeros_like(totals))
        inverse = 1.0 / (k.inverse[...] + self.carried * totals)
        mixed = (k.mixed[...] + self.carried * numerator) * inverse
        k.inverse[...] = inverse
        k.mixed[...] = mixed
        k.mixed_low[...] = mixed.astype(LOW)
        k.mixed_turned[...] = mixed.T.astype(LOW)

    def backward(self, d_mixed):
        k = self.k
        value = self.value[...]
        d_out = d_mixed[...].astype(FULL)
        d_numer = d_out * k.inverse[...]
        d_low = d_numer.astype(LOW)
        product = d_numer * k.mixed[...]
        d_totals = [
            -jnp.sum(product[:, head * HEAD : (head + 1) * HEAD], axis=1, keepdims=True) for head in range(self.heads)
        ]
        build = k.state_build
        build[...] = jnp.zeros_like(build)
        state = jnp.zeros((FEATS, value.shape[1]), FULL)
        for head in range(self.heads):
            feats = self.features(self.query, head) * self.carried
            state = state + self.of_head(head, inner(feats.astype(LOW), d_low))
            build[FEATS + head : FEATS + head + 1, :FEATS] = jnp.sum(feats * d_totals[head], axis=0, keepdims=True)
        build[:FEATS] = state
        k.state_own[...] = build[...].astype(LOW)
        self.send_state(False)
        yield
        carry = k.carry[:FEATS].astype(LOW)
        k.d_key_acc[...] = jnp.zeros_like(k.d_key_acc)
        k.d_value_acc[...] = jnp.zeros_like(k.d_value_acc)
        for head in range(self.heads):
            norm = k.carry[FEATS + head : FEATS + head + 1, :FEATS]
            d_feats = self.carried * (through(self.of_head(head, d_low), carry) + d_totals[head] * norm)
            k.d_query_acc[:, head * FEAT : (head + 1) * FEAT] = self.features_back(d_feats, self.query, head)
        for block in range(self.count):
            allowed = self.mask(block)
            upto = (block + 1) * BLOCK
            rows = slice(block * BLOCK, upto)
            for head in range(self.heads):
                places = slice(head * HEAD, (head + 1) * HEAD)
                narrow = slice(head * FEAT, (head + 1) * FEAT)
                query = self.half(self.query, head, only=block)
                key = self.half(self.key, head, block + 1)
                score = through(query, key)
                d_rows = d_low[rows, places]
                d_score = through(d_rows, value[:upto, places]) + d_totals[head][rows]
                d_score = (allowed * d_score * (1.0 + score)).astype(LOW)
                score = (allowed * (1.0 + score + 0.5 * score * score)).astype(LOW)
                k.d_query_acc[rows, narrow] += plain(d_score, key)
                k.d_key_acc[:upto, narrow] += inner(d_score, query)
                k.d_value_acc[:upto, places] += inner(score, d_rows)
            yield
        self.take_state(k.grad_carry, False)
        carry = k.grad_carry[:FEATS].astype(LOW)
        for head in range(self.heads):
            norm = k.grad_carry[FEATS + head : FEATS + head + 1, :FEATS]
            d_feats = self.tail * (through(self.of_head(head, value), carry) + norm)
            k.d_key_acc[:, head * FEAT : (head + 1) * FEAT] += self.features_back(d_feats, self.key, head)
            feats = self.features(self.key, head).astype(LOW)
            k.d_value_acc[...] += self.of_head(head, self.tail * plain(feats, carry))


def window_mask(k, line, first, count):
    start = line.index * k.query2.shape[0] + first
    query = ramp((count, 1), 0, start)
    key = ramp((1, count + WINDOW), 1, start - WINDOW)
    return (
        (key <= query)
        & (key > query - WINDOW)
        & (key >= 0)
        & (segment_of(k.lengths, key) == segment_of(k.lengths, query))
    )


def window_weights(query, key, allowed):
    score = jnp.where(allowed, through(query, key) * HEAD**-0.5, FLOOR_SCORE)
    weight = jnp.exp(score - jnp.max(score, axis=1, keepdims=True))
    return weight / jnp.sum(weight, axis=1, keepdims=True)


def window_forward(k, line, chunk):
    cols = k.keys.shape[1]
    heads = cols // HEAD
    lane = ramp((1, cols), 1, 0) // HEAD
    for side in range(2):
        first = (2 * (chunk // 2) + side) * BLOCK + chunk % 2 * HALF
        own = slice(first, first + HALF)
        span = slice(first, first + HALF + WINDOW)
        hidden = jnp.where(window_mask(k, line, first, HALF), 0.0, FLOOR_SCORE)
        query = k.query2[own]
        stack = jnp.concatenate([jnp.where(lane == head, query, jnp.zeros_like(query)) for head in range(heads)], axis=0)
        score = through(stack, k.keys[span]) * HEAD**-0.5 + jnp.concatenate([hidden] * heads, axis=0)
        weight = jnp.exp(score - jnp.max(score, axis=1, keepdims=True))
        weight = weight / jnp.sum(weight, axis=1, keepdims=True)
        found = plain(weight.astype(LOW), k.values[span])
        whole = jnp.zeros((HALF, cols), FULL)
        for head in range(heads):
            whole = whole + jnp.where(lane == head, found[head * HALF : (head + 1) * HALF], 0.0)
        k.window_low[own] = whole.astype(LOW)


def window_backward(k, line, block):
    own = slice(block * BLOCK, (block + 1) * BLOCK)
    allowed = window_mask(k, line, block * BLOCK, BLOCK)
    span = slice(block * BLOCK, (block + 1) * BLOCK + WINDOW)
    grads = []
    for head in range(k.keys.shape[1] // HEAD):
        places = slice(head * HEAD, (head + 1) * HEAD)
        query = k.query2[own, places]
        key = k.keys[span, places]
        d_out = k.d_window[own, places]
        weight = window_weights(query, key, allowed)
        d_weight = through(d_out, k.values[span, places])
        d_score = weight * (d_weight - jnp.sum(weight * d_weight, axis=1, keepdims=True)) * HEAD**-0.5
        d_score = d_score.astype(LOW)
        grads.append(plain(d_score, key))
        k.d_keys[span, places] += inner(d_score, query)
        k.d_values[span, places] += inner(weight.astype(LOW), d_out)
    whole = jnp.concatenate(grads, axis=1)
    k.d_query2[own] = whole.astype(LOW)
    k.d_turned2[: whole.shape[1], own] = whole.T.astype(LOW)


X_FIRST, Z_FIRST = (1, 2, 4), (2, 4, 1)
ORDERS = [X_FIRST, Z_FIRST, X_FIRST, X_FIRST, X_FIRST, X_FIRST, X_FIRST, X_FIRST, X_FIRST, X_FIRST, X_FIRST]
PLAN = [[(4, 0), (1, 1), (0, 1), (2, 0), (4, 1)], [(0, 2), (3, 0)], [], [(4, 2)], [(5, 0), (2, 1)], [], [(1, 2)], [], [(3, 1), (5, 1)], [(2, 2)], [(7, 0), (5, 2), (7, 1), (6, 0)], [], [(7, 2), (2, 3), (6, 1)], [(10, 0)], [(8, 0), (7, 3), (9, 0), (6, 2), (4, 3), (5, 3), (3, 2), (10, 1), (8, 1), (10, 2), (9, 1), (8, 2), (11, 0), (11, 1), (1, 3), (3, 3), (11, 2), (9, 2), (0, 3), (6, 3), (8, 3), (9, 3)]]


def first_kernel(k, size):
    group, line = Group(), Line(size)
    greet([group.pair, group.partner], line)()
    width = k.inputs.shape[1]
    rows = k.query.shape[0]
    cols = k.value.shape[1]
    total_a, total_b, total_c = (Total(group, k.keep, k.totals[i]) for i in range(3))
    closing = [total_a, total_b]

    def offer(step, block, raw):
        values = raw.astype(FULL)
        k.start[pl.ds(2 * (block // 2), 2)] = values.reshape(2, HALF, width)
        k.normed_one[block] = norm_apply(values, k.gains[0:1]).reshape(2, HALF, width)
        place = k.normed_one.at[block]
        copy = send(place, place, k.near_sems.at[0, step], k.near_sems.at[1, step], group.pair)
        copy.wait_recv()
        return copy

    def project_one(pair):
        normed = flat(k.normed_one[pl.ds(2 * pair, 2)])
        place = pl.ds(pl.multiple_of(pair * 2 * BLOCK, 2 * BLOCK), 2 * BLOCK)
        k.key[place] = through(normed, k.w_key_one[...]).astype(LOW)
        k.value[place] = plain(normed, k.w_value_one[...]).astype(LOW)
        k.query[place] = through(normed, k.w_query_one[...]).astype(LOW)

    def offer_cot(step, half, raw):
        place = k.cot.at[pl.ds(2 * half, 2), group.low]
        place[...] = raw.reshape(2, HALF, width)
        return send(place, place, k.near_sems.at[0, 2 + step], k.near_sems.at[1, 2 + step], group.pair)

    far = send(k.inputs, k.rows_in, k.far_sems.at[0, 0], k.far_sems.at[1, 0], group.partner)
    copies = [offer(0, group.index, k.inputs[...])]
    project_one(group.high)
    far.wait_recv()
    far_cot = send(k.cotangent, k.cot_in, k.far_sems.at[0, 1], k.far_sems.at[1, 1], group.partner)
    copies.append(offer(1, lax.rem(group.index + 2, 4), k.rows_in[...]))
    project_one(1 - group.high)
    copies.append(offer_cot(0, group.high, k.cotangent[...]))
    taylor = Taylor(line, k, k.query, k.key, k.value)

    def turn_ahead():
        for index, weight in enumerate((k.w_gate_one, k.w_gate_two, k.w_up_two)):
            k.turned[index] = weight()[...].T
        far_cot.wait_recv()
        copies.append(offer_cot(1, 1 - group.high, k.cot_in[...]))
        for copy in copies[2:]:
            copy.wait_recv()
        k.store(k.cot)
        for chunk in range(0, CHUNKS, 2):
            found = through(flat(k.cot[chunk : chunk + 2]), k.w_down_two()[...])
            k.d_hidden[chunk : chunk + 2] = found.reshape(2, 2 * HALF, -1)

    taylor.forward(turn_ahead)
    for item in (k.start, k.normed_one, k.query, k.key, k.value, k.mixed, k.inverse, k.mixed_turned, k.carry):
        k.store(item)

    share = Share(group, k.normed_two, k.share_sems.at[0], group.own_chunks)
    closing.append(share)

    def enter_mlp(chunk, total):
        middle = k.start[chunk : chunk + 1] + total
        k.middle[chunk : chunk + 1] = middle
        return norm_apply(middle, k.gains[1:2])

    def mlp_one(chunk):
        normed = flat(k.normed_two[chunk])
        gate = plain(normed, k.turned[0])
        up_val = through(normed, k.w_up_one()[...])
        k.gate[chunk] = gate.astype(LOW).reshape(k.gate.shape[1:])
        k.up[chunk] = up_val.astype(LOW).reshape(k.up.shape[1:])
        hidden = gate_forward(gate, up_val)
        k.hidden_one[:, chunk * BLOCK : (chunk + 1) * BLOCK] = hidden.T.astype(LOW)
        return plain(hidden.astype(LOW), k.w_down_one()[...])

    order = [2, 3, 0, 1]
    for chunk in (2, 0):
        part = plain(chunk_rows(k.mixed_low, chunk, 2), k.w_out_one()[...])
        total_a.give(chunk, part, 2, by_rows=True)
    for chunk in order:
        total_a.swap(chunk)
    relay(total_a, total_b, share, enter_mlp, mlp_one, order=order)
    for item in (k.middle, k.normed_two, k.gate, k.up, k.hidden_one):
        k.store(item)

    share = Share(group, k.normed_three, k.share_sems.at[1], group.own_rows)
    closing.append(share)

    def project_two(chunk):
        normed = chunk_rows(k.normed_three, chunk)
        put_rows(k.keys, chunk, plain(normed, k.w_key_two()[...]).astype(LOW), WINDOW)
        put_rows(k.values, chunk, plain(normed, k.w_value_two()[...]).astype(LOW), WINDOW)
        put_rows(k.query2, chunk, plain(normed, k.w_query_two()[...]).astype(LOW))

    def attend(chunk):
        window_forward(k, line, chunk)
        total_a.give(chunk, plain(chunk_rows(k.window_low, chunk), k.w_out_two()[...]))

    for step in range(CHUNKS + 1):
        if step < CHUNKS:
            chunk = order[step]
            after = k.middle[chunk : chunk + 1] + total_b.take(chunk)
            k.after[chunk : chunk + 1] = after
            share.give(chunk, norm_apply(after, k.gains[2:3]))
        if step > 0:
            chunk = order[step - 1]
            share.await_other(chunk)
            project_two(chunk)
        if step == 2:
            halo = Halo(k, 0, (k.keys, k.values), slice(rows, rows + WINDOW), line.after)
            total_a.close()
            total_a = Total(group, k.keep, k.totals[0])
            attend(3)
    total_a.swap(3)
    for item in closing[1:]:
        item.close()
    closing = [halo, total_a, total_c]
    attend(1)
    for index, target in enumerate((k.keys, k.values)):
        target[:WINDOW] = halo.take(index)
    total_a.swap(1)
    attend(0)
    total_a.swap(0)
    attend(2)
    total_a.swap(2)
    total_b = Total(group, k.keep, k.totals[1])
    closing.append(total_b)
    k.window_turned[...] = k.window_low[...].T
    k.store(k.after)
    k.store(k.normed_three)
    k.store(k.window_turned)

    gain = k.gains[3:4]
    share = Share(group, k.normed_four, k.share_sems.at[2], group.own_chunks)
    closing.append(share)

    def enter_turn(chunk, total):
        middle = k.after[chunk : chunk + 1] + total
        k.middle_two[chunk : chunk + 1] = middle
        return norm_apply(middle, gain)

    def mlp_two(chunk):
        normed = flat(k.normed_four[chunk])
        gate = plain(normed, k.turned[1])
        up_val = plain(normed, k.turned[2])
        d_gate, d_up = gate_backward(k.d_hidden[chunk], gate, up_val)
        d_gate, d_up = d_gate.astype(LOW), d_up.astype(LOW)
        back = plain(d_gate, k.w_gate_two()[...]) + plain(d_up, k.w_up_two()[...])
        k.gate_two[chunk] = gate
        k.up_two[chunk] = up_val
        k.d_gate_low[chunk] = d_gate
        k.d_up_low[chunk] = d_up
        return back

    order = [3, 1, 0, 2]
    relay(total_a, total_b, share, enter_turn, mlp_two, order=order)
    begun = []
    if k.scatter:
        begun = [
            Scatter(line, product(left, right), order, [k.gives[i]], [k.begun[i]], [k.give_sems.at[i]])
            for i, (left, right, order) in enumerate(
                ((k.normed_four, k.d_gate_two, X_FIRST), (k.normed_four, k.d_up_two, Z_FIRST))
            )
        ]
    spans = [slice(chunk * BLOCK, (chunk + 1) * BLOCK) for chunk in range(CHUNKS)]
    for chunk in range(CHUNKS):
        k.d_gate_two[:, spans[chunk]] = k.d_gate_low[chunk].T
    for item in begun[:1]:
        item.start(0)
    for chunk in range(CHUNKS):
        k.d_up_two[:, spans[chunk]] = k.d_up_low[chunk].T
    for item in begun[1:]:
        item.start(0)
    for chunk in range(CHUNKS):
        hidden = gate_forward(k.gate_two[chunk], k.up_two[chunk]).astype(LOW)
        k.hidden[chunk] = hidden
        k.hidden_two[:, spans[chunk]] = hidden.T
    for chunk in range(0, CHUNKS, 2):
        total_c.give(chunk, plain(flat(k.hidden[chunk : chunk + 2]), k.w_down_two()[...]), 2)
    total_c.swap_half()
    for item in (k.normed_four, k.hidden_two, k.d_gate_two, k.d_up_two):
        k.store(item)

    share = Share(group, k.grad_three, k.share_sems.at[3], group.own_rows)
    closing.append(share)
    k.gain_grad[...] = jnp.zeros_like(k.gain_grad)
    k.d_keys[...] = jnp.zeros_like(k.d_keys)
    k.d_values[...] = jnp.zeros_like(k.d_values)
    for step in range(CHUNKS + 1):
        if step < CHUNKS:
            chunk = order[step]
            d_values, d_gain = norm_back(total_b.take(chunk)[0], k.middle_two[chunk], gain)
            grad = k.cot[chunk, pl.ds(group.low, 1)].astype(FULL) + d_values[None]
            k.grad[chunk : chunk + 1] = grad
            k.gain_grad[...] += group.mine(chunk) * d_gain
            share.give(chunk, grad.astype(LOW))
        if step > 0:
            chunk = order[step - 1]
            share.await_other(chunk)
            put_rows(k.d_window, chunk, through(chunk_rows(k.grad_three, chunk), k.w_out_two()[...]).astype(LOW))
        if step == 3:
            window_backward(k, line, 0)
            halo = Halo(k, 1, (k.d_keys, k.d_values), slice(0, WINDOW), line.before)
            closing.append(halo)
            window_backward(k, line, 1)
    k.store(k.grad)
    k.store(k.grad_three)
    window_backward(k, line, 2)
    window_backward(k, line, 3)
    k.store(k.d_query2)
    k.result[...] = (flat(k.middle_two[pl.ds(2 * group.high, 2)]) + flat(total_c.take_half())).astype(LOW)
    for index, (target, out) in enumerate(((k.d_keys, k.d_key2), (k.d_values, k.d_value2))):
        target[rows : rows + WINDOW] += halo.take(index).astype(FULL)
        whole = target[WINDOW:]
        out[...] = whole.astype(LOW)
        k.store(out)
        k.d_turned2[(index + 1) * cols : (index + 2) * cols] = whole.T.astype(LOW)
    k.store(k.d_turned2)
    for item in begun:
        item.arrive(0)
        item.sent()
    for item in closing:
        item.close()
    for copy in [far, far_cot] + copies:
        copy.wait_send()
    taylor.close(True)


class Halo:
    def __init__(self, k, turn, sources, rows, peer):
        self.into = k.halo_in.at[turn]
        self.copies = []
        for index, source in enumerate(sources):
            k.halo_out[turn, index] = source[rows].astype(LOW)
            self.copies.append(
                send(
                    k.halo_out.at[turn, index],
                    k.halo_in.at[turn, index],
                    k.halo_sems.at[0, turn, index],
                    k.halo_sems.at[1, turn, index],
                    peer,
                )
            )

    def take(self, index):
        self.copies[index].wait_recv()
        return self.into[index]

    def close(self):
        for copy in self.copies:
            copy.wait_send()


def second_kernel(k, size):
    group, line = Group(), Line(size)
    meet = greet([group.pair, group.partner], line)
    width = k.gains.shape[1]
    total_a, total_b = (Total(group, k.keep, k.totals[i]) for i in range(2))
    share_mlp = Share(group, k.grad_two, k.share_sems.at[0], group.own_chunks)
    share = Share(group, k.grad_one, k.share_sems.at[1], group.own_rows)
    taylor = Taylor(line, k, k.query(), k.key(), k.value())
    background = list(PLAN)
    sums = {}

    def tick():
        if k.scatter:
            for name, level in background.pop(0):
                act(name, level)

    def normed_rows(chunk):
        return (
            through(chunk_rows(k.d_query2(), chunk, 2), k.w_query_two()[...])
            + through(chunk_rows(k.d_key2(), chunk, 2), k.w_key_two()[...])
            + through(chunk_rows(k.d_value2(), chunk, 2), k.w_value_two()[...])
        )

    def back(chunk, total, values, gain, row):
        d_values, d_gain = norm_back(flat(total), flat(values[chunk : chunk + 2]), gain)
        k.gain_rows[row : row + 1] += group.mine(chunk) * d_gain
        return d_values.reshape(2, HALF, width)

    def enter_mlp(chunk, total):
        grad = k.grad()[chunk : chunk + 2] + back(chunk, total, k.after(), k.gains[2:3], 2)
        k.grad()[chunk : chunk + 2] = grad
        return grad.astype(LOW)

    def mlp(chunk):
        d_hidden = through(flat(k.grad_two[chunk : chunk + 2]), k.w_down_one()[...])
        gate = flat(k.gate()[chunk : chunk + 2]).astype(FULL)
        up_val = flat(k.up()[chunk : chunk + 2]).astype(FULL)
        d_gate, d_up = gate_backward(d_hidden, gate, up_val)
        columns = slice(chunk * BLOCK, (chunk + 2) * BLOCK)
        k.d_gate_one[:, columns] = d_gate.T.astype(LOW)
        k.d_up_one[:, columns] = d_up.T.astype(LOW)
        return plain(d_gate.astype(LOW), k.w_gate_one()[...]) + plain(d_up.astype(LOW), k.w_up_one()[...])

    if k.scatter:
        pieces = [
            (k.normed_four, k.d_gate_two),
            (k.normed_four, k.d_up_two),
            (k.cot, k.hidden_two),
            (k.grad_three, k.window_turned),
            (k.normed_three, k.d_turned2),
            (k.normed_two, k.d_gate_one),
            (k.normed_two, k.d_up_one),
            (k.grad_two, k.hidden_one),
            (k.normed_one, k.d_turned),
            (k.grad_one, k.mixed_turned),
        ]
        sources = [product(left, right) for left, right in pieces]
        sources.append((lambda: None, lambda block: k.gain_rows[:, columns_of(block)]))
        begun = {0: 0, 1: 1}
        before = {5: 0, 6: 2, 7: 1}

        gain_copies = []

        def gain_step(step):
            if step:
                gain_copies[-1].wait_recv()
                k.gain_sum[step] = k.gain_sum[step - 1] + k.gain_in_sum[step - 1]
            else:
                k.gain_sum[0] = sums[10].finish()
            if step < 2:
                signals = k.gain_sems.at[0, step], k.gain_sems.at[1, step]
                peer = (group.pair, group.partner)[step]
                gain_copies.append(send(k.gain_sum.at[step], k.gain_in_sum.at[step], *signals, peer))
                return
            share_of = BLOCK // 4
            found = jnp.zeros((8, share_of), FULL)
            for index in range(4):
                part = k.gain_sum[2][:, index * share_of : (index + 1) * share_of]
                found = found + jnp.where(group.index == index, 1.0, 0.0) * part
            k.gain_out[...] = found

        def sum_of(name):
            if name not in sums:
                got = list(k.gots[name])
                if name in begun:
                    got[0] = k.begun[begun[name]]()
                if name in before:
                    sums[before[name]].sent()
                sems = [sem.at[name] for sem in k.sems]
                give = k.gives[before.get(name, name)]
                order = ORDERS[name]
                sums[name] = Scatter(line, sources[name], order, give, got, sems, 1 if name in begun else 0)
            return sums[name]

        def act(name, level):
            if name == 11:
                return gain_step(level)
            sum_of(name)
            if level < len(ORDERS[name]):
                sums[name].start(level)
            else:
                k.sums[name][...] = sums[name].finish()
                k.store(k.sums[name])

    k.gain_rows[...] = jnp.zeros_like(k.gain_rows)
    k.gain_rows[3:4] = k.gain_in[...]
    if k.scatter:
        name, _ = background[0][0]
        for index in sum_of(name).places(0):
            sums[name].prepare(0, index)
        meet()
        sums[name].start(0, prepared=True)
        background[0] = background[0][1:]
    else:
        meet()
    for chunk in range(0, CHUNKS, 2):
        total_a.give(chunk, normed_rows(chunk), 2, by_rows=True)
    for chunk in range(0, CHUNKS, 2):
        total_a.swap(chunk, 2)
    tick()
    relay(total_a, total_b, share_mlp, enter_mlp, mlp, 2, between=tick)
    for step in range(3):
        if step < 2:
            chunk = 2 * step
            grad = k.grad()[chunk : chunk + 2] + back(chunk, total_b.take(chunk, 2), k.middle(), k.gains[1:2], 1)
            k.grad()[chunk : chunk + 2] = grad
            share.give(chunk, grad.astype(LOW), 2)
        if step > 0:
            chunk = 2 * step - 2
            share.await_other(chunk)
            rows = through(chunk_rows(k.grad_one, chunk, 2), k.w_out_one()[...])
            k.d_mixed[chunk * BLOCK : (chunk + 2) * BLOCK] = rows.astype(LOW)
        tick()

    total_a.close()
    total_c = Total(group, k.keep, k.totals[0])
    k.mixed, k.inverse, k.carry = k.mixed(), k.inverse(), k.carry()
    for _ in taylor.backward(k.d_mixed):
        tick()
    d_query = 0.5 * k.d_query_acc[...]
    d_key = 0.5 * k.d_key_acc[...]
    d_value = k.d_value_acc[...]
    small, cols = d_query.shape[1], d_value.shape[1]
    k.d_query_low[...] = d_query.astype(LOW)
    k.d_key_low[...] = d_key.astype(LOW)
    k.d_value_low[...] = d_value.astype(LOW)
    k.d_turned[:small] = d_query.T.astype(LOW)
    k.d_turned[small : 2 * small] = d_key.T.astype(LOW)
    k.d_turned[2 * small : 2 * small + cols] = d_value.T.astype(LOW)
    for chunk in range(0, CHUNKS, 2):
        part = (
            plain(chunk_rows(k.d_query_low, chunk, 2), k.w_query_one()[...])
            + plain(chunk_rows(k.d_key_low, chunk, 2), k.w_key_one()[...])
            + through(chunk_rows(k.d_value_low, chunk, 2), k.w_value_one()[...])
        )
        total_c.give(chunk, part, 2, by_rows=True)
    total_c.swap_half()
    tick()
    half = pl.ds(2 * group.high, 2)
    d_values, d_gain = norm_back(flat(total_c.take_half()), flat(k.start()[half]), k.gains[0:1])
    k.input_grad[...] = flat(k.grad()[half]) + d_values
    k.gain_rows[0:1] = d_gain

    tick()
    if k.scatter:
        while background:
            tick()
        for name in set(sums) - set(before.values()):
            sums[name].sent()
        for copy in gain_copies:
            copy.wait_send()
    else:
        for item in (k.d_gate_one, k.d_up_one, k.d_turned, k.grad_one, k.grad_two):
            k.store(item)
        k.gain_out[...] = k.gain_rows[...]
    for item in (total_b, total_c, share_mlp, share):
        item.close()
    taylor.close(False)


def finish_kernel(k, small, cols):
    k.result[...] = k.result_in[...]
    k.input_grad[...] = k.input_grad_in[...]
    k.gains[...] = k.gains_in[0:4]
    for source, target in zip(k.sums, k.same):
        target[...] = source[...]
    for source, targets in zip(k.threes, k.turned):
        first = 0
        for target in targets:
            if target.shape[1] == BLOCK:
                target[...] = source[first : first + target.shape[0]]
                first += target.shape[0]
            else:
                target[...] = source[first : first + target.shape[1]].T
                first += target.shape[1]


def run_kernel(kernel, ident, ins, outs, scratch, flops, later=None, saved=None, apart=None, scalars=None, extra=None):
    later, saved, apart, scalars = (found or {} for found in (later, saved, apart, scalars))
    is_shape = lambda leaf: isinstance(leaf, tuple) and isinstance(leaf[0], tuple)

    def buffer(array):
        return pltpu.VMEM(array.shape, array.dtype)

    def held(tree):
        return jax.tree.map(lambda leaf: pltpu.VMEM(*leaf), tree, is_leaf=is_shape)

    def sems(tree):
        return jax.tree.map(lambda leaf: pltpu.SemaphoreType.DMA(()), tree, is_leaf=is_shape)

    arguments = (ins, later, scalars)
    results = (outs, saved, apart)
    own = (
        scratch,
        jax.tree.map(buffer, later),
        jax.tree.map(lambda leaf: pltpu.SemaphoreType.DMA(()), later),
        held(saved),
        sems(saved),
    )
    flat_in, tree_in = jax.tree.flatten(arguments)
    flat_out, tree_out = jax.tree.flatten(results, is_leaf=is_shape)
    flat_own, tree_own = jax.tree.flatten(own)

    def body(*refs):
        in_refs = jax.tree.unflatten(tree_in, refs[: len(flat_in)])
        out_refs = jax.tree.unflatten(tree_out, refs[len(flat_in) : len(flat_in) + len(flat_out)])
        own_refs = jax.tree.unflatten(tree_own, refs[len(flat_in) + len(flat_out) :])
        k = types.SimpleNamespace(**(extra or {}))
        for tree in (in_refs[0], in_refs[2], out_refs[0], out_refs[2], own_refs[0], own_refs[3]):
            k.__dict__.update(tree)
        waited = []
        for name in later:
            source = in_refs[1][name]
            parts = zip(*(jax.tree.leaves(tree) for tree in (source, own_refs[1][name], own_refs[2][name])))
            found = [Later(*part) for part in parts]
            waited += found
            setattr(k, name, found if isinstance(source, list) else found[0])
        saves = []
        for name in saved:
            parts = zip(*(jax.tree.leaves(tree[name]) for tree in (own_refs[3], out_refs[1], own_refs[4])))
            saves += [Saved(*part) for part in parts]

        def store(ref):
            for item in saves:
                if item.ref is ref:
                    item.store()

        k.store = store
        kernel(k)
        for item in waited:
            item()
        for item in saves:
            if item.copy is None:
                item.store()
        for item in saves:
            item.copy.wait()

    shapes = [jax.ShapeDtypeStruct(*leaf) for leaf in flat_out]
    moved = sum(a.size * a.dtype.itemsize for a in flat_in) + sum(
        math.prod(a.shape) * a.dtype.itemsize for a in shapes
    )
    there = pl.BlockSpec(memory_space=pl.ANY)
    here = pl.BlockSpec(memory_space=pltpu.VMEM)
    scalar = pl.BlockSpec(memory_space=pltpu.SMEM)

    def places(trees, kinds):
        return [kind for tree, kind in zip(trees, kinds) for _ in jax.tree.leaves(tree, is_leaf=is_shape)]

    found = pl.pallas_call(
        body,
        out_shape=shapes,
        in_specs=places(arguments, (here, there, scalar)),
        out_specs=places(results, (here, there, there)),
        scratch_shapes=flat_own,
        cost_estimate=pl.CostEstimate(flops=flops, bytes_accessed=moved, transcendentals=0),
        compiler_params=pltpu.CompilerParams(
            collective_id=ident, has_side_effects=ident is not None, vmem_limit_bytes=VMEM_BYTES
        ),
    )(*flat_in)
    found = jax.tree.unflatten(tree_out, found)
    return types.SimpleNamespace(**found[0], **found[1], **found[2])


def halve(array, axis):
    size = lax.axis_size(axis)
    index = lax.axis_index(axis)
    pieces = array.reshape((size, array.shape[0] // size) + array.shape[1:])
    distance = 1
    while distance < size:
        bit = (index // distance) % 2
        pairs = pieces.reshape((pieces.shape[0] // 2, 2) + pieces.shape[1:])
        keep = lax.dynamic_index_in_dim(pairs, bit, axis=1, keepdims=False)
        give = lax.dynamic_index_in_dim(pairs, 1 - bit, axis=1, keepdims=False)
        got = lax.ppermute(give, axis, [(i, i ^ distance) for i in range(size)])
        pieces = (keep.astype(FULL) + got.astype(FULL)).astype(array.dtype)
        distance *= 2
    return pieces[0]


def scatter_plain(left, right):
    return halve(inner(flat(left), right.T).astype(LOW), "seq").astype(FULL).T


def scatter_gains(gains):
    count = lax.axis_size("tensor")
    n_seq = lax.axis_size("seq")
    shaped = gains.reshape(4, n_seq, -1).transpose(1, 0, 2)
    mine = halve(shaped, "seq")[0]
    distance = 1
    while distance < count:
        mine = mine + lax.ppermute(mine, "tensor", [(i, i ^ distance) for i in range(count)])
        distance *= 2
    width = mine.shape[-1] // count
    return lax.dynamic_slice_in_dim(mine, lax.axis_index("tensor") * width, width, 1)


def on_device(
    inputs,
    cotangent,
    seq_lengths,
    norm_gains,
    query_one,
    key_one,
    value_one,
    out_one,
    gate_one,
    up_one,
    down_one,
    query_two,
    key_two,
    value_two,
    out_two,
    gate_two,
    up_two,
    down_two,
):
    rows, width = inputs.shape
    size = lax.axis_size("seq")
    stretch = 4 * rows
    units = gate_one.shape[1]
    cols = value_one.shape[1]
    small = query_one.shape[1]
    scatter = width // size == BLOCK
    count = int(math.log2(size))
    wide = ((4, 2, HALF, width), LOW)
    own = ((CHUNKS, HALF, width), FULL)
    heads = ((stretch, cols), LOW)
    heads_full = ((stretch, cols), FULL)
    narrow = ((stretch, small), LOW)
    unit_rows = ((CHUNKS, 2, HALF, units), LOW)
    turned_units = ((units, stretch), LOW)
    turned_cols = ((cols, stretch), LOW)
    state = ((FEATS + NORM_ROWS, cols), FULL)
    padded = ((stretch + WINDOW, cols), LOW)
    one_flops = 2 * stretch * width
    blocks = functools.partial(Scatter.blocks, size)
    choice, feature_rows = feature_tables()
    tables = dict(feature_choice=choice, feature_rows=feature_rows)
    tensor_sums = dict(
        keep=pltpu.VMEM(*own),
        share_sems=pltpu.SemaphoreType.DMA((4, 2, CHUNKS)),
    )
    got = ((size // 2, units, BLOCK), LOW)
    ahead = run_kernel(
        functools.partial(first_kernel, size=size),
        0,
        dict(
            gains=norm_gains,
            inputs=inputs,
            cotangent=cotangent,
            w_query_one=query_one.T,
            w_key_one=key_one.T,
            w_value_one=value_one,
            **tables,
        ),
        dict(result=((rows, width), LOW), gain_grad=((1, width), FULL)),
        dict(
            **tensor_sums,
            **Taylor.scratch(size, cols),
            totals=[Total.scratch(width) for _ in range(3)],
            rows_in=pltpu.VMEM((rows, width), LOW),
            cot_in=pltpu.VMEM((rows, width), LOW),
            near_sems=pltpu.SemaphoreType.DMA((2, 4)),
            far_sems=pltpu.SemaphoreType.DMA((2, 2)),
            mixed_low=pltpu.VMEM(*heads),
            turned=pltpu.VMEM((3, width, units), LOW),
            query_feats=pltpu.VMEM((cols // HEAD, stretch, FEATS), LOW),
            query2=pltpu.VMEM(*heads),
            keys=pltpu.VMEM(*padded),
            values=pltpu.VMEM(*padded),
            window_low=pltpu.VMEM(*heads),
            d_window=pltpu.VMEM(*heads),
            d_keys=pltpu.VMEM(padded[0], FULL),
            d_values=pltpu.VMEM(padded[0], FULL),
            middle_two=pltpu.VMEM(*own),
            hidden=pltpu.VMEM((CHUNKS, 2 * HALF, units), LOW),
            d_hidden=pltpu.VMEM((CHUNKS, 2 * HALF, units), FULL),
            gate_two=pltpu.VMEM((CHUNKS, 2 * HALF, units), FULL),
            up_two=pltpu.VMEM((CHUNKS, 2 * HALF, units), FULL),
            d_gate_low=pltpu.VMEM((CHUNKS, 2 * HALF, units), LOW),
            d_up_low=pltpu.VMEM((CHUNKS, 2 * HALF, units), LOW),
            halo_out=pltpu.VMEM((2, 2, WINDOW, cols), LOW),
            halo_in=pltpu.VMEM((2, 2, WINDOW, cols), LOW),
            halo_sems=pltpu.SemaphoreType.DMA((2, 2, 2)),
            gives=[pltpu.VMEM(*got), pltpu.VMEM(*got)] if scatter else [],
            give_sems=pltpu.SemaphoreType.DMA((2, 2, size // 2)),
        ),
        one_flops * (8 * cols + 9 * units),
        later=dict(
            w_out_one=out_one,
            w_gate_one=gate_one.T,
            w_up_one=up_one.T,
            w_down_one=down_one,
            w_key_two=key_two,
            w_value_two=value_two,
            w_query_two=query_two,
            w_out_two=out_two,
            w_gate_two=gate_two.T,
            w_up_two=up_two.T,
            w_down_two=down_two,
        ),
        saved=dict(
            start=own,
            middle=own,
            after=own,
            grad=own,
            normed_one=wide,
            normed_two=wide,
            normed_three=wide,
            normed_four=wide,
            cot=wide,
            grad_three=wide,
            query=narrow,
            key=narrow,
            value=heads,
            mixed=heads_full,
            inverse=heads_full,
            mixed_turned=turned_cols,
            carry=state,
            gate=unit_rows,
            up=unit_rows,
            hidden_one=turned_units,
            hidden_two=turned_units,
            d_gate_two=turned_units,
            d_up_two=turned_units,
            window_turned=turned_cols,
            d_query2=heads,
            d_key2=heads,
            d_value2=heads,
            d_turned2=((3 * cols, stretch), LOW),
        ),
        apart=dict(begun=[got, got]) if scatter else None,
        scalars=dict(lengths=seq_lengths),
        extra=dict(scatter=scatter),
    )
    widths = [units, units, units, cols, 3 * cols, units, units, units, 2 * small + cols, cols]
    carried = dict(
        d_query2=ahead.d_query2,
        d_key2=ahead.d_key2,
        d_value2=ahead.d_value2,
        w_query_two=query_two,
        w_key_two=key_two,
        w_value_two=value_two,
    )
    summed = dict(
        normed_four=ahead.normed_four,
        d_up_two=ahead.d_up_two,
        d_gate_two=ahead.d_gate_two,
        cot=ahead.cot,
        hidden_two=ahead.hidden_two,
        grad_three=ahead.grad_three,
        window_turned=ahead.window_turned,
        normed_three=ahead.normed_three,
        d_turned2=ahead.d_turned2,
        normed_two=ahead.normed_two,
        hidden_one=ahead.hidden_one,
        normed_one=ahead.normed_one,
        mixed_turned=ahead.mixed_turned,
    )
    chain = dict(
        after=ahead.after,
        grad=ahead.grad,
        w_down_one=down_one,
        gate=ahead.gate,
        up=ahead.up,
        w_gate_one=gate_one.T,
        w_up_one=up_one.T,
        middle=ahead.middle,
        w_out_one=out_one,
        query=ahead.query,
        key=ahead.key,
        value=ahead.value,
        mixed=ahead.mixed,
        inverse=ahead.inverse,
        carry=ahead.carry,
        w_query_one=query_one.T,
        w_key_one=key_one.T,
        w_value_one=value_one,
        start=ahead.start,
    )
    early = ("normed_three", "d_turned2", "normed_four", "d_up_two", "d_gate_two", "cot", "hidden_two")
    made = dict(
        d_gate_one=turned_units,
        d_up_one=turned_units,
        d_turned=((2 * small + cols, stretch), LOW),
        grad_two=wide,
        grad_one=wide,
    )
    if scatter:
        gain_blocks = [pltpu.VMEM((size >> (at + 1), 8, BLOCK), FULL) for at in range(count)]
        buffers = dict(
            gives=[[] if name in (5, 6, 7) else blocks(wide_) for name, wide_ in enumerate(widths)] + [gain_blocks],
            gots=[blocks(wide_) for wide_ in widths] + [gain_blocks],
            sems=[pltpu.SemaphoreType.DMA((11, 2, size >> (at + 1))) for at in range(count)],
            gain_sum=pltpu.VMEM((3, 8, BLOCK), FULL),
            gain_in_sum=pltpu.VMEM((2, 8, BLOCK), FULL),
            gain_sems=pltpu.SemaphoreType.DMA((2, 2)),
            **{name: pltpu.VMEM(*leaf) for name, leaf in made.items()},
        )
        for name in (0, 1):
            buffers["gots"][name][0] = None
        inputs_later = dict(
            **{name: summed[name] for name in early[:2]},
            **carried,
            **{name: summed[name] for name in early[2:]},
            begun=ahead.begun,
            **chain,
            **{name: array for name, array in summed.items() if name not in early},
        )
        kept = dict(sums=[((wide_, BLOCK), FULL) for wide_ in widths])
    else:
        buffers = {}
        inputs_later = dict(**carried, **chain)
        kept = made
    behind = run_kernel(
        functools.partial(second_kernel, size=size),
        1,
        dict(gains=norm_gains, gain_in=ahead.gain_grad, **tables),
        dict(input_grad=((rows, width), FULL), gain_out=((8, BLOCK // 4 if scatter else width), FULL)),
        dict(
            **tensor_sums,
            **Taylor.scratch(size, cols),
            totals=[Total.scratch(width) for _ in range(2)],
            d_mixed=pltpu.VMEM(*heads),
            gain_rows=pltpu.VMEM((8, width), FULL),
            grad_carry=pltpu.VMEM(*state),
            d_query_acc=pltpu.VMEM((stretch, small), FULL),
            d_key_acc=pltpu.VMEM((stretch, small), FULL),
            d_value_acc=pltpu.VMEM((stretch, cols), FULL),
            d_query_low=pltpu.VMEM(*narrow),
            d_key_low=pltpu.VMEM(*narrow),
            d_value_low=pltpu.VMEM(*heads),
            **buffers,
        ),
        one_flops * (6 * cols + 9 * units),
        later=inputs_later,
        saved=kept,
        scalars=dict(lengths=seq_lengths),
        extra=dict(scatter=scatter),
    )
    if not scatter:
        sums = [
            scatter_plain(left, right)
            for left, right in (
                (ahead.normed_four, ahead.d_gate_two),
                (ahead.normed_four, ahead.d_up_two),
                (ahead.cot, ahead.hidden_two),
                (ahead.grad_three, ahead.window_turned),
                (ahead.normed_three, ahead.d_turned2),
                (ahead.normed_two, behind.d_gate_one),
                (ahead.normed_two, behind.d_up_one),
                (behind.grad_two, ahead.hidden_one),
                (ahead.normed_one, behind.d_turned),
                (behind.grad_one, ahead.mixed_turned),
            )
        ]
        gains = scatter_gains(behind.gain_out[:4])
        three_one, three_two = sums[8], sums[4]
        return (
            (ahead.result, behind.input_grad, gains)
            + (three_one[:small].T, three_one[small : 2 * small].T, three_one[2 * small :].T)
            + (sums[9], sums[5].T, sums[6].T, sums[7])
            + tuple(three_two[first : first + cols].T for first in range(0, 3 * cols, cols))
            + (sums[3], sums[0].T, sums[1].T, sums[2])
        )
    block = ((BLOCK, cols), FULL)
    unit = ((units, BLOCK), FULL)
    done = run_kernel(
        functools.partial(finish_kernel, small=small, cols=cols),
        None,
        dict(
            result_in=ahead.result,
            input_grad_in=behind.input_grad,
            gains_in=behind.gain_out,
            sums=[behind.sums[name] for name in (0, 1, 2, 3, 5, 6, 7, 9)],
            threes=[behind.sums[8], behind.sums[4]],
        ),
        dict(
            result=((rows, width), LOW),
            input_grad=((rows, width), FULL),
            gains=((4, BLOCK // 4), FULL),
            same=[unit, unit, unit, ((cols, BLOCK), FULL), unit, unit, unit, ((cols, BLOCK), FULL)],
            turned=[[((small, BLOCK), FULL), ((small, BLOCK), FULL), block], [block, block, block]],
        ),
        {},
        stretch,
    )
    same, turned = done.same, done.turned
    return (
        (done.result, done.input_grad, done.gains)
        + (turned[0][0].T, turned[0][1].T, turned[0][2])
        + (same[7], same[4].T, same[5].T, same[6])
        + tuple(turned[1])
        + (same[3], same[0].T, same[1].T, same[2])
    )


def solution(mesh):
    both = P(("seq", "tensor"), None)
    split = P(None, "tensor")
    stacked = P("tensor", None)
    columns_out = P("seq", "tensor")
    rows_out = P("tensor", "seq")
    layer_in = (split, split, split, stacked, split, split, stacked)
    layer_out = (columns_out, columns_out, columns_out, rows_out, columns_out, columns_out, rows_out)
    return jax.shard_map(
        on_device,
        mesh=mesh,
        in_specs=(both, both, P(), P()) + layer_in + layer_in,
        out_specs=(both, both, P(None, ("seq", "tensor"))) + layer_out + layer_out,
        check_vma=False,
    )
```
